32 devices in a mesh: dp: 8 (over z, core), ctx: 4 (over y, x).
Axes of the slice: x: 2, y: 2, z: 4, core: 2. Of those that a mesh axis runs over, the one named last changes fastest.
Arguments:
- byte_ids: int32 [8, 2048], P('dp', 'ctx'), may hold values from 0 to 255
- lengths: int32 [8, 4], P('dp'), may hold values from 64 to 1856, as said below
- embed: bfloat16 [256, 768], P(None, ('dp', 'ctx')), may hold values from -6 to 6
- conv_weight: bfloat16 [4, 768], P(None, ('dp', 'ctx')), may hold values from -3 to 3
- conv_bias: bfloat16 [768], P(('dp', 'ctx')), may hold values from -2 to 2
- scorer: bfloat16 [768], P(('dp', 'ctx')), may hold values from -0.4375 to 0.4375
- norm_attn: bfloat16 [2, 768], P(None, ('dp', 'ctx')), may hold values from 0.5 to 1.5
- query_w: bfloat16 [2, 768, 768], P(None, ('dp', 'ctx')), may hold values from -0.0546875 to 0.0546875
- key_w: bfloat16 [2, 768, 768], P(None, ('dp', 'ctx')), may hold values from -0.21875 to 0.21875
- value_w: bfloat16 [2, 768, 768], P(None, ('dp', 'ctx')), may hold values from -0.21875 to 0.21875
- attn_out_w: bfloat16 [2, 768, 768], P(None, ('dp', 'ctx')), may hold values from -1.25 to 1.25
- norm_ffn: bfloat16 [2, 768], P(None, ('dp', 'ctx')), may hold values from 0.5 to 1.5
- gate_w: bfloat16 [2, 768, 2048], P(None, ('dp', 'ctx')), may hold values from -0.21875 to 0.21875
- up_w: bfloat16 [2, 768, 2048], P(None, ('dp', 'ctx')), may hold values from -0.21875 to 0.21875
- down_w: bfloat16 [2, 2048, 768], P(None, ('dp', 'ctx')), may hold values from -0.125 to 0.125
- out_grad: bfloat16 [8, 1024, 768], P('dp', 'ctx'), may hold values from -6 to 6
Outputs:
- encoded: bfloat16 [8, 1024, 768], P('dp', 'ctx')
- grad_embed: float32 [256, 768], P(None, ('dp', 'ctx'))
- grad_conv_weight: float32 [4, 768], P(None, ('dp', 'ctx'))
- grad_conv_bias: float32 [768], P(('dp', 'ctx'))
- grad_scorer: float32 [768], P(('dp', 'ctx'))
- grad_norm_attn: float32 [2, 768], P(None, ('dp', 'ctx'))
- grad_query_w: float32 [2, 768, 768], P(None, ('dp', 'ctx'))
- grad_key_w: float32 [2, 768, 768], P(None, ('dp', 'ctx'))
- grad_value_w: float32 [2, 768, 768], P(None, ('dp', 'ctx'))
- grad_attn_out_w: float32 [2, 768, 768], P(None, ('dp', 'ctx'))
- grad_norm_ffn: float32 [2, 768], P(None, ('dp', 'ctx'))
- grad_gate_w: float32 [2, 768, 2048], P(None, ('dp', 'ctx'))
- grad_up_w: float32 [2, 768, 2048], P(None, ('dp', 'ctx'))
- grad_down_w: float32 [2, 2048, 768], P(None, ('dp', 'ctx'))
The draws below stay inside these ranges and needn't reach their ends.
Inputs may be any that keep to these rules, and one draw needn't show every extreme that they name: `lengths`: every length is even; each group holds 4 sequences packed end to end from its first byte, followed by padding; in each group one sequence starts among the first 512 bytes and ends among the last 512 bytes.
All inputs are finite; a program needn't handle non-finite values.
Results may differ from the reference program's by a relative error of at most 0.019.
Values may be sent and summed in bfloat16 or wider, within the bound.
A program may use at most 256 MiB of HBM per device.

```python
import math
import jax
import jax.numpy as jnp
import numpy as np
from jax import lax

D = 768
FF = 2048
HEADS = 12
HEAD_DIM = 64
VOCAB = 256
CONV = 4
LAYERS = 2
SEQS = 4
TOK_DEV = 256
GROUPS = 8
GROUP_TOK = 1024
GROUP_BYTES = 2048


def draw_lengths(key, part):
    key = jax.random.fold_in(key, 11)
    short_key, pad_key, long_key, full_key = jax.random.split(key, 4)
    shorts = 2 * jax.random.randint(short_key, (GROUPS, SEQS), TOK_DEV // 8, TOK_DEV // 4 + 1)
    pads = 2 * jax.random.randint(pad_key, (GROUPS,), 0, TOK_DEV // 8 + 1)
    long_at = jax.random.randint(long_key, (GROUPS,), 0, SEQS)
    full_group = jax.random.randint(full_key, (), 0, GROUPS)
    rows = jnp.arange(GROUPS)
    shorts = jnp.where(rows[:, None] == full_group, 2 * (TOK_DEV // 8), shorts)
    pads = jnp.where(rows == full_group, 0, pads)
    is_long = jnp.arange(SEQS)[None, :] == long_at[:, None]
    short_total = jnp.sum(jnp.where(is_long, 0, shorts), 1)
    long_length = GROUP_BYTES - pads - short_total
    return jnp.where(is_long, long_length[:, None], shorts).astype(jnp.int32)


def touch_ends(entries, rng, low, top_value):
    longest = entries.shape.index(max(entries.shape))
    spots = []
    for shift in (0, 1):
        where = [jax.random.randint(jax.random.fold_in(rng, axis), (), 0, length) for axis, length in enumerate(entries.shape)]
        where[longest] = (where[longest] + shift) % entries.shape[longest]
        spots.append(tuple(where))
    return entries.at[spots[0]].set(low).at[spots[1]].set(top_value)


def level_of(rng, dims, cuts, smallest, high):
    loudness, own = 1.0, jax.random.fold_in(rng, 6)
    for axis_at, blocks in cuts:
        draws = jnp.exp(jax.random.uniform(jax.random.fold_in(own, axis_at), (blocks,), jnp.float32, smallest / len(cuts), high / len(cuts)))
        loudness = loudness * jnp.repeat(draws, dims[axis_at] // blocks).reshape([-1 if axis == axis_at else 1 for axis in range(len(dims))])
    return loudness


def cumulative_ranks(number_of, lean):
    portions = [(1 << 20) // math.isqrt(standing ** lean) + 1 for standing in range(1, number_of + 1)]
    width = 1 + sum(portions) // (1 << 30)
    return np.cumsum(np.array([max(1, weight // width) for weight in portions]))


def ranked(own_key, dims, count, skew):
    listing = cumulative_ranks(count, skew)
    lot = jax.random.randint(jax.random.fold_in(own_key, 1), dims, 0, int(listing[count - 1]))
    grade = jnp.searchsorted(jnp.asarray(listing, jnp.int32), lot, side="right")
    return jax.random.permutation(jax.random.fold_in(own_key, 2), count)[grade].astype(jnp.int32)


def centred(stream_key, dims, width, limit, shards=(), kind=jnp.bfloat16):
    loudness = level_of(stream_key, dims, shards, -0.22, 0.18) if shards else 1.0
    result = jax.random.normal(stream_key, dims, jnp.float32) * width * loudness
    return jnp.minimum(jnp.maximum(result, -limit), limit).astype(kind)


def setup_inputs(seed: int = 0) -> dict:
    key_list = jax.random.split(jax.random.key(seed), 17)
    return {
        "byte_ids": touch_ends(ranked(key_list[0], (GROUPS, GROUP_BYTES), VOCAB, 2), jax.random.fold_in(key_list[0], 3), 0, VOCAB - 1).astype(jnp.int32),
        "lengths": draw_lengths(jax.random.fold_in(key_list[16], 71), 0),
        "embed": centred(key_list[2], (VOCAB, D), 1.0, 6.0, ((1, 32),)),
        "conv_weight": centred(key_list[3], (CONV, D), 0.5, 3.0, ((1, 32),)),
        "conv_bias": centred(key_list[4], (D,), 0.3, 2.0, ((0, 32),)),
        "scorer": centred(key_list[5], (D,), (D // 4) ** -0.5, 0.4375, ((0, 32),)),
        "norm_attn": jnp.clip(1.0 + 0.1 * jax.random.normal(key_list[6], (LAYERS, D), jnp.float32), 0.5, 1.5).astype(jnp.bfloat16),
        "query_w": centred(key_list[7], (LAYERS, D, D), (D * 16) ** -0.5, 0.0546875, ((1, 32),)),
        "key_w": centred(key_list[8], (LAYERS, D, D), D ** -0.5, 0.21875, ((1, 32),)),
        "value_w": centred(key_list[9], (LAYERS, D, D), D ** -0.5, 0.21875, ((1, 32),)),
        "attn_out_w": centred(key_list[10], (LAYERS, D, D), (D // 32) ** -0.5, 1.25, ((1, 32),)),
        "norm_ffn": jnp.clip(1.0 + 0.1 * jax.random.normal(key_list[11], (LAYERS, D), jnp.float32), 0.5, 1.5).astype(jnp.bfloat16),
        "gate_w": centred(key_list[12], (LAYERS, D, FF), D ** -0.5, 0.21875, ((1, 32),)),
        "up_w": centred(key_list[13], (LAYERS, D, FF), D ** -0.5, 0.21875, ((1, 32),)),
        "down_w": centred(key_list[14], (LAYERS, FF, D), FF ** -0.5, 0.125, ((1, 32),)),
        "out_grad": centred(key_list[15], (GROUPS, GROUP_TOK, D), 1.0, 6.0, ((0, 8), (1, 4))),
    }


NORM_EPS = 1e-06
NEG_FILL = -1000000000.0
PRECISE = lax.Precision.HIGHEST

@jax.custom_vjp
def low(v):
    return lax.optimization_barrier(v.astype(jnp.bfloat16)).astype(jnp.float32)

@jax.custom_vjp
def low_back(v):
    return v

def low_keep(v):
    return (low(v), None)

def low_pass(kept, grad):
    return (grad,)

def back_keep(v):
    return (v, None)

def back_low(kept, grad):
    return (low(grad),)
low.defvjp(low_keep, low_pass)
low_back.defvjp(back_keep, back_low)

def rms_scale(values, gain):
    return values * lax.rsqrt(lax.optimization_barrier(jnp.mean(values * values, -1, keepdims=True)) + NORM_EPS) * gain

def segment_of(places, ends):
    return lax.optimization_barrier(jnp.sum((places[:, None] >= ends[None, :]).astype(jnp.int32), 1)).astype(jnp.int32)

def offset_in(places, segs, ends, seq_lengths):
    starts = (ends - seq_lengths).astype(jnp.int32)
    picks = segs[:, None] == jnp.arange(ends.shape[0], dtype=jnp.int32)[None, :]
    return (places - lax.optimization_barrier(jnp.sum(jnp.where(picks, starts[None, :], 0), 1))).astype(jnp.int32)

def mix_bytes(ids, seq_lengths, embed_t, conv_w, conv_b, scorer_v):
    byte_count = ids.shape[0]
    places = jnp.arange(byte_count, dtype=jnp.int32)
    ends = jnp.cumsum(seq_lengths).astype(jnp.int32)
    segs = segment_of(places, ends)
    rel = offset_in(places, segs, ends, seq_lengths)
    valid = (places < ends[-1]).astype(jnp.float32)
    embedded = jnp.take(embed_t, ids, axis=0) * valid[:, None]
    padded = jnp.pad(embedded, ((1, 2), (0, 0)))
    seg_pad = jnp.pad(segs, (1, 2), constant_values=-1)
    conv_out = conv_b[None, :] + sum((conv_w[tap][None, :] * padded[tap:tap + byte_count] * (seg_pad[tap:tap + byte_count] == segs).astype(jnp.float32)[:, None] for tap in range(4)))
    conv_out = conv_out * valid[:, None]
    conv_wide = jnp.pad(conv_out, ((3, 3), (0, 0)))
    seg_wide = jnp.pad(segs, (3, 3), constant_values=-1)
    pooled_list = []
    for block_size in (1, 2, 3, 4):
        pooled = jnp.zeros(conv_out.shape, jnp.float32)
        for shift_by in range(1 - block_size, block_size):
            same = (seg_wide[3 + shift_by:3 + shift_by + byte_count] == segs) & ((rel + shift_by) // block_size == rel // block_size)
            weight = jnp.where(same, 1.0 / block_size, 0.0).astype(jnp.float32)
            pooled = pooled + weight[:, None] * conv_wide[3 + shift_by:3 + shift_by + byte_count]
        pooled_list.append(pooled)
    stacked = jnp.stack(pooled_list)
    logits = jnp.einsum('bnd,d->bn', stacked, scorer_v, precision=PRECISE)
    choose = jax.nn.softmax(logits, 0)
    chosen = lax.optimization_barrier(jnp.sum(choose[..., None] * stacked, 0))
    return (chosen.reshape(byte_count // 2, 2, -1).mean(1), ends)

def attend_block(q_block, q_seg_block, k_heads, v_heads, tok_seg):
    scores = low_back(jnp.einsum('qhd,khd->hqk', q_block, k_heads, precision=PRECISE))
    same = q_seg_block[None, :, None] == tok_seg[None, None, :]
    scores = jnp.where(same, scores, NEG_FILL)
    attn_probs = jax.nn.softmax(scores, -1)
    return jnp.einsum('hqk,khd->qhd', low(attn_probs), v_heads, precision=PRECISE)

def encoder_layer(stream, tok_seg, gain_attn, w_query, w_key, w_value, w_out, gain_ffn, w_gate, w_up, w_down):
    row_count = stream.shape[0]
    normed = low(rms_scale(stream, gain_attn))
    query_act = low_back(low(jnp.dot(normed, w_query, precision=PRECISE)))
    key_act = low_back(low(jnp.dot(normed, w_key, precision=PRECISE)))
    value_act = low_back(low(jnp.dot(normed, w_value, precision=PRECISE)))
    block_rows = min(512, row_count)
    q_blocks = query_act.reshape(row_count // block_rows, block_rows, HEADS, HEAD_DIM)
    seg_blocks = tok_seg.reshape(row_count // block_rows, block_rows)
    k_heads = key_act.reshape(row_count, HEADS, HEAD_DIM)
    v_heads = value_act.reshape(row_count, HEADS, HEAD_DIM)

    def one_block(block_item):
        return attend_block(block_item[0], block_item[1], k_heads, v_heads, tok_seg)
    attended = lax.map(jax.checkpoint(one_block), (q_blocks, seg_blocks))
    attended = low_back(low(attended.reshape(row_count, -1)))
    middle = stream + low_back(jnp.dot(attended, w_out, precision=PRECISE))
    normed_ffn = low(rms_scale(middle, gain_ffn))
    gate_act = low_back(jnp.dot(normed_ffn, w_gate, precision=PRECISE))
    up_act = low_back(jnp.dot(normed_ffn, w_up, precision=PRECISE))
    hidden = low(jax.nn.gelu(gate_act, approximate=True) * up_act)
    return middle + low_back(jnp.dot(hidden, w_down, precision=PRECISE))

def encode_group(param_list, ids, seq_lengths):
    embed_t, conv_w, conv_b, scorer_v, norm_a, w_query, w_key, w_value, w_out, norm_f, w_gate, w_up, w_down = param_list
    stream, ends = mix_bytes(ids, seq_lengths, embed_t, conv_w, conv_b, scorer_v)
    row_count = stream.shape[0]
    tok_seg = segment_of(2 * jnp.arange(row_count, dtype=jnp.int32), ends)
    for layer_index in range(norm_a.shape[0]):
        stream = encoder_layer(stream, tok_seg, norm_a[layer_index], w_query[layer_index], w_key[layer_index], w_value[layer_index], w_out[layer_index], norm_f[layer_index], w_gate[layer_index], w_up[layer_index], w_down[layer_index])
    return stream

def reference(byte_ids, lengths, embed, conv_weight, conv_bias, scorer, norm_attn, query_w, key_w, value_w, attn_out_w, norm_ffn, gate_w, up_w, down_w, out_grad):
    params = tuple((param.astype(jnp.float32) for param in (embed, conv_weight, conv_bias, scorer, norm_attn, query_w, key_w, value_w, attn_out_w, norm_ffn, gate_w, up_w, down_w)))

    def whole_pass(param_list):

        def per_group(group_item):
            return encode_group(param_list, group_item[0], group_item[1])
        return lax.map(per_group, (byte_ids, lengths))
    encoded, back_fn = jax.vjp(whole_pass, params)
    grads = back_fn(out_grad.astype(jnp.float32))[0]
    return (encoded.astype(jnp.bfloat16), grads[0], grads[1], grads[2], grads[3], grads[4], grads[5], grads[6], grads[7], grads[8], grads[9], grads[10], grads[11], grads[12])
```

```python
import functools
import jax
import jax.numpy as jnp
from jax import lax
from jax.experimental import pallas as pl
from jax.experimental.pallas import tpu as pltpu
from jax.sharding import PartitionSpec as P
MESH = pl.DeviceIdType.MESH
CORES = 2


def grid_of():
    dp, ctx = lax.axis_size("dp"), lax.axis_size("ctx")
    rows = 2 if ctx % 2 == 0 else 1
    return dp // CORES, rows, ctx // rows


def place_of():
    _, _, nx = grid_of()
    d, c = lax.axis_index("dp"), lax.axis_index("ctx")
    return d // CORES, d % CORES, c // nx, c % nx


def device(z, core, y, x):
    _, _, nx = grid_of()
    return (z * CORES + core, y * nx + x)


def peers():
    nz, ny, nx = grid_of()
    z, core, y, x = place_of()
    zs = [lax.rem(z + i, nz) for i in range(1, nz)]
    ys = [lax.rem(y + i, ny) for i in range(1, ny)]
    xs = [lax.rem(x + i, nx) for i in range(1, nx)]
    return zs, ys, xs


def greet(extra=()):
    z, core, y, x = place_of()
    zs, ys, xs = peers()
    barrier = pltpu.get_barrier_semaphore()
    targets = [device(p, core, y, x) for p in zs]
    targets += [device(z, core, p, x) for p in ys]
    targets += [device(z, core, y, p) for p in xs]
    targets += [device(z, 1 - core, y, x)]
    targets += list(extra)
    for target in targets:
        pl.semaphore_signal(barrier, inc=1, device_id=target, device_id_type=MESH)
    pl.semaphore_wait(barrier, len(targets))


def remote(src, dst, sems, k, target):
    return pltpu.make_async_remote_copy(
        src_ref=src, dst_ref=dst, send_sem=sems.at[0, k], recv_sem=sems.at[1, k],
        device_id=target, device_id_type=MESH)


def halves(width):
    left = -(-width // 256) * 128
    return pl.ds(0, left), pl.ds(left, width - left)


class GatherChunk:
    def __init__(self, shard, out, sems, local_sem):
        self.shard, self.out, self.sems, self.local_sem = shard, out, sems, local_sem
        self.halves = halves(shard.shape[-1])
        self.started = []

    @staticmethod
    def count():
        nz, ny, nx = grid_of()
        return (nz - 1) + 2 * (nx - 1) + 2 * (ny - 1) + 1

    def send(self, where, target, kind):
        k = sum(len(group) for group in self.started) + len(self.current)
        copy = remote(self.out.at[where], self.out.at[where], self.sems, k, target)
        copy.start()
        self.current.append(copy)

    def stage(self, number):
        z, core, y, x = place_of()
        zs, ys, xs = peers()
        left, right = self.halves
        if number > 1:
            for copy in self.started[-1]:
                copy.wait_recv()
        self.current = []
        if number == 0:
            own = pltpu.make_async_copy(self.shard, self.out.at[z, core, y, x], self.local_sem)
            own.start()
            for i, p in enumerate(zs):
                copy = remote(self.shard, self.out.at[z, core, y, x], self.sems, i, device(p, core, y, x))
                copy.start()
                self.current.append(copy)
            self.own = own
        elif number == 1:
            for copy in self.started[-1]:
                copy.wait_recv()
            self.own.wait()
            for p in xs:
                self.send((slice(None), core, y, x, slice(None), left), device(z, core, y, p), 0)
            for p in ys:
                self.send((slice(None), core, y, x, slice(None), right), device(z, core, p, x), 0)
        elif number == 2:
            for p in ys:
                self.send((slice(None), core, y, slice(None), slice(None), left), device(z, core, p, x), 0)
            for p in xs:
                self.send((slice(None), core, slice(None), x, slice(None), right), device(z, core, y, p), 0)
        elif number == 3:
            self.send((slice(None), core), device(z, 1 - core, y, x), 0)
        self.started.append(self.current)
        if number == 4:
            for group in self.started:
                for copy in group:
                    copy.wait_send()


def gather_kernel(n, *refs):
    shards, outs, (sems, local_sems) = refs[:n], refs[n:2 * n], refs[2 * n:]
    greet()
    chunks = [GatherChunk(shards[i], outs[i], sems.at[i], local_sems.at[i]) for i in range(n)]
    for t in range(n + 4):
        for number in range(4):
            if 0 <= t - number < n:
                chunks[t - number].stage(number)
    for chunk in chunks:
        chunk.stage(4)


def gather_all(shards, collective_id):
    nz, ny, nx = grid_of()
    n = len(shards)
    outs = pl.pallas_call(
        functools.partial(gather_kernel, n),
        out_shape=[jax.ShapeDtypeStruct((nz, CORES, ny, nx) + s.shape, s.dtype) for s in shards],
        in_specs=[pl.BlockSpec(memory_space=pl.ANY)] * n,
        out_specs=[pl.BlockSpec(memory_space=pl.ANY)] * n,
        scratch_shapes=[pltpu.SemaphoreType.DMA((n, 2, GatherChunk.count())), pltpu.SemaphoreType.DMA((n,))],
        compiler_params=pltpu.CompilerParams(collective_id=collective_id, has_side_effects=True),
        name="gather_weights",
    )(*shards)
    return [o.reshape((-1,) + o.shape[5:]) for o in outs]


def add_into(dst, src, lead):
    if not lead:
        dst[...] = (dst[...].astype(jnp.float32) + src[...].astype(jnp.float32)).astype(dst.dtype)
        return

    def body(i, carry):
        add_into(dst.at[i], src.at[i], lead[1:])
        return carry
    lax.fori_loop(0, lead[0], body, 0)


class ScatterChunk:
    def __init__(self, parts, out, held, across, first, second, last, sems, local_sem):
        self.parts, self.out, self.held, self.across = parts, out, held, across
        self.first, self.second, self.last, self.sems, self.local_sem = first, second, last, sems, local_sem
        self.halves = halves(parts.shape[-1])
        self.copies = []
        self.k = 0

    count = GatherChunk.count

    @staticmethod
    def scratch(shape, dtype):
        nz, ny, nx = grid_of()
        r, n = shape
        return [pltpu.VMEM((nz, ny, nx, r, n), dtype), pltpu.VMEM((nz, ny, nx, r, n), dtype),
                pltpu.VMEM((nx - 1, nz, ny, r, halves(n)[0].size), dtype), pltpu.VMEM((ny - 1, nz, nx, r, halves(n)[1].size), dtype),
                pltpu.VMEM((ny - 1, nz, r, halves(n)[0].size), dtype), pltpu.VMEM((nx - 1, nz, r, halves(n)[1].size), dtype),
                pltpu.VMEM((nz - 1, r, n), dtype)]

    def send(self, src, dst, target):
        copy = remote(src, dst, self.sems, self.k, target)
        self.k += 1
        copy.start()
        self.current.append(copy)

    def stage(self, number):
        nz, ny, nx = grid_of()
        z, core, y, x = place_of()
        zs, ys, xs = peers()
        left, right = self.halves
        held = self.held
        every = slice(None)
        if number:
            for copy in self.current:
                copy.wait_recv()
        done = self.current if number else []
        self.current = []
        if number == 0:
            self.own = pltpu.make_async_copy(self.parts.at[:, core], held, self.local_sem)
            self.own.start()
            self.send(self.parts.at[:, 1 - core], self.across, device(z, 1 - core, y, x))
        elif number == 1:
            self.own.wait()
            add_into(held, self.across, (nz, ny, nx))
            for i, p in enumerate(xs):
                self.send(held.at[:, :, p, :, left], self.first[0].at[i], device(z, core, y, p))
            for i, p in enumerate(ys):
                self.send(held.at[:, p, :, :, right], self.first[1].at[i], device(z, core, p, x))
        elif number == 2:
            for i in range(nx - 1):
                add_into(held.at[:, :, x, :, left], self.first[0].at[i], (nz, ny))
            for i in range(ny - 1):
                add_into(held.at[:, y, :, :, right], self.first[1].at[i], (nz, nx))
            for i, p in enumerate(ys):
                self.send(held.at[:, p, x, :, left], self.second[0].at[i], device(z, core, p, x))
            for i, p in enumerate(xs):
                self.send(held.at[:, y, p, :, right], self.second[1].at[i], device(z, core, y, p))
        elif number == 3:
            for i in range(ny - 1):
                add_into(held.at[:, y, x, :, left], self.second[0].at[i], (nz,))
            for i in range(nx - 1):
                add_into(held.at[:, y, x, :, right], self.second[1].at[i], (nz,))
            for i, p in enumerate(zs):
                self.send(held.at[p, y, x], self.last.at[i], device(p, core, y, x))
        elif number == 4:
            total = held[z, y, x].astype(jnp.float32)
            for i in range(nz - 1):
                total = total + self.last[i].astype(jnp.float32)
            self.out[...] = total
        self.copies += done
        if number == 4:
            for copy in self.copies:
                copy.wait_send()


def scatter_kernel(n, *refs):
    parts, outs, rest = refs[:n], refs[n:2 * n], refs[2 * n:]
    sems, local_sems = rest[-2:]
    greet()
    chunks = []
    for i in range(n):
        s = rest[7 * i:7 * i + 7]
        chunks.append(ScatterChunk(parts[i], outs[i], s[0], s[1], s[2:4], s[4:6], s[6], sems.at[i], local_sems.at[i]))
    for t in range(n + 4):
        for number in range(5):
            if 0 <= t - number < n:
                chunks[t - number].stage(number)


def scatter_all(parts, collective_id):
    nz, ny, nx = grid_of()
    n = len(parts)
    devices = nz * CORES * ny * nx
    parts = [p.reshape((nz, CORES, ny, nx, p.shape[0] // devices) + p.shape[1:]) for p in parts]
    scratch = []
    for p in parts:
        scratch += ScatterChunk.scratch(p.shape[4:], p.dtype)
    return pl.pallas_call(
        functools.partial(scatter_kernel, n),
        out_shape=[jax.ShapeDtypeStruct(p.shape[4:], jnp.float32) for p in parts],
        in_specs=[pl.BlockSpec(memory_space=pl.ANY)] * n,
        out_specs=[pl.BlockSpec(memory_space=pltpu.VMEM)] * n,
        scratch_shapes=scratch + [pltpu.SemaphoreType.DMA((n, 2, GatherChunk.count())), pltpu.SemaphoreType.DMA((n,))],
        compiler_params=pltpu.CompilerParams(collective_id=collective_id, has_side_effects=True, vmem_limit_bytes=60 << 20),
        name="scatter_grads",
    )(*parts)

HEADS = 12
HEAD_DIM = 64
CONV = 4


NORM_EPS = 1e-06
NEG_FILL = -1000000000.0
PRECISE = lax.Precision.HIGHEST


def padded(shard, sides, width):
    for axis, dim in sides:
        count, length = (lax.axis_size(axis), shard.shape[dim])
        up = [(i, (i + 1) % count) for i in range(count - 1)]
        down = [(j, i) for i, j in up]
        last = lax.slice_in_dim(shard, length - width, length, axis=dim)
        leading = lax.slice_in_dim(shard, 0, width, axis=dim)
        before = lax.ppermute(last, axis, up)
        after = lax.ppermute(leading, axis, down)
        shard = jnp.concatenate([before, shard, after], axis=dim)
    return shard


def rms_scale(values, gain):
    return values * lax.rsqrt(jnp.mean(values * values, -1, keepdims=True) + NORM_EPS) * gain


def gated_unit(gate_act, up_act):
    return jax.nn.gelu(gate_act, approximate=True) * up_act


def segment_of(places, ends):
    return jnp.sum((places[:, None] >= ends[None, :]).astype(jnp.int32), 1)


def offset_in(places, segs, ends, seq_lengths):
    starts = ends - seq_lengths
    picks = segs[:, None] == jnp.arange(ends.shape[0], dtype=jnp.int32)[None, :]
    return places - jnp.sum(jnp.where(picks, starts[None, :], 0), 1)


def gbst_mix(byte_ext, valid_ext, seg_ext, rel_ext, embed_t, conv_w, conv_b, scorer_v):
    width_ext = byte_ext.shape[0]
    byte_count = width_ext - 10
    onehot = (byte_ext[:, None] == jnp.arange(embed_t.shape[0], dtype=jnp.int32)[None, :]).astype(
        jnp.float32
    )
    onehot = onehot * valid_ext[:, None]
    embedded = jnp.dot(onehot, embed_t, precision=PRECISE)
    conv_span = width_ext - 3
    conv_out = conv_b[None, :] + sum(
        (
            conv_w[tap][None, :]
            * embedded[tap : tap + conv_span]
            * (seg_ext[tap : tap + conv_span] == seg_ext[1 : 1 + conv_span]).astype(jnp.float32)[
                :, None
            ]
            for tap in range(4)
        )
    )
    conv_out = conv_out * valid_ext[1 : 1 + conv_span, None]
    own_seg = seg_ext[5 : 5 + byte_count]
    own_rel = rel_ext[5 : 5 + byte_count]
    pooled_list = []
    for block_size in (1, 2, 3, 4):
        pooled = jnp.zeros((byte_count, embed_t.shape[1]), jnp.float32)
        for shift_by in range(1 - block_size, block_size):
            same = (seg_ext[5 + shift_by : 5 + shift_by + byte_count] == own_seg) & (
                (own_rel + shift_by) // block_size == own_rel // block_size
            )
            weight = jnp.where(same, 1.0 / block_size, 0.0).astype(jnp.float32)
            pooled = pooled + weight[:, None] * conv_out[4 + shift_by : 4 + shift_by + byte_count]
        pooled_list.append(pooled)
    stacked = jnp.stack(pooled_list)
    logits = jnp.einsum("bnd,d->bn", stacked, scorer_v, precision=PRECISE)
    choose = jax.nn.softmax(logits, 0)
    chosen = jnp.sum(choose[..., None] * stacked, 0)
    return chosen.reshape(byte_count // 2, 2, -1).mean(1)


def block_scores(q_heads, key_block, q_seg, key_seg_row):
    scores = jnp.einsum("qhd,khd->hqk", q_heads, key_block, preferred_element_type=jnp.float32)
    same = q_seg[None, :, None] == key_seg_row[None, None, :]
    return jnp.where(same, scores, NEG_FILL)


def softmax_totals(q_heads, q_seg, key_blocks, seg_blocks):
    row_count, head_count = (q_heads.shape[0], q_heads.shape[1])

    def softmax_block_step(state_pair, block_item):
        top_score, exp_total = state_pair
        key_block, seg_row = block_item
        scores = block_scores(q_heads, key_block, q_seg, seg_row)
        new_top = jnp.maximum(top_score, jnp.max(scores, -1))
        exp_total = exp_total * jnp.exp(top_score - new_top) + jnp.sum(
            jnp.exp(scores - new_top[..., None]), -1
        )
        return ((new_top, exp_total), None)

    initial = (
        jnp.full((head_count, row_count), NEG_FILL, jnp.float32),
        jnp.zeros((head_count, row_count), jnp.float32),
    )
    (top_score, exp_total), _ = lax.scan(softmax_block_step, initial, (key_blocks, seg_blocks))
    return top_score + jnp.log(exp_total)


def weighted_values(q_heads, q_seg, key_blocks, value_blocks, seg_blocks, log_total):

    def weighted_block_step(running, block_item):
        key_block, value_block, seg_row = block_item
        attn_probs = jnp.exp(
            block_scores(q_heads, key_block, q_seg, seg_row) - log_total[..., None]
        )
        running = running + jnp.einsum(
            "hqk,khd->qhd",
            attn_probs.astype(jnp.bfloat16),
            value_block,
            preferred_element_type=jnp.float32,
        )
        return (running, None)

    running, _ = lax.scan(
        weighted_block_step,
        jnp.zeros(q_heads.shape, jnp.float32),
        (key_blocks, value_blocks, seg_blocks),
    )
    return running


def attention_back(q_heads, q_seg, key_blocks, value_blocks, seg_blocks, log_total, grad_heads):

    def inner_step(running, block_item):
        key_block, value_block, seg_row = block_item
        attn_probs = jnp.exp(
            block_scores(q_heads, key_block, q_seg, seg_row) - log_total[..., None]
        )
        grad_probs = jnp.einsum(
            "qhd,khd->hqk", grad_heads, value_block, preferred_element_type=jnp.float32
        )
        return (running + jnp.sum(attn_probs * grad_probs, -1), None)

    inner_sum, _ = lax.scan(
        inner_step, jnp.zeros(log_total.shape, jnp.float32), (key_blocks, value_blocks, seg_blocks)
    )

    def grad_step(running, block_item):
        key_block, value_block, seg_row = block_item
        attn_probs = jnp.exp(
            block_scores(q_heads, key_block, q_seg, seg_row) - log_total[..., None]
        )
        grad_probs = jnp.einsum(
            "qhd,khd->hqk", grad_heads, value_block, preferred_element_type=jnp.float32
        )
        grad_scores = (attn_probs * (grad_probs - inner_sum[..., None])).astype(jnp.bfloat16)
        running = running + jnp.einsum(
            "hqk,khd->qhd", grad_scores, key_block, preferred_element_type=jnp.float32
        )
        grad_key = jnp.einsum(
            "hqk,qhd->khd", grad_scores, q_heads, preferred_element_type=jnp.float32
        )
        grad_value = jnp.einsum(
            "hqk,qhd->khd",
            attn_probs.astype(jnp.bfloat16),
            grad_heads,
            preferred_element_type=jnp.float32,
        )
        return (running, (grad_key, grad_value))

    grad_query, key_parts = lax.scan(
        grad_step, jnp.zeros(q_heads.shape, jnp.float32), (key_blocks, value_blocks, seg_blocks)
    )
    grad_key, grad_value = key_parts
    merged = grad_key.shape[2] * grad_key.shape[3]
    return (grad_query, inner_sum, grad_key.reshape(-1, merged), grad_value.reshape(-1, merged))


def layer_forward(stream_in, weights, masks):
    gain_attn, w_query, w_key, w_value, w_out, gain_ffn, w_gate, w_up, w_down = weights
    q_seg, tok_seg, seg_blocks = masks
    row_count = stream_in.shape[0]
    normed = rms_scale(stream_in, gain_attn.astype(jnp.float32)).astype(jnp.bfloat16)
    query_act = jnp.dot(normed, w_query, preferred_element_type=jnp.float32).astype(jnp.bfloat16)
    key_act = jnp.dot(normed, w_key, preferred_element_type=jnp.float32).astype(jnp.bfloat16)
    value_act = jnp.dot(normed, w_value, preferred_element_type=jnp.float32).astype(jnp.bfloat16)
    both = lax.all_gather(jnp.concatenate([key_act, value_act], 1), "ctx", axis=0, tiled=True)
    key_all, value_all = both[:, : both.shape[1] // 2], both[:, both.shape[1] // 2 :]
    block_count, block_rows = seg_blocks.shape
    q_heads = query_act.reshape(row_count, HEADS, HEAD_DIM)
    key_own = key_act.reshape(row_count, HEADS, HEAD_DIM)
    value_own = value_act.reshape(row_count, HEADS, HEAD_DIM)
    key_blocks = key_all.reshape(block_count, block_rows, HEADS, HEAD_DIM)
    value_blocks = value_all.reshape(block_count, block_rows, HEADS, HEAD_DIM)
    log_total = softmax_totals(q_heads, q_seg, key_blocks, seg_blocks)
    attended = weighted_values(q_heads, q_seg, key_blocks, value_blocks, seg_blocks, log_total)
    attended = attended.reshape(row_count, -1).astype(jnp.bfloat16)
    middle = stream_in + jnp.dot(attended, w_out, preferred_element_type=jnp.float32)
    normed_ffn = rms_scale(middle, gain_ffn.astype(jnp.float32)).astype(jnp.bfloat16)
    gate_act = jnp.dot(normed_ffn, w_gate, preferred_element_type=jnp.float32)
    up_act = jnp.dot(normed_ffn, w_up, preferred_element_type=jnp.float32)
    hidden = gated_unit(gate_act, up_act).astype(jnp.bfloat16)
    result = middle + jnp.dot(hidden, w_down, preferred_element_type=jnp.float32)
    saved = (
        normed,
        q_heads,
        key_own,
        value_own,
        key_blocks,
        value_blocks,
        log_total,
        attended,
        middle,
        normed_ffn,
        gate_act,
        up_act,
        hidden,
    )
    return (result, saved)


def layer_backward(stream_in, weights, masks, saved, grad_out):
    gain_attn, w_query, w_key, w_value, w_out, gain_ffn, w_gate, w_up, w_down = weights
    q_seg, tok_seg, seg_blocks = masks
    (
        normed,
        q_heads,
        key_own,
        value_own,
        key_blocks,
        value_blocks,
        log_total,
        attended,
        middle,
        normed_ffn,
        gate_act,
        up_act,
        hidden,
    ) = saved
    row_count = stream_in.shape[0]
    grad_f = grad_out.astype(jnp.bfloat16)
    d_down = jnp.dot(hidden.T, grad_f, preferred_element_type=jnp.float32)
    grad_hidden = jnp.dot(grad_f, w_down.T, preferred_element_type=jnp.float32)
    _, gated_back = jax.vjp(gated_unit, gate_act, up_act)
    grad_gate, grad_up = gated_back(grad_hidden)
    grad_gate = grad_gate.astype(jnp.bfloat16)
    grad_up = grad_up.astype(jnp.bfloat16)
    d_gate = jnp.dot(normed_ffn.T, grad_gate, preferred_element_type=jnp.float32)
    d_up = jnp.dot(normed_ffn.T, grad_up, preferred_element_type=jnp.float32)
    grad_nffn = jnp.dot(grad_gate, w_gate.T, preferred_element_type=jnp.float32) + jnp.dot(
        grad_up, w_up.T, preferred_element_type=jnp.float32
    )
    _, norm_back = jax.vjp(rms_scale, middle, gain_ffn.astype(jnp.float32))
    grad_mid, d_gain_ffn = norm_back(grad_nffn)
    grad_mid = grad_mid + grad_out
    grad_att = grad_mid.astype(jnp.bfloat16)
    d_out = jnp.dot(attended.T, grad_att, preferred_element_type=jnp.float32)
    grad_heads = jnp.dot(grad_att, w_out.T, preferred_element_type=jnp.float32).astype(jnp.bfloat16)
    grad_heads = grad_heads.reshape(row_count, HEADS, HEAD_DIM)
    grad_query, inner_sum, grad_key_all, grad_value_all = attention_back(
        q_heads, q_seg, key_blocks, value_blocks, seg_blocks, log_total, grad_heads
    )
    both = lax.psum_scatter(
        jnp.concatenate([grad_key_all, grad_value_all], 1).astype(jnp.bfloat16), "ctx", scatter_dimension=0, tiled=True
    )
    grad_key, grad_value = both[:, : both.shape[1] // 2], both[:, both.shape[1] // 2 :]
    grad_query = grad_query.reshape(row_count, -1).astype(jnp.bfloat16)
    grad_key = grad_key.astype(jnp.bfloat16)
    grad_value = grad_value.astype(jnp.bfloat16)
    d_query = jnp.dot(normed.T, grad_query, preferred_element_type=jnp.float32)
    d_key = jnp.dot(normed.T, grad_key, preferred_element_type=jnp.float32)
    d_value = jnp.dot(normed.T, grad_value, preferred_element_type=jnp.float32)
    grad_normed = (
        jnp.dot(grad_query, w_query.T, preferred_element_type=jnp.float32)
        + jnp.dot(grad_key, w_key.T, preferred_element_type=jnp.float32)
        + jnp.dot(grad_value, w_value.T, preferred_element_type=jnp.float32)
    )
    _, first_back = jax.vjp(rms_scale, stream_in, gain_attn.astype(jnp.float32))
    grad_in, d_gain_attn = first_back(grad_normed)
    grad_in = grad_in + grad_mid
    return (
        grad_in,
        (d_gain_attn, d_query, d_key, d_value, d_out, d_gain_ffn, d_gate, d_up, d_down),
    )


def packed_small(embed, conv_weight, conv_bias, scorer, norm_attn, norm_ffn):
    rows = jnp.concatenate([embed, conv_weight, conv_bias[None], scorer[None], norm_attn, norm_ffn], 0).T
    return jnp.pad(rows, ((0, 0), (0, -rows.shape[1] % 128)))


def split_small(rows, vocab, layers):
    at = vocab + CONV
    return (rows[:vocab], rows[vocab:at], rows[at], rows[at + 1], rows[at + 2 : at + 2 + layers],
            rows[at + 2 + layers : at + 2 + 2 * layers])


def on_device(
    byte_ids,
    lengths,
    embed,
    conv_weight,
    conv_bias,
    scorer,
    norm_attn,
    query_w,
    key_w,
    value_w,
    attn_out_w,
    norm_ffn,
    gate_w,
    up_w,
    down_w,
    out_grad,
):
    ctx_count = lax.axis_size("ctx")
    ctx_place = lax.axis_index("ctx")
    layer_count = query_w.shape[0]
    vocab = embed.shape[0]
    model = query_w.shape[2]
    byte_count = byte_ids.shape[1]
    tok_count = byte_count // 2
    seq_lengths = lengths[0]
    at = jnp.arange(seq_lengths.shape[0])
    ends = jnp.sum(jnp.where(at[:, None] >= at[None, :], seq_lengths[None, :], 0), 1).astype(jnp.int32)
    total_bytes = ends[-1]
    first_byte = ctx_place * byte_count
    byte_ext = padded(byte_ids[0], (("ctx", 0),), 5)
    ext_places = first_byte - 5 + jnp.arange(byte_count + 10, dtype=jnp.int32)
    valid_ext = ((ext_places >= 0) & (ext_places < total_bytes)).astype(jnp.float32)
    seg_ext = segment_of(ext_places, ends)
    rel_ext = offset_in(ext_places, seg_ext, ends, seq_lengths)
    group_tok = tok_count * ctx_count
    block_rows = min(512, group_tok)
    tok_seg = segment_of(2 * jnp.arange(group_tok, dtype=jnp.int32), ends)
    q_seg = segment_of(first_byte + 2 * jnp.arange(tok_count, dtype=jnp.int32), ends)
    seg_blocks = tok_seg.reshape(group_tok // block_rows, block_rows)
    masks = (q_seg, tok_seg, seg_blocks)

    small = packed_small(embed, conv_weight, conv_bias, scorer, norm_attn, norm_ffn)
    shards = [small]
    for layer in range(layer_count):
        shards.append(jnp.concatenate([query_w[layer], key_w[layer], value_w[layer], attn_out_w[layer]], 1))
        shards.append(jnp.concatenate([gate_w[layer], up_w[layer]], 1))
        shards.append(down_w[layer])
    small_full, *full = [a.reshape(-1, a.shape[-1]) for a in gather_all(shards, 0)]
    embed_full, conv_full, bias_full, scorer_full, norm_a, norm_f = split_small(small_full.T, vocab, layer_count)

    def gbst_local(embed_t, conv_w, conv_b, scorer_v):
        return gbst_mix(byte_ext, valid_ext, seg_ext, rel_ext, embed_t, conv_w, conv_b, scorer_v)

    stream, gbst_back = jax.vjp(
        gbst_local,
        embed_full.astype(jnp.float32),
        conv_full.astype(jnp.float32),
        bias_full.astype(jnp.float32),
        scorer_full.astype(jnp.float32),
    )
    kept = []
    for layer in range(layer_count):
        attn, ffn, down = full[3 * layer : 3 * layer + 3]
        weights = (norm_a[layer], attn[:, :model], attn[:, model : 2 * model], attn[:, 2 * model : 3 * model],
                   attn[:, 3 * model :], norm_f[layer], ffn[:, : ffn.shape[1] // 2], ffn[:, ffn.shape[1] // 2 :], down)
        before = stream
        stream, saved = layer_forward(stream, weights, masks)
        kept.append((before, weights, saved))
    encoded = stream.astype(jnp.bfloat16)[None]
    grad_stream = out_grad[0].astype(jnp.float32)
    partial = []
    gains = []
    for layer in reversed(range(layer_count)):
        before, weights, saved = kept[layer]
        grad_stream, grads = layer_backward(before, weights, masks, saved, grad_stream)
        d_gain_attn, d_query, d_key, d_value, d_out, d_gain_ffn, d_gate, d_up, d_down = grads
        partial = [jnp.concatenate([d_query, d_key, d_value, d_out], 1), jnp.concatenate([d_gate, d_up], 1), d_down] + partial
        gains = [(d_gain_attn, d_gain_ffn)] + gains
    grads = gbst_back(grad_stream)
    small_grad = packed_small(*grads, jnp.stack([a for a, _ in gains]), jnp.stack([f for _, f in gains]))
    outs = scatter_all([p.astype(jnp.bfloat16) for p in [small_grad] + partial], 1)
    small_out, *rest = outs
    g_embed, g_conv, g_bias, g_scorer, g_norm_a, g_norm_f = split_small(small_out.T, vocab, layer_count)
    attn_out, ffn_out, down_out = rest[0::3], rest[1::3], rest[2::3]
    columns = [jnp.stack([a[:, i * model : (i + 1) * model] for a in attn_out]) for i in range(4)]
    wide = ffn_out[0].shape[1] // 2
    return (
        encoded,
        g_embed,
        g_conv,
        g_bias,
        g_scorer,
        g_norm_a,
        columns[0],
        columns[1],
        columns[2],
        columns[3],
        g_norm_f,
        jnp.stack([a[:, :wide] for a in ffn_out]),
        jnp.stack([a[:, wide:] for a in ffn_out]),
        jnp.stack(down_out),
    )


def solution(mesh):
    placed = (
        P("dp", "ctx"),
        P("dp", None),
        P(None, ("dp", "ctx")),
        P(None, ("dp", "ctx")),
        P(("dp", "ctx")),
        P(("dp", "ctx")),
        P(None, ("dp", "ctx")),
        P(None, ("dp", "ctx"), None),
        P(None, ("dp", "ctx"), None),
        P(None, ("dp", "ctx"), None),
        P(None, ("dp", "ctx"), None),
        P(None, ("dp", "ctx")),
        P(None, ("dp", "ctx"), None),
        P(None, ("dp", "ctx"), None),
        P(None, ("dp", "ctx"), None),
        P("dp", "ctx", None),
    )
    return jax.shard_map(
        on_device,
        mesh=mesh,
        in_specs=placed,
        out_specs=(
            P("dp", "ctx", None),
            P(None, ("dp", "ctx")),
            P(None, ("dp", "ctx")),
            P(("dp", "ctx")),
            P(("dp", "ctx")),
            P(None, ("dp", "ctx")),
            P(None, ("dp", "ctx"), None),
            P(None, ("dp", "ctx"), None),
            P(None, ("dp", "ctx"), None),
            P(None, ("dp", "ctx"), None),
            P(None, ("dp", "ctx")),
            P(None, ("dp", "ctx"), None),
            P(None, ("dp", "ctx"), None),
            P(None, ("dp", "ctx"), None),
        ),
        check_vma=False,
    )
```

```python
import functools
import jax
import jax.numpy as jnp
from jax import lax
from jax.experimental import pallas as pl
from jax.experimental.pallas import tpu as pltpu
from jax.sharding import PartitionSpec as P


CONV = 4
PRECISE = lax.Precision.HIGHEST


def padded(shard, sides, width):
    for axis, dim in sides:
        count, length = (lax.axis_size(axis), shard.shape[dim])
        up = [(i, (i + 1) % count) for i in range(count - 1)]
        down = [(j, i) for i, j in up]
        last = lax.slice_in_dim(shard, length - width, length, axis=dim)
        leading = lax.slice_in_dim(shard, 0, width, axis=dim)
        before = lax.ppermute(last, axis, up)
        after = lax.ppermute(leading, axis, down)
        shard = jnp.concatenate([before, shard, after], axis=dim)
    return shard


MESH = pl.DeviceIdType.MESH
CORES = 2


def grid_of():
    dp, ctx = lax.axis_size("dp"), lax.axis_size("ctx")
    rows = 2 if ctx % 2 == 0 else 1
    return dp // CORES, rows, ctx // rows


def place_of():
    _, _, nx = grid_of()
    d, c = lax.axis_index("dp"), lax.axis_index("ctx")
    return d // CORES, d % CORES, c // nx, c % nx


def device(z, core, y, x):
    _, _, nx = grid_of()
    return (z * CORES + core, y * nx + x)


def peers():
    nz, ny, nx = grid_of()
    z, core, y, x = place_of()
    zs = [lax.rem(z + i, nz) for i in range(1, nz)]
    ys = [lax.rem(y + i, ny) for i in range(1, ny)]
    xs = [lax.rem(x + i, nx) for i in range(1, nx)]
    return zs, ys, xs


def greet(extra=()):
    z, core, y, x = place_of()
    zs, ys, xs = peers()
    barrier = pltpu.get_barrier_semaphore()
    targets = [device(p, core, y, x) for p in zs]
    targets += [device(z, core, p, x) for p in ys]
    targets += [device(z, core, y, p) for p in xs]
    targets += [device(z, 1 - core, y, x)]
    targets += list(extra)
    for target in targets:
        pl.semaphore_signal(barrier, inc=1, device_id=target, device_id_type=MESH)
    pl.semaphore_wait(barrier, len(targets))


def remote(src, dst, sems, k, target):
    return pltpu.make_async_remote_copy(
        src_ref=src, dst_ref=dst, send_sem=sems.at[0, k], recv_sem=sems.at[1, k],
        device_id=target, device_id_type=MESH)


def halves(width):
    left = -(-width // 256) * 128
    return pl.ds(0, left), pl.ds(left, width - left)


class GatherChunk:
    def __init__(self, shard, out, sems, local_sem):
        self.shard, self.out, self.sems, self.local_sem = shard, out, sems, local_sem
        self.halves = halves(shard.shape[-1])
        self.started = []

    @staticmethod
    def count():
        nz, ny, nx = grid_of()
        return (nz - 1) + 2 * (nx - 1) + 2 * (ny - 1) + 1

    def send(self, where, target, kind):
        k = sum(len(group) for group in self.started) + len(self.current)
        copy = remote(self.out.at[where], self.out.at[where], self.sems, k, target)
        copy.start()
        self.current.append(copy)

    def stage(self, number):
        z, core, y, x = place_of()
        zs, ys, xs = peers()
        left, right = self.halves
        if number > 1:
            for copy in self.started[-1]:
                copy.wait_recv()
        self.current = []
        if number == 0:
            own = pltpu.make_async_copy(self.shard, self.out.at[z, core, y, x], self.local_sem)
            own.start()
            for i, p in enumerate(zs):
                copy = remote(self.shard, self.out.at[z, core, y, x], self.sems, i, device(p, core, y, x))
                copy.start()
                self.current.append(copy)
            self.own = own
        elif number == 1:
            for copy in self.started[-1]:
                copy.wait_recv()
            self.own.wait()
            for p in xs:
                self.send((slice(None), core, y, x, slice(None), left), device(z, core, y, p), 0)
            for p in ys:
                self.send((slice(None), core, y, x, slice(None), right), device(z, core, p, x), 0)
        elif number == 2:
            for p in ys:
                self.send((slice(None), core, y, slice(None), slice(None), left), device(z, core, p, x), 0)
            for p in xs:
                self.send((slice(None), core, slice(None), x, slice(None), right), device(z, core, y, p), 0)
        elif number == 3:
            self.send((slice(None), core), device(z, 1 - core, y, x), 0)
        self.started.append(self.current)
        if number == 4:
            for group in self.started:
                for copy in group:
                    copy.wait_send()


def gather_kernel(n, *refs):
    shards, outs, (sems, local_sems) = refs[:n], refs[n:2 * n], refs[2 * n:]
    greet()
    chunks = [GatherChunk(shards[i], outs[i], sems.at[i], local_sems.at[i]) for i in range(n)]
    for t in range(n + 4):
        for number in range(4):
            if 0 <= t - number < n:
                chunks[t - number].stage(number)
    for chunk in chunks:
        chunk.stage(4)


def gather_all(shards, collective_id):
    nz, ny, nx = grid_of()
    n = len(shards)
    outs = pl.pallas_call(
        functools.partial(gather_kernel, n),
        out_shape=[jax.ShapeDtypeStruct((nz, CORES, ny, nx) + s.shape, s.dtype) for s in shards],
        in_specs=[pl.BlockSpec(memory_space=pl.ANY)] * n,
        out_specs=[pl.BlockSpec(memory_space=pl.ANY)] * n,
        scratch_shapes=[pltpu.SemaphoreType.DMA((n, 2, GatherChunk.count())), pltpu.SemaphoreType.DMA((n,))],
        compiler_params=pltpu.CompilerParams(collective_id=collective_id, has_side_effects=True),
        name="gather_weights",
    )(*shards)
    return [o.reshape((-1,) + o.shape[5:]) for o in outs]


def add_into(dst, src, lead):
    if not lead:
        dst[...] = (dst[...].astype(jnp.float32) + src[...].astype(jnp.float32)).astype(dst.dtype)
        return

    def body(i, carry):
        add_into(dst.at[i], src.at[i], lead[1:])
        return carry
    lax.fori_loop(0, lead[0], body, 0)


class ScatterChunk:
    def __init__(self, parts, out, held, across, first, second, last, sems, local_sem):
        self.parts, self.out, self.held, self.across = parts, out, held, across
        self.first, self.second, self.last, self.sems, self.local_sem = first, second, last, sems, local_sem
        self.halves = halves(parts.shape[-1])
        self.copies = []
        self.k = 0

    count = GatherChunk.count

    @staticmethod
    def scratch(shape, dtype):
        nz, ny, nx = grid_of()
        r, n = shape
        return [pltpu.VMEM((nz, ny, nx, r, n), dtype), pltpu.VMEM((nz, ny, nx, r, n), dtype),
                pltpu.VMEM((nx - 1, nz, ny, r, halves(n)[0].size), dtype), pltpu.VMEM((ny - 1, nz, nx, r, halves(n)[1].size), dtype),
                pltpu.VMEM((ny - 1, nz, r, halves(n)[0].size), dtype), pltpu.VMEM((nx - 1, nz, r, halves(n)[1].size), dtype),
                pltpu.VMEM((nz - 1, r, n), dtype)]

    def send(self, src, dst, target):
        copy = remote(src, dst, self.sems, self.k, target)
        self.k += 1
        copy.start()
        self.current.append(copy)

    def stage(self, number):
        nz, ny, nx = grid_of()
        z, core, y, x = place_of()
        zs, ys, xs = peers()
        left, right = self.halves
        held = self.held
        every = slice(None)
        if number:
            for copy in self.current:
                copy.wait_recv()
        done = self.current if number else []
        self.current = []
        if number == 0:
            self.own = pltpu.make_async_copy(self.parts.at[:, core], held, self.local_sem)
            self.own.start()
            self.send(self.parts.at[:, 1 - core], self.across, device(z, 1 - core, y, x))
        elif number == 1:
            self.own.wait()
            add_into(held, self.across, (nz, ny, nx))
            for i, p in enumerate(xs):
                self.send(held.at[:, :, p, :, left], self.first[0].at[i], device(z, core, y, p))
            for i, p in enumerate(ys):
                self.send(held.at[:, p, :, :, right], self.first[1].at[i], device(z, core, p, x))
        elif number == 2:
            for i in range(nx - 1):
                add_into(held.at[:, :, x, :, left], self.first[0].at[i], (nz, ny))
            for i in range(ny - 1):
                add_into(held.at[:, y, :, :, right], self.first[1].at[i], (nz, nx))
            for i, p in enumerate(ys):
                self.send(held.at[:, p, x, :, left], self.second[0].at[i], device(z, core, p, x))
            for i, p in enumerate(xs):
                self.send(held.at[:, y, p, :, right], self.second[1].at[i], device(z, core, y, p))
        elif number == 3:
            for i in range(ny - 1):
                add_into(held.at[:, y, x, :, left], self.second[0].at[i], (nz,))
            for i in range(nx - 1):
                add_into(held.at[:, y, x, :, right], self.second[1].at[i], (nz,))
            for i, p in enumerate(zs):
                self.send(held.at[p, y, x], self.last.at[i], device(p, core, y, x))
        elif number == 4:
            total = held[z, y, x].astype(jnp.float32)
            for i in range(nz - 1):
                total = total + self.last[i].astype(jnp.float32)
            self.out[...] = total
        self.copies += done
        if number == 4:
            for copy in self.copies:
                copy.wait_send()


def scatter_kernel(n, *refs):
    parts, outs, rest = refs[:n], refs[n:2 * n], refs[2 * n:]
    sems, local_sems = rest[-2:]
    greet()
    chunks = []
    for i in range(n):
        s = rest[7 * i:7 * i + 7]
        chunks.append(ScatterChunk(parts[i], outs[i], s[0], s[1], s[2:4], s[4:6], s[6], sems.at[i], local_sems.at[i]))
    for t in range(n + 4):
        for number in range(5):
            if 0 <= t - number < n:
                chunks[t - number].stage(number)


def scatter_all(parts, collective_id):
    nz, ny, nx = grid_of()
    n = len(parts)
    devices = nz * CORES * ny * nx
    parts = [p.reshape((nz, CORES, ny, nx, p.shape[0] // devices) + p.shape[1:]) for p in parts]
    scratch = []
    for p in parts:
        scratch += ScatterChunk.scratch(p.shape[4:], p.dtype)
    return pl.pallas_call(
        functools.partial(scatter_kernel, n),
        out_shape=[jax.ShapeDtypeStruct(p.shape[4:], jnp.float32) for p in parts],
        in_specs=[pl.BlockSpec(memory_space=pl.ANY)] * n,
        out_specs=[pl.BlockSpec(memory_space=pltpu.VMEM)] * n,
        scratch_shapes=scratch + [pltpu.SemaphoreType.DMA((n, 2, GatherChunk.count())), pltpu.SemaphoreType.DMA((n,))],
        compiler_params=pltpu.CompilerParams(collective_id=collective_id, has_side_effects=True, vmem_limit_bytes=60 << 20),
        name="scatter_grads",
    )(*parts)
HEADS = 12
HEAD_DIM = 64
CHUNK = 256
NORM_EPS = 1e-06
NEG_FILL = -1000000000.0
GELU_A = 0.7978845608028654
GELU_B = 0.044715


def dot(a, b):
    return jnp.dot(a, b, preferred_element_type=jnp.float32)


def dot_nt(a, b):
    return lax.dot_general(a, b, (((1,), (1,)), ((), ())), preferred_element_type=jnp.float32)


def low(v):
    return v.astype(jnp.bfloat16)


def flip(v):
    return low(v.astype(jnp.float32).T)


def inverse_rms(v):
    return lax.rsqrt(jnp.mean(v * v, -1, keepdims=True) + NORM_EPS)


def ends_of(lengths_ref):
    ends, total = [], 0
    for i in range(lengths_ref.shape[-1]):
        total = total + lengths_ref[0, i]
        ends.append(total)
    return ends


def segments(places, ends):
    seg = jnp.zeros(places.shape, jnp.int32)
    for end in ends:
        seg = seg + jnp.where(places >= end, 1, 0)
    return seg


def heads_each():
    return -(-HEADS // lax.axis_size("ctx"))


def others():
    size, me = lax.axis_size("ctx"), lax.axis_index("ctx")
    return [lax.rem(me + 1 + i, size) for i in range(size)]


def greet_group():
    barrier = pltpu.get_barrier_semaphore()
    peers_ = others()[:-1]
    for p in peers_:
        pl.semaphore_signal(barrier, inc=1, device_id=(lax.axis_index("dp"), p), device_id_type=MESH)
    pl.semaphore_wait(barrier, len(peers_))


def to_group(src, dst, sems, index, p):
    return pltpu.make_async_remote_copy(
        src_ref=src, dst_ref=dst, send_sem=sems.at[(0,) + index], recv_sem=sems.at[(1,) + index],
        device_id=(lax.axis_index("dp"), p), device_id_type=MESH)


def tokens_of(p, count):
    return pl.ds(pl.multiple_of(p * count, count), count)


def spread_heads(src, dst, sems, local_sem, each):
    me = lax.axis_index("ctx")
    count = src.shape[2]
    copies = []
    for h in range(each):
        rows = pl.ds(h * HEAD_DIM, HEAD_DIM)
        made = []
        for i, p in enumerate(others()):
            theirs = pl.ds(pl.multiple_of((p * each + h) * HEAD_DIM, HEAD_DIM), HEAD_DIM)
            a, b = src.at[:, theirs], dst.at[:, rows, tokens_of(me, count)]
            if i == lax.axis_size("ctx") - 1:
                copy = pltpu.make_async_copy(a, b, local_sem.at[h])
            else:
                copy = to_group(a, b, sems, (h, i), p)
            copy.start()
            made.append(copy)
        copies.append(made)
    return copies


def arrive(made):
    for copy in made[:-1]:
        copy.wait_recv()
    made[-1].wait()


def attention_forward(each, seg_all, ends, qkv, lse, out_send, att, qkv_copies, sems):
    size, me = lax.axis_size("ctx"), lax.axis_index("ctx")
    count = att.shape[1]
    copies = []
    for h in range(each):
        arrive(qkv_copies[h])
        rows = pl.ds(h * HEAD_DIM, HEAD_DIM)
        key = flip(qkv[1, rows, :])
        value_t = qkv[2, rows, :]
        theirs = pl.ds(pl.multiple_of((me * each + h) * HEAD_DIM, HEAD_DIM), HEAD_DIM)
        for i, p in enumerate(others()):
            tokens = tokens_of(p, count)
            seg_q = segments(2 * (p * count + lax.broadcasted_iota(jnp.int32, (1, count), 1)), ends)
            scores = dot(key, qkv[0, rows, tokens])
            scores = jnp.where(seg_all[...] == seg_q, scores, NEG_FILL)
            top = jnp.max(scores, 0, keepdims=True)
            probs = jnp.exp(scores - top)
            total = jnp.sum(probs, 0, keepdims=True)
            lse[h, :, tokens] = top + jnp.log(total)
            result = low(dot(value_t, low(probs)) / total)
            if i == size - 1:
                att[theirs, :] = result
            else:
                out_send[h, i] = result
                copy = to_group(out_send.at[h, i], att.at[theirs], sems, (h, i), p)
                copy.start()
                copies.append(copy)
    return copies


def gelu_parts(gate):
    inner = jnp.tanh(GELU_A * (gate + GELU_B * gate * gate * gate))
    half = 0.5 * (1.0 + inner)
    slope = half + 0.5 * gate * (1.0 - inner * inner) * GELU_A * (1.0 + 3.0 * GELU_B * gate * gate)
    return gate * half, slope


def layer_forward_kernel(lengths, x, gain_a, gain_f, w_attn_hbm, w_ffn_hbm, w_down_hbm,
                         out, middle, normed_t, qkv, lse, att, gate_out, up_out, nffn_t,
                         w_attn, w_ffn, w_down, qkv_all, out_send, seg_all, nffn,
                         sems_in, sems_out, local_sems, w_sems):
    each = heads_each()
    model = x.shape[1]
    loads = [pltpu.make_async_copy(a, b, w_sems.at[i]) for i, (a, b) in enumerate(
        ((w_attn_hbm, w_attn), (w_ffn_hbm, w_ffn), (w_down_hbm, w_down)))]
    for load in loads:
        load.start()
    greet_group()
    ends = ends_of(lengths)
    seg_all[...] = segments(2 * lax.broadcasted_iota(jnp.int32, seg_all.shape, 0), ends)
    stream = x[...]
    normed = low(stream * inverse_rms(stream) * gain_a[...])
    normed_t[...] = flip(normed)
    if qkv_all.shape[1] > model:
        qkv_all[:, model:, :] = jnp.zeros((3, qkv_all.shape[1] - model, qkv_all.shape[2]), jnp.bfloat16)
    loads[0].wait()
    for part in range(3):
        for c in range(model // CHUNK):
            columns = pl.ds(part * model + c * CHUNK, CHUNK)
            qkv_all[part, c * CHUNK:(c + 1) * CHUNK, :] = low(dot(normed, w_attn[:, columns]).T)
    qkv_copies = spread_heads(qkv_all, qkv, sems_in, local_sems, each)
    out_copies = attention_forward(each, seg_all, ends, qkv, lse, out_send, att, qkv_copies, sems_out)
    for copy in out_copies:
        copy.wait_recv()
    attended = flip(att[:model, :])
    mid = stream + dot(attended, w_attn[:, 3 * model:])
    middle[...] = mid
    after = low(mid * inverse_rms(mid) * gain_f[...])
    nffn[...] = after
    nffn_t[...] = flip(after)
    out[...] = mid
    loads[1].wait()
    loads[2].wait()
    hidden_count = w_down.shape[0]

    def step(c, carry):
        columns = pl.ds(pl.multiple_of(c * CHUNK, CHUNK), CHUNK)
        gate = dot(nffn[...], w_ffn[:, columns])
        up = dot(nffn[...], w_ffn[:, pl.ds(pl.multiple_of(hidden_count + c * CHUNK, CHUNK), CHUNK)])
        gate_out[:, columns] = gate
        up_out[:, columns] = up
        hidden = low(gelu_parts(gate)[0] * up)
        out[...] += dot(hidden, w_down[columns, :])
        return carry
    lax.fori_loop(0, hidden_count // CHUNK, step, 0)
    for made in qkv_copies:
        for copy in made[:-1]:
            copy.wait_send()
    for copy in out_copies:
        copy.wait_send()


VMEM = pl.BlockSpec(memory_space=pltpu.VMEM)
ANY = pl.BlockSpec(memory_space=pl.ANY)
SMEM = pl.BlockSpec(memory_space=pltpu.SMEM)


def layer_forward(lengths, x, gain_a, gain_f, w_attn, w_ffn, w_down, collective_id):
    size, each = lax.axis_size("ctx"), heads_each()
    count, model = x.shape
    wide = w_down.shape[0]
    group = count * size
    rows = each * size * HEAD_DIM
    f32, bf16 = jnp.float32, jnp.bfloat16
    made = lambda shape, dtype: jax.ShapeDtypeStruct(shape, dtype)
    return pl.pallas_call(
        layer_forward_kernel,
        out_shape=[made((count, model), f32), made((count, model), f32), made((model, count), bf16),
                   made((3, each * HEAD_DIM, group), bf16), made((each, 1, group), f32), made((rows, count), bf16),
                   made((count, wide), f32), made((count, wide), f32), made((model, count), bf16)],
        in_specs=[SMEM, VMEM, VMEM, VMEM, ANY, ANY, ANY],
        out_specs=[VMEM] * 9,
        scratch_shapes=[
            pltpu.VMEM(w_attn.shape, bf16), pltpu.VMEM(w_ffn.shape, bf16), pltpu.VMEM(w_down.shape, bf16),
            pltpu.VMEM((3, rows, count), bf16), pltpu.VMEM((each, size - 1, HEAD_DIM, count), bf16),
            pltpu.VMEM((group, count), jnp.int32), pltpu.VMEM((count, model), bf16),
            pltpu.SemaphoreType.DMA((2, each, size - 1)), pltpu.SemaphoreType.DMA((2, each, size - 1)),
            pltpu.SemaphoreType.DMA((each,)), pltpu.SemaphoreType.DMA((3,))],
        compiler_params=pltpu.CompilerParams(collective_id=collective_id, has_side_effects=True, vmem_limit_bytes=56 << 20),
        name="layer_forward",
    )(lengths, x, gain_a, gain_f, w_attn, w_ffn, w_down)


def layer_backward_kernel(lengths, grad, x, gain_a, gain_f, middle, normed_t, qkv, lse, att, gate_in, up_in, nffn_t,
                          w_attn_hbm, w_ffn_hbm, w_down_hbm,
                          grad_in, d_gain_a, d_gain_f, d_attn_hbm, d_ffn_hbm, d_down_hbm,
                          w_attn, w_ffn, w_down, d_attn, d_ffn, d_down, go_all, go, dqkv, q_send, kv_send, seg_all, total,
                          grad_low, mid_low, sems_in, sems_q, sems_kv, local_sems, w_sems, d_sems):
    each = heads_each()
    size, me = lax.axis_size("ctx"), lax.axis_index("ctx")
    count, model = x.shape
    wide = w_down.shape[0]
    loads = [pltpu.make_async_copy(a, b, w_sems.at[i]) for i, (a, b) in enumerate(
        ((w_down_hbm, w_down), (w_ffn_hbm, w_ffn), (w_attn_hbm, w_attn)))]
    for load in loads:
        load.start()
    greet_group()
    ends = ends_of(lengths)
    seg_all[...] = segments(2 * lax.broadcasted_iota(jnp.int32, seg_all.shape, 0), ends)
    grad_low[...] = low(grad[...])
    total[...] = jnp.zeros(total.shape, jnp.float32)
    loads[0].wait()
    loads[1].wait()

    def step(c, carry):
        columns = pl.ds(pl.multiple_of(c * CHUNK, CHUNK), CHUNK)
        later = pl.ds(pl.multiple_of(wide + c * CHUNK, CHUNK), CHUNK)
        g_hidden = dot_nt(grad_low[...], w_down[columns, :])
        up = up_in[:, columns]
        act, slope = gelu_parts(gate_in[:, columns])
        g_gate = low(g_hidden * up * slope)
        g_up = low(g_hidden * act)
        d_down[columns, :] = low(dot(low((act * up).T), grad_low[...]))
        d_ffn[:, columns] = low(dot(nffn_t[...], g_gate))
        d_ffn[:, later] = low(dot(nffn_t[...], g_up))
        total[...] += dot_nt(g_gate, w_ffn[:, columns]) + dot_nt(g_up, w_ffn[:, later])
        return carry
    lax.fori_loop(0, wide // CHUNK, step, 0)
    saves = [pltpu.make_async_copy(d_ffn, d_ffn_hbm, d_sems.at[0]), pltpu.make_async_copy(d_down, d_down_hbm, d_sems.at[1])]
    for save in saves:
        save.start()

    def norm_back(values, gain, upstream):
        scale = inverse_rms(values)
        scaled = upstream * gain
        along = jnp.mean(values * scaled, -1, keepdims=True)
        return scale * scaled - values * (scale * scale * scale * along), jnp.sum(upstream * values * scale, 0, keepdims=True)

    back, d_gain = norm_back(middle[...], gain_f[...], total[...])
    d_gain_f[...] = d_gain
    grad_in[...] = grad[...] + back
    mid_low[...] = low(grad_in[...])
    if go_all.shape[1] > model:
        go_all[:, model:, :] = jnp.zeros((1, go_all.shape[1] - model, count), jnp.bfloat16)
    loads[2].wait()
    for c in range(model // CHUNK):
        rows = slice(c * CHUNK, (c + 1) * CHUNK)
        go_all[0, rows, :] = low(dot_nt(mid_low[...], w_attn[rows, 3 * model:]).T)
    go_copies = spread_heads(go_all, go, sems_in, local_sems, each)
    for c in range(model // CHUNK):
        rows = slice(c * CHUNK, (c + 1) * CHUNK)
        d_attn[rows, 3 * model:] = low(dot(att[rows, :], mid_low[...]))
    sent = []
    for h in range(each):
        arrive(go_copies[h])
        rows = pl.ds(h * HEAD_DIM, HEAD_DIM)
        theirs = pl.ds(pl.multiple_of((me * each + h) * HEAD_DIM, HEAD_DIM), HEAD_DIM)
        key_t = qkv[1, rows, :]
        key, value = flip(key_t), flip(qkv[2, rows, :])
        g_key = jnp.zeros((HEAD_DIM, count * size), jnp.float32)
        g_value = jnp.zeros((HEAD_DIM, count * size), jnp.float32)
        for i, p in enumerate(others()):
            tokens = tokens_of(p, count)
            seg_q = segments(2 * (p * count + lax.broadcasted_iota(jnp.int32, (1, count), 1)), ends)
            query_t, go_t = qkv[0, rows, tokens], go[0, rows, tokens]
            scores = jnp.where(seg_all[...] == seg_q, dot(key, query_t), NEG_FILL)
            probs = jnp.exp(scores - lse[h, :, tokens])
            g_probs = dot(value, go_t)
            inner = jnp.sum(probs * g_probs, 0, keepdims=True)
            g_scores = low(probs * (g_probs - inner))
            g_query = low(dot(key_t, g_scores))
            g_key = g_key + dot_nt(query_t, g_scores)
            g_value = g_value + dot_nt(go_t, low(probs))
            if i == size - 1:
                dqkv[0, theirs, :] = g_query
            else:
                q_send[h, i] = g_query
                copy = to_group(q_send.at[h, i], dqkv.at[0, theirs], sems_q, (h, i), p)
                copy.start()
                sent.append(copy)
        kv_send[h, 0] = low(g_key)
        kv_send[h, 1] = low(g_value)
        for i, p in enumerate(others()):
            if i == size - 1:
                dqkv[1:, theirs, :] = kv_send[h, :, :, tokens_of(me, count)]
            else:
                copy = to_group(kv_send.at[h, :, :, tokens_of(p, count)], dqkv.at[pl.ds(1, 2), theirs], sems_kv, (h, i), p)
                copy.start()
                sent.append(copy)
    for copy in sent:
        copy.wait_recv()
    summed = jnp.zeros((model, count), jnp.float32)
    for part in range(3):
        for c in range(model // CHUNK):
            rows = slice(c * CHUNK, (c + 1) * CHUNK)
            columns = slice(part * model + c * CHUNK, part * model + (c + 1) * CHUNK)
            d_attn[:, columns] = low(dot_nt(normed_t[...], dqkv[part, rows, :]))
        summed = summed + dot(w_attn[:, part * model:(part + 1) * model], dqkv[part, :model, :])
    saves.append(pltpu.make_async_copy(d_attn, d_attn_hbm, d_sems.at[2]))
    saves[-1].start()
    back, d_gain = norm_back(x[...], gain_a[...], summed.T)
    d_gain_a[...] = d_gain
    grad_in[...] += back
    for made in go_copies:
        for copy in made[:-1]:
            copy.wait_send()
    for copy in sent:
        copy.wait_send()
    for save in saves:
        save.wait()


def layer_backward(lengths, grad, x, gain_a, gain_f, kept, w_attn, w_ffn, w_down, collective_id):
    size, each = lax.axis_size("ctx"), heads_each()
    count, model = x.shape
    wide = w_down.shape[0]
    group = count * size
    rows = each * size * HEAD_DIM
    f32, bf16 = jnp.float32, jnp.bfloat16
    made = lambda shape, dtype: jax.ShapeDtypeStruct(shape, dtype)
    return pl.pallas_call(
        layer_backward_kernel,
        out_shape=[made((count, model), f32), made((1, model), f32), made((1, model), f32),
                   made(w_attn.shape, bf16), made(w_ffn.shape, bf16), made(w_down.shape, bf16)],
        in_specs=[SMEM] + [VMEM] * 12 + [ANY] * 3,
        out_specs=[VMEM] * 3 + [ANY] * 3,
        scratch_shapes=[
            pltpu.VMEM(w_attn.shape, bf16), pltpu.VMEM(w_ffn.shape, bf16), pltpu.VMEM(w_down.shape, bf16),
            pltpu.VMEM(w_attn.shape, bf16), pltpu.VMEM(w_ffn.shape, bf16), pltpu.VMEM(w_down.shape, bf16),
            pltpu.VMEM((1, rows, count), bf16), pltpu.VMEM((1, each * HEAD_DIM, group), bf16),
            pltpu.VMEM((3, rows, count), bf16), pltpu.VMEM((each, size - 1, HEAD_DIM, count), bf16),
            pltpu.VMEM((each, 2, HEAD_DIM, group), bf16), pltpu.VMEM((group, count), jnp.int32),
            pltpu.VMEM((count, model), f32), pltpu.VMEM((count, model), bf16), pltpu.VMEM((count, model), bf16),
            pltpu.SemaphoreType.DMA((2, each, size - 1)), pltpu.SemaphoreType.DMA((2, each, size - 1)),
            pltpu.SemaphoreType.DMA((2, each, size - 1)), pltpu.SemaphoreType.DMA((each,)),
            pltpu.SemaphoreType.DMA((3,)), pltpu.SemaphoreType.DMA((3,))],
        compiler_params=pltpu.CompilerParams(collective_id=collective_id, has_side_effects=True, vmem_limit_bytes=60 << 20),
        name="layer_backward",
    )(lengths, grad, x, gain_a, gain_f, *kept, w_attn, w_ffn, w_down)


def segment_of(places, ends):
    return jnp.sum((places[:, None] >= ends[None, :]).astype(jnp.int32), 1)


def offset_in(places, segs, ends, seq_lengths):
    starts = ends - seq_lengths
    picks = segs[:, None] == jnp.arange(ends.shape[0], dtype=jnp.int32)[None, :]
    return places - jnp.sum(jnp.where(picks, starts[None, :], 0), 1)


def gbst_mix(byte_ext, valid_ext, seg_ext, rel_ext, embed_t, conv_w, conv_b, scorer_v):
    width_ext = byte_ext.shape[0]
    byte_count = width_ext - 10
    onehot = (byte_ext[:, None] == jnp.arange(embed_t.shape[0], dtype=jnp.int32)[None, :]).astype(
        jnp.float32
    )
    onehot = onehot * valid_ext[:, None]
    embedded = jnp.dot(onehot, embed_t, precision=PRECISE)
    conv_span = width_ext - 3
    conv_out = conv_b[None, :] + sum(
        (
            conv_w[tap][None, :]
            * embedded[tap : tap + conv_span]
            * (seg_ext[tap : tap + conv_span] == seg_ext[1 : 1 + conv_span]).astype(jnp.float32)[
                :, None
            ]
            for tap in range(4)
        )
    )
    conv_out = conv_out * valid_ext[1 : 1 + conv_span, None]
    own_seg = seg_ext[5 : 5 + byte_count]
    own_rel = rel_ext[5 : 5 + byte_count]
    pooled_list = []
    for block_size in (1, 2, 3, 4):
        pooled = jnp.zeros((byte_count, embed_t.shape[1]), jnp.float32)
        for shift_by in range(1 - block_size, block_size):
            same = (seg_ext[5 + shift_by : 5 + shift_by + byte_count] == own_seg) & (
                (own_rel + shift_by) // block_size == own_rel // block_size
            )
            weight = jnp.where(same, 1.0 / block_size, 0.0).astype(jnp.float32)
            pooled = pooled + weight[:, None] * conv_out[4 + shift_by : 4 + shift_by + byte_count]
        pooled_list.append(pooled)
    stacked = jnp.stack(pooled_list)
    logits = jnp.einsum("bnd,d->bn", stacked, scorer_v, precision=PRECISE)
    choose = jax.nn.softmax(logits, 0)
    chosen = jnp.sum(choose[..., None] * stacked, 0)
    return chosen.reshape(byte_count // 2, 2, -1).mean(1)


def packed_small(embed, conv_weight, conv_bias, scorer, norm_attn, norm_ffn):
    rows = jnp.concatenate([embed, conv_weight, conv_bias[None], scorer[None], norm_attn, norm_ffn], 0).T
    return jnp.pad(rows, ((0, 0), (0, -rows.shape[1] % 128)))


def split_small(rows, vocab, layers):
    at = vocab + CONV
    return (rows[:vocab], rows[vocab:at], rows[at], rows[at + 1], rows[at + 2 : at + 2 + layers],
            rows[at + 2 + layers : at + 2 + 2 * layers])


def on_device(
    byte_ids,
    lengths,
    embed,
    conv_weight,
    conv_bias,
    scorer,
    norm_attn,
    query_w,
    key_w,
    value_w,
    attn_out_w,
    norm_ffn,
    gate_w,
    up_w,
    down_w,
    out_grad,
):
    ctx_count = lax.axis_size("ctx")
    ctx_place = lax.axis_index("ctx")
    layer_count = query_w.shape[0]
    vocab = embed.shape[0]
    model = query_w.shape[2]
    byte_count = byte_ids.shape[1]
    seq_lengths = lengths[0]
    at = jnp.arange(seq_lengths.shape[0])
    ends = jnp.sum(jnp.where(at[:, None] >= at[None, :], seq_lengths[None, :], 0), 1).astype(jnp.int32)
    total_bytes = ends[-1]
    first_byte = ctx_place * byte_count
    byte_ext = padded(byte_ids[0], (("ctx", 0),), 5)
    ext_places = first_byte - 5 + jnp.arange(byte_count + 10, dtype=jnp.int32)
    valid_ext = ((ext_places >= 0) & (ext_places < total_bytes)).astype(jnp.float32)
    seg_ext = segment_of(ext_places, ends)
    rel_ext = offset_in(ext_places, seg_ext, ends, seq_lengths)
    small = packed_small(embed, conv_weight, conv_bias, scorer, norm_attn, norm_ffn)
    shards = [small]
    for layer in range(layer_count):
        shards.append(jnp.concatenate([query_w[layer], key_w[layer], value_w[layer], attn_out_w[layer]], 1))
        shards.append(jnp.concatenate([gate_w[layer], up_w[layer]], 1))
        shards.append(down_w[layer])
    small_full, *full = [a.reshape(-1, a.shape[-1]) for a in gather_all(shards, 0)]
    embed_full, conv_full, bias_full, scorer_full, norm_a, norm_f = split_small(small_full.T, vocab, layer_count)

    def gbst_local(embed_t, conv_w, conv_b, scorer_v):
        return gbst_mix(byte_ext, valid_ext, seg_ext, rel_ext, embed_t, conv_w, conv_b, scorer_v)

    stream, gbst_back = jax.vjp(
        gbst_local,
        embed_full.astype(jnp.float32),
        conv_full.astype(jnp.float32),
        bias_full.astype(jnp.float32),
        scorer_full.astype(jnp.float32),
    )
    gains_a, gains_f = norm_a.astype(jnp.float32), norm_f.astype(jnp.float32)
    kept = []
    for layer in range(layer_count):
        weights = full[3 * layer : 3 * layer + 3]
        before = stream
        stream, *saved = layer_forward(lengths, stream, gains_a[layer][None], gains_f[layer][None], *weights, 2)
        kept.append((before, saved))
    encoded = stream.astype(jnp.bfloat16)[None]
    grad_stream = out_grad[0].astype(jnp.float32)
    partial = []
    gains = []
    for layer in reversed(range(layer_count)):
        before, saved = kept[layer]
        weights = full[3 * layer : 3 * layer + 3]
        grad_stream, d_gain_attn, d_gain_ffn, *grads = layer_backward(
            lengths, grad_stream, before, gains_a[layer][None], gains_f[layer][None], saved, *weights, 3
        )
        partial = list(grads) + partial
        gains = [(d_gain_attn[0], d_gain_ffn[0])] + gains
    grads = gbst_back(grad_stream)
    small_grad = packed_small(*grads, jnp.stack([a for a, _ in gains]), jnp.stack([f for _, f in gains]))
    outs = scatter_all([p.astype(jnp.bfloat16) for p in [small_grad] + partial], 1)
    small_out, *rest = outs
    g_embed, g_conv, g_bias, g_scorer, g_norm_a, g_norm_f = split_small(small_out.T, vocab, layer_count)
    attn_out, ffn_out, down_out = rest[0::3], rest[1::3], rest[2::3]
    columns = [jnp.stack([a[:, i * model : (i + 1) * model] for a in attn_out]) for i in range(4)]
    wide = ffn_out[0].shape[1] // 2
    return (
        encoded,
        g_embed,
        g_conv,
        g_bias,
        g_scorer,
        g_norm_a,
        columns[0],
        columns[1],
        columns[2],
        columns[3],
        g_norm_f,
        jnp.stack([a[:, :wide] for a in ffn_out]),
        jnp.stack([a[:, wide:] for a in ffn_out]),
        jnp.stack(down_out),
    )


def solution(mesh):
    placed = (
        P("dp", "ctx"),
        P("dp", None),
        P(None, ("dp", "ctx")),
        P(None, ("dp", "ctx")),
        P(("dp", "ctx")),
        P(("dp", "ctx")),
        P(None, ("dp", "ctx")),
        P(None, ("dp", "ctx"), None),
        P(None, ("dp", "ctx"), None),
        P(None, ("dp", "ctx"), None),
        P(None, ("dp", "ctx"), None),
        P(None, ("dp", "ctx")),
        P(None, ("dp", "ctx"), None),
        P(None, ("dp", "ctx"), None),
        P(None, ("dp", "ctx"), None),
        P("dp", "ctx", None),
    )
    return jax.shard_map(
        on_device,
        mesh=mesh,
        in_specs=placed,
        out_specs=(
            P("dp", "ctx", None),
            P(None, ("dp", "ctx")),
            P(None, ("dp", "ctx")),
            P(("dp", "ctx")),
            P(("dp", "ctx")),
            P(None, ("dp", "ctx")),
            P(None, ("dp", "ctx"), None),
            P(None, ("dp", "ctx"), None),
            P(None, ("dp", "ctx"), None),
            P(None, ("dp", "ctx"), None),
            P(None, ("dp", "ctx")),
            P(None, ("dp", "ctx"), None),
            P(None, ("dp", "ctx"), None),
            P(None, ("dp", "ctx"), None),
        ),
        check_vma=False,
    )
```

```python
import functools
import math
import jax
import jax.numpy as jnp
from jax import lax
from jax.experimental import pallas as pl
from jax.experimental.pallas import tpu as pltpu
from jax.sharding import PartitionSpec as P


MESH = pl.DeviceIdType.MESH
CORES = 2
LANES = 128
THIRD = 0.18


def grid_of():
    dp, ctx = lax.axis_size("dp"), lax.axis_size("ctx")
    rows = 2 if ctx % 2 == 0 else 1
    return dp // CORES, rows, ctx // rows


def place_of():
    _, _, nx = grid_of()
    d, c = lax.axis_index("dp"), lax.axis_index("ctx")
    return d // CORES, d % CORES, c // nx, c % nx


def device(z, core, y, x):
    _, _, nx = grid_of()
    return (z * CORES + core, y * nx + x)


def along(axis):
    place = list(place_of())
    nz, ny, nx = grid_of()
    size = (nz, CORES, ny, nx)[axis]
    found = []
    for i in range(1, size):
        there = list(place)
        there[axis] = lax.rem(place[axis] + i, size)
        found.append((there[axis], device(*there)))
    return found


def sibling():
    z, core, y, x = place_of()
    return device(z, 1 - core, y, x)


def greet_all():
    barrier = pltpu.get_barrier_semaphore()
    targets = [target for axis in (0, 2, 3) for _, target in along(axis)] + [sibling()]
    _, ny, nx = grid_of()
    z, core, y, x = place_of()
    for i in range(1, ny):
        for j in range(1, nx):
            targets.append(device(z, core, lax.rem(y + i, ny), lax.rem(x + j, nx)))
    for target in targets:
        pl.semaphore_signal(barrier, inc=1, device_id=target, device_id_type=MESH)
    pl.semaphore_wait(barrier, len(targets))
    return targets


ORDERS = ((0, 3, 2), (0, 2, 3), (3, 2, 0))


def pieces_of(width, third):
    units = width // LANES
    last = int(units * third)
    left = (units - last + 1) // 2
    found, at = [], 0
    for order, size in zip(ORDERS, (left, units - last - left, last)):
        if size:
            found.append((pl.ds(at * LANES, size * LANES), order))
        at += size
    return found


def hops(width, third):
    nz, ny, nx = grid_of()
    return len(pieces_of(width, third)) * (nz - 1 + ny - 1 + nx - 1) + 1


class Sender:
    def __init__(self, sems):
        self.sems, self.count, self.flying = sems, 0, []

    def send(self, src, dst, target):
        copy = pltpu.make_async_remote_copy(
            src_ref=src, dst_ref=dst, send_sem=self.sems.at[0, self.count], recv_sem=self.sems.at[1, self.count],
            device_id=target, device_id_type=MESH)
        copy.start()
        self.count += 1
        self.flying.append(copy)
        return copy

    def finish(self):
        for copy in self.flying:
            copy.wait_send()


class GatherChunk(Sender):
    phases = 4

    def __init__(self, shard, out, sems, local_sem, third):
        super().__init__(sems)
        self.shard, self.out, self.local_sem = shard, out, local_sem
        self.pieces = pieces_of(shard.shape[-1], third)
        self.waiting = []

    def stage(self, number):
        place = place_of()
        for copy in self.waiting:
            copy.wait_recv()
        self.waiting = []
        if number == 0:
            self.own = pltpu.make_async_copy(self.shard, self.out.at[place], self.local_sem)
            self.own.start()
        if number == 1:
            self.own.wait()
        if number < 3:
            for columns, order in self.pieces:
                have = order[:number]
                where = tuple(slice(None) if axis in have else place[axis] for axis in range(4)) + (slice(None), columns)
                src = self.out.at[where] if number else self.shard.at[:, columns]
                for _, target in along(order[number]):
                    self.waiting.append(self.send(src, self.out.at[where], target))
        else:
            where = (slice(None), place[1])
            self.waiting.append(self.send(self.out.at[where], self.out.at[where], sibling()))

    def arrive(self):
        for copy in self.waiting:
            copy.wait_recv()
        self.waiting = []


class Ticker:
    def __init__(self, chunks):
        self.chunks, self.steps, self.done = chunks, [], [0] * len(chunks)
        phases = chunks[0].phases
        for t in range(len(chunks) + phases):
            for number in [0] + list(range(phases - 1, 0, -1)):
                if 0 <= t - number < len(chunks):
                    self.steps.append((t - number, number))

    def tick(self, count=1):
        for _ in range(count):
            if self.steps:
                i, number = self.steps.pop(0)
                self.chunks[i].stage(number)
                self.done[i] = number + 1

    def until(self, i):
        while self.done[i] < self.chunks[i].phases:
            self.tick()

    def need(self, i):
        self.until(i)
        self.chunks[i].arrive()


def gather_kernel(n, third, *refs):
    shards, outs, sems, local_sems = refs[:n], refs[n:2 * n], refs[2 * n:3 * n], refs[3 * n]
    greet_all()
    chunks = [GatherChunk(shards[i], outs[i], sems[i], local_sems.at[i], third) for i in range(n)]
    ticker = Ticker(chunks)
    for i in range(n):
        ticker.need(i)
    for chunk in chunks:
        chunk.finish()


def gather_all(shards, collective_id, third=THIRD):
    nz, ny, nx = grid_of()
    n = len(shards)
    outs = pl.pallas_call(
        functools.partial(gather_kernel, n, third),
        out_shape=[jax.ShapeDtypeStruct((nz, CORES, ny, nx) + s.shape, s.dtype) for s in shards],
        in_specs=[pl.BlockSpec(memory_space=pl.ANY)] * n,
        out_specs=[pl.BlockSpec(memory_space=pl.ANY)] * n,
        scratch_shapes=[pltpu.SemaphoreType.DMA((2, hops(s.shape[-1], third))) for s in shards] + [pltpu.SemaphoreType.DMA((n,))],
        compiler_params=pltpu.CompilerParams(collective_id=collective_id, has_side_effects=True),
        name="gather_weights",
    )(*shards)
    return [o.reshape((-1,) + o.shape[5:]) for o in outs]


def add_into(dst, src, lead):
    if not lead:
        dst[...] = (dst[...].astype(jnp.float32) + src[...].astype(jnp.float32)).astype(dst.dtype)
        return

    def body(i, carry):
        add_into(dst.at[i], src.at[i], lead[1:])
        return carry
    lax.fori_loop(0, lead[0], body, 0)


class ScatterChunk(Sender):
    phases = 5

    def __init__(self, parts, out, scratch, sems, local_sem, third):
        super().__init__(sems)
        self.parts, self.out, self.local_sem = parts, out, local_sem
        self.held, self.across, *landing = scratch
        self.pieces = [(columns, order[::-1], landing[3 * i:3 * i + 3])
                       for i, (columns, order) in enumerate(pieces_of(parts.shape[-1], third))]
        self.waiting = []

    @staticmethod
    def scratch(shape, dtype, third):
        sizes = dict(zip((0, 2, 3), grid_of()))
        whole = (*sizes.values(), *shape)
        found = [whole, whole]
        for columns, order in pieces_of(shape[-1], third):
            order = order[::-1]
            for number in range(3):
                rest = [sizes[a] for a in sizes if a in order[number + 1:]]
                found.append((sizes[order[number]] - 1, *rest, shape[0], columns.size))
        return [pltpu.VMEM(s, dtype) for s in found]

    def stage(self, number):
        place = place_of()
        sizes = dict(zip((0, 2, 3), grid_of()))
        for copy in self.waiting:
            copy.wait_recv()
        self.waiting = []
        if number == 0:
            self.own = pltpu.make_async_copy(self.parts.at[:, place[1]], self.held, self.local_sem)
            self.own.start()
            self.waiting.append(self.send(self.parts.at[:, 1 - place[1]], self.across, sibling()))
            return
        if number == 1:
            self.own.wait()
            add_into(self.held, self.across, list(sizes.values()))
        for columns, order, landing in self.pieces:
            if number > 1:
                mine = order[:number - 1]
                where = tuple(place[a] if a in mine else slice(None) for a in sizes) + (slice(None), columns)
                lead = [sizes[a] for a in sizes if a not in mine]
                landed = landing[number - 2]
                if number < 4:
                    for i in range(landed.shape[0]):
                        add_into(self.held.at[where], landed.at[i], lead)
                else:
                    total = self.held[where].astype(jnp.float32)
                    for i in range(landed.shape[0]):
                        total = total + landed[i].astype(jnp.float32)
                    self.out[:, columns] = total
            if number < 4:
                axis, mine = order[number - 1], order[:number - 1]
                for i, (there, target) in enumerate(along(axis)):
                    where = tuple(there if a == axis else place[a] if a in mine else slice(None) for a in sizes)
                    src = self.held.at[where + (slice(None), columns)]
                    self.waiting.append(self.send(src, landing[number - 1].at[i], target))


def scatter_kernel(n, third, counts, *refs):
    parts, outs, rest = refs[:n], refs[n:2 * n], list(refs[2 * n:])
    greet_all()
    chunks = []
    for i in range(n):
        scratch = [rest.pop(0) for _ in range(counts[i])]
        chunks.append(ScatterChunk(parts[i], outs[i], scratch, rest.pop(0), rest.pop(0), third))
    ticker = Ticker(chunks)
    for i in range(n):
        ticker.until(i)
    for chunk in chunks:
        chunk.finish()


def scatter_scratch(shape, dtype, third):
    scratch = ScatterChunk.scratch(shape, dtype, third)
    return scratch + [pltpu.SemaphoreType.DMA((2, hops(shape[-1], third))), pltpu.SemaphoreType.DMA]


def scatter_all(parts, collective_id, third=THIRD):
    nz, ny, nx = grid_of()
    n = len(parts)
    devices = nz * CORES * ny * nx
    parts = [p.reshape((nz, CORES, ny, nx, p.shape[0] // devices) + p.shape[1:]) for p in parts]
    scratch, counts = [], []
    for p in parts:
        made = scatter_scratch(p.shape[4:], p.dtype, third)
        counts.append(len(made) - 2)
        scratch += made
    return pl.pallas_call(
        functools.partial(scatter_kernel, n, third, counts),
        out_shape=[jax.ShapeDtypeStruct(p.shape[4:], jnp.float32) for p in parts],
        in_specs=[pl.BlockSpec(memory_space=pl.ANY)] * n,
        out_specs=[pl.BlockSpec(memory_space=pltpu.VMEM)] * n,
        scratch_shapes=scratch,
        compiler_params=pltpu.CompilerParams(collective_id=collective_id, has_side_effects=True, vmem_limit_bytes=60 << 20),
        name="scatter_grads",
    )(*parts)


HEADS = 12
HEAD_DIM = 64
CHUNK = 256
NORM_EPS = 1e-06
NEG_FILL = -1000000000.0
GELU_A = 0.7978845608028654
GELU_B = 0.044715


def dot(a, b):
    return jnp.dot(a, b, preferred_element_type=jnp.float32)


def dot_nt(a, b):
    return lax.dot_general(a, b, (((1,), (1,)), ((), ())), preferred_element_type=jnp.float32)


def low(v):
    return v.astype(jnp.bfloat16)


def flip(v):
    return low(v.astype(jnp.float32).T)


def inverse_rms(v):
    return lax.rsqrt(jnp.mean(v * v, -1, keepdims=True) + NORM_EPS)


def ends_of(lengths_ref):
    ends, total = [], 0
    for i in range(lengths_ref.shape[-1]):
        total = total + lengths_ref[0, i]
        ends.append(total)
    return ends


def segments(places, ends):
    seg = jnp.zeros(places.shape, jnp.int32)
    for end in ends:
        seg = seg + jnp.where(places >= end, 1, 0)
    return seg


def heads_each():
    return -(-HEADS // lax.axis_size("ctx"))


def others():
    size, me = lax.axis_size("ctx"), lax.axis_index("ctx")
    return [lax.rem(me + 1 + i, size) for i in range(size)]


def greet_group():
    barrier = pltpu.get_barrier_semaphore()
    peers_ = others()[:-1]
    for p in peers_:
        pl.semaphore_signal(barrier, inc=1, device_id=(lax.axis_index("dp"), p), device_id_type=MESH)
    pl.semaphore_wait(barrier, len(peers_))


def to_group(src, dst, sems, index, p):
    return pltpu.make_async_remote_copy(
        src_ref=src, dst_ref=dst, send_sem=sems.at[(0,) + index], recv_sem=sems.at[(1,) + index],
        device_id=(lax.axis_index("dp"), p), device_id_type=MESH)


def tokens_of(p, count):
    return pl.ds(pl.multiple_of(p * count, count), count)


def spread_heads(src, dst, sems, local_sem, each):
    me = lax.axis_index("ctx")
    count = src.shape[2]
    copies = []
    for h in range(each):
        rows = pl.ds(h * HEAD_DIM, HEAD_DIM)
        made = []
        for i, p in enumerate(others()):
            theirs = pl.ds(pl.multiple_of((p * each + h) * HEAD_DIM, HEAD_DIM), HEAD_DIM)
            a, b = src.at[:, theirs], dst.at[:, rows, tokens_of(me, count)]
            if i == lax.axis_size("ctx") - 1:
                copy = pltpu.make_async_copy(a, b, local_sem.at[h])
            else:
                copy = to_group(a, b, sems, (h, i), p)
            copy.start()
            made.append(copy)
        copies.append(made)
    return copies


def arrive(made):
    for copy in made[:-1]:
        copy.wait_recv()
    made[-1].wait()


def attention_forward(each, seg_all, ends, qkv, lse, out_send, att, qkv_copies, sems, tick=lambda: None):
    size, me = lax.axis_size("ctx"), lax.axis_index("ctx")
    count = att.shape[1]
    copies = []
    for h in range(each):
        arrive(qkv_copies[h])
        rows = pl.ds(h * HEAD_DIM, HEAD_DIM)
        key = flip(qkv[1, rows, :])
        value_t = qkv[2, rows, :]
        theirs = pl.ds(pl.multiple_of((me * each + h) * HEAD_DIM, HEAD_DIM), HEAD_DIM)
        for i, p in enumerate(others()):
            tokens = tokens_of(p, count)
            seg_q = segments(2 * (p * count + lax.broadcasted_iota(jnp.int32, (1, count), 1)), ends)
            scores = dot(key, qkv[0, rows, tokens])
            scores = jnp.where(seg_all[...] == seg_q, scores, NEG_FILL)
            top = jnp.max(scores, 0, keepdims=True)
            probs = jnp.exp(scores - top)
            total = jnp.sum(probs, 0, keepdims=True)
            lse[h, :, tokens] = top + jnp.log(total)
            result = low(dot(value_t, low(probs)) / total)
            if i == size - 1:
                att[theirs, :] = result
            else:
                out_send[h, i] = result
                copy = to_group(out_send.at[h, i], att.at[theirs], sems, (h, i), p)
                copy.start()
                copies.append(copy)
            tick()
    return copies


def gelu_parts(gate):
    inner = jnp.tanh(GELU_A * (gate + GELU_B * gate * gate * gate))
    half = 0.5 * (1.0 + inner)
    slope = half + 0.5 * gate * (1.0 - inner * inner) * GELU_A * (1.0 + 3.0 * GELU_B * gate * gate)
    return gate * half, slope


def layer_forward_kernel(lengths, x, gain_a, gain_f, w_attn_hbm, w_ffn_hbm, w_down_hbm,
                         out, middle, normed_t, qkv, lse, att, gate_out, up_out, nffn_t,
                         w_attn, w_ffn, w_down, qkv_all, out_send, seg_all, nffn,
                         sems_in, sems_out, local_sems, w_sems):
    each = heads_each()
    model = x.shape[1]
    loads = [pltpu.make_async_copy(a, b, w_sems.at[i]) for i, (a, b) in enumerate(
        ((w_attn_hbm, w_attn), (w_ffn_hbm, w_ffn), (w_down_hbm, w_down)))]
    for load in loads:
        load.start()
    greet_group()
    ends = ends_of(lengths)
    seg_all[...] = segments(2 * lax.broadcasted_iota(jnp.int32, seg_all.shape, 0), ends)
    stream = x[...]
    normed = low(stream * inverse_rms(stream) * gain_a[...])
    normed_t[...] = flip(normed)
    if qkv_all.shape[1] > model:
        qkv_all[:, model:, :] = jnp.zeros((3, qkv_all.shape[1] - model, qkv_all.shape[2]), jnp.bfloat16)
    loads[0].wait()
    for part in range(3):
        for c in range(model // CHUNK):
            columns = pl.ds(part * model + c * CHUNK, CHUNK)
            qkv_all[part, c * CHUNK:(c + 1) * CHUNK, :] = low(dot(normed, w_attn[:, columns]).T)
    qkv_copies = spread_heads(qkv_all, qkv, sems_in, local_sems, each)
    out_copies = attention_forward(each, seg_all, ends, qkv, lse, out_send, att, qkv_copies, sems_out)
    for copy in out_copies:
        copy.wait_recv()
    attended = flip(att[:model, :])
    mid = stream + dot(attended, w_attn[:, 3 * model:])
    middle[...] = mid
    after = low(mid * inverse_rms(mid) * gain_f[...])
    nffn[...] = after
    nffn_t[...] = flip(after)
    out[...] = mid
    loads[1].wait()
    loads[2].wait()
    hidden_count = w_down.shape[0]

    def step(c, carry):
        columns = pl.ds(pl.multiple_of(c * CHUNK, CHUNK), CHUNK)
        gate = dot(nffn[...], w_ffn[:, columns])
        up = dot(nffn[...], w_ffn[:, pl.ds(pl.multiple_of(hidden_count + c * CHUNK, CHUNK), CHUNK)])
        gate_out[:, columns] = gate
        up_out[:, columns] = up
        hidden = low(gelu_parts(gate)[0] * up)
        out[...] += dot(hidden, w_down[columns, :])
        return carry
    lax.fori_loop(0, hidden_count // CHUNK, step, 0)
    for made in qkv_copies:
        for copy in made[:-1]:
            copy.wait_send()
    for copy in out_copies:
        copy.wait_send()


VMEM = pl.BlockSpec(memory_space=pltpu.VMEM)
ANY = pl.BlockSpec(memory_space=pl.ANY)
SMEM = pl.BlockSpec(memory_space=pltpu.SMEM)


def layer_forward(lengths, x, gain_a, gain_f, w_attn, w_ffn, w_down, collective_id):
    size, each = lax.axis_size("ctx"), heads_each()
    count, model = x.shape
    wide = w_down.shape[0]
    group = count * size
    rows = each * size * HEAD_DIM
    f32, bf16 = jnp.float32, jnp.bfloat16
    made = lambda shape, dtype: jax.ShapeDtypeStruct(shape, dtype)
    return pl.pallas_call(
        layer_forward_kernel,
        out_shape=[made((count, model), f32), made((count, model), f32), made((model, count), bf16),
                   made((3, each * HEAD_DIM, group), bf16), made((each, 1, group), f32), made((rows, count), bf16),
                   made((count, wide), f32), made((count, wide), f32), made((model, count), bf16)],
        in_specs=[SMEM, VMEM, VMEM, VMEM, ANY, ANY, ANY],
        out_specs=[VMEM] * 9,
        scratch_shapes=[
            pltpu.VMEM(w_attn.shape, bf16), pltpu.VMEM(w_ffn.shape, bf16), pltpu.VMEM(w_down.shape, bf16),
            pltpu.VMEM((3, rows, count), bf16), pltpu.VMEM((each, size - 1, HEAD_DIM, count), bf16),
            pltpu.VMEM((group, count), jnp.int32), pltpu.VMEM((count, model), bf16),
            pltpu.SemaphoreType.DMA((2, each, size - 1)), pltpu.SemaphoreType.DMA((2, each, size - 1)),
            pltpu.SemaphoreType.DMA((each,)), pltpu.SemaphoreType.DMA((3,))],
        compiler_params=pltpu.CompilerParams(collective_id=collective_id, has_side_effects=True, vmem_limit_bytes=56 << 20),
        name="layer_forward",
    )(lengths, x, gain_a, gain_f, w_attn, w_ffn, w_down)


def layer_backward_kernel(lengths, grad, x, gain_a, gain_f, middle, normed_t, qkv, lse, att, gate_in, up_in, nffn_t,
                          w_attn_hbm, w_ffn_hbm, w_down_hbm,
                          grad_in, d_gain_a, d_gain_f, d_attn_hbm, d_ffn_hbm, d_down_hbm,
                          w_attn, w_ffn, w_down, d_attn, d_ffn, d_down, go_all, go, dqkv, q_send, kv_send, seg_all, total,
                          grad_low, mid_low, sems_in, sems_q, sems_kv, local_sems, w_sems, d_sems):
    each = heads_each()
    size, me = lax.axis_size("ctx"), lax.axis_index("ctx")
    count, model = x.shape
    wide = w_down.shape[0]
    loads = [pltpu.make_async_copy(a, b, w_sems.at[i]) for i, (a, b) in enumerate(
        ((w_down_hbm, w_down), (w_ffn_hbm, w_ffn), (w_attn_hbm, w_attn)))]
    for load in loads:
        load.start()
    greet_group()
    ends = ends_of(lengths)
    seg_all[...] = segments(2 * lax.broadcasted_iota(jnp.int32, seg_all.shape, 0), ends)
    grad_low[...] = low(grad[...])
    total[...] = jnp.zeros(total.shape, jnp.float32)
    loads[0].wait()
    loads[1].wait()

    def step(c, carry):
        columns = pl.ds(pl.multiple_of(c * CHUNK, CHUNK), CHUNK)
        later = pl.ds(pl.multiple_of(wide + c * CHUNK, CHUNK), CHUNK)
        g_hidden = dot_nt(grad_low[...], w_down[columns, :])
        up = up_in[:, columns]
        act, slope = gelu_parts(gate_in[:, columns])
        g_gate = low(g_hidden * up * slope)
        g_up = low(g_hidden * act)
        d_down[columns, :] = low(dot(low((act * up).T), grad_low[...]))
        d_ffn[:, columns] = low(dot(nffn_t[...], g_gate))
        d_ffn[:, later] = low(dot(nffn_t[...], g_up))
        total[...] += dot_nt(g_gate, w_ffn[:, columns]) + dot_nt(g_up, w_ffn[:, later])
        return carry
    lax.fori_loop(0, wide // CHUNK, step, 0)
    saves = [pltpu.make_async_copy(d_ffn, d_ffn_hbm, d_sems.at[0]), pltpu.make_async_copy(d_down, d_down_hbm, d_sems.at[1])]
    for save in saves:
        save.start()

    def norm_back(values, gain, upstream):
        scale = inverse_rms(values)
        scaled = upstream * gain
        along = jnp.mean(values * scaled, -1, keepdims=True)
        return scale * scaled - values * (scale * scale * scale * along), jnp.sum(upstream * values * scale, 0, keepdims=True)

    back, d_gain = norm_back(middle[...], gain_f[...], total[...])
    d_gain_f[...] = d_gain
    grad_in[...] = grad[...] + back
    mid_low[...] = low(grad_in[...])
    if go_all.shape[1] > model:
        go_all[:, model:, :] = jnp.zeros((1, go_all.shape[1] - model, count), jnp.bfloat16)
    loads[2].wait()
    for c in range(model // CHUNK):
        rows = slice(c * CHUNK, (c + 1) * CHUNK)
        go_all[0, rows, :] = low(dot_nt(mid_low[...], w_attn[rows, 3 * model:]).T)
    go_copies = spread_heads(go_all, go, sems_in, local_sems, each)
    for c in range(model // CHUNK):
        rows = slice(c * CHUNK, (c + 1) * CHUNK)
        d_attn[rows, 3 * model:] = low(dot(att[rows, :], mid_low[...]))
    sent = []
    for h in range(each):
        arrive(go_copies[h])
        rows = pl.ds(h * HEAD_DIM, HEAD_DIM)
        theirs = pl.ds(pl.multiple_of((me * each + h) * HEAD_DIM, HEAD_DIM), HEAD_DIM)
        key_t = qkv[1, rows, :]
        key, value = flip(key_t), flip(qkv[2, rows, :])
        g_key = jnp.zeros((HEAD_DIM, count * size), jnp.float32)
        g_value = jnp.zeros((HEAD_DIM, count * size), jnp.float32)
        for i, p in enumerate(others()):
            tokens = tokens_of(p, count)
            seg_q = segments(2 * (p * count + lax.broadcasted_iota(jnp.int32, (1, count), 1)), ends)
            query_t, go_t = qkv[0, rows, tokens], go[0, rows, tokens]
            scores = jnp.where(seg_all[...] == seg_q, dot(key, query_t), NEG_FILL)
            probs = jnp.exp(scores - lse[h, :, tokens])
            g_probs = dot(value, go_t)
            inner = jnp.sum(probs * g_probs, 0, keepdims=True)
            g_scores = low(probs * (g_probs - inner))
            g_query = low(dot(key_t, g_scores))
            g_key = g_key + dot_nt(query_t, g_scores)
            g_value = g_value + dot_nt(go_t, low(probs))
            if i == size - 1:
                dqkv[0, theirs, :] = g_query
            else:
                q_send[h, i] = g_query
                copy = to_group(q_send.at[h, i], dqkv.at[0, theirs], sems_q, (h, i), p)
                copy.start()
                sent.append(copy)
        kv_send[h, 0] = low(g_key)
        kv_send[h, 1] = low(g_value)
        for i, p in enumerate(others()):
            if i == size - 1:
                dqkv[1:, theirs, :] = kv_send[h, :, :, tokens_of(me, count)]
            else:
                copy = to_group(kv_send.at[h, :, :, tokens_of(p, count)], dqkv.at[pl.ds(1, 2), theirs], sems_kv, (h, i), p)
                copy.start()
                sent.append(copy)
    for copy in sent:
        copy.wait_recv()
    summed = jnp.zeros((model, count), jnp.float32)
    for part in range(3):
        for c in range(model // CHUNK):
            rows = slice(c * CHUNK, (c + 1) * CHUNK)
            columns = slice(part * model + c * CHUNK, part * model + (c + 1) * CHUNK)
            d_attn[:, columns] = low(dot_nt(normed_t[...], dqkv[part, rows, :]))
        summed = summed + dot(w_attn[:, part * model:(part + 1) * model], dqkv[part, :model, :])
    saves.append(pltpu.make_async_copy(d_attn, d_attn_hbm, d_sems.at[2]))
    saves[-1].start()
    back, d_gain = norm_back(x[...], gain_a[...], summed.T)
    d_gain_a[...] = d_gain
    grad_in[...] += back
    for made in go_copies:
        for copy in made[:-1]:
            copy.wait_send()
    for copy in sent:
        copy.wait_send()
    for save in saves:
        save.wait()


def layer_backward(lengths, grad, x, gain_a, gain_f, kept, w_attn, w_ffn, w_down, collective_id):
    size, each = lax.axis_size("ctx"), heads_each()
    count, model = x.shape
    wide = w_down.shape[0]
    group = count * size
    rows = each * size * HEAD_DIM
    f32, bf16 = jnp.float32, jnp.bfloat16
    made = lambda shape, dtype: jax.ShapeDtypeStruct(shape, dtype)
    return pl.pallas_call(
        layer_backward_kernel,
        out_shape=[made((count, model), f32), made((1, model), f32), made((1, model), f32),
                   made(w_attn.shape, bf16), made(w_ffn.shape, bf16), made(w_down.shape, bf16)],
        in_specs=[SMEM] + [VMEM] * 12 + [ANY] * 3,
        out_specs=[VMEM] * 3 + [ANY] * 3,
        scratch_shapes=[
            pltpu.VMEM(w_attn.shape, bf16), pltpu.VMEM(w_ffn.shape, bf16), pltpu.VMEM(w_down.shape, bf16),
            pltpu.VMEM(w_attn.shape, bf16), pltpu.VMEM(w_ffn.shape, bf16), pltpu.VMEM(w_down.shape, bf16),
            pltpu.VMEM((1, rows, count), bf16), pltpu.VMEM((1, each * HEAD_DIM, group), bf16),
            pltpu.VMEM((3, rows, count), bf16), pltpu.VMEM((each, size - 1, HEAD_DIM, count), bf16),
            pltpu.VMEM((each, 2, HEAD_DIM, group), bf16), pltpu.VMEM((group, count), jnp.int32),
            pltpu.VMEM((count, model), f32), pltpu.VMEM((count, model), bf16), pltpu.VMEM((count, model), bf16),
            pltpu.SemaphoreType.DMA((2, each, size - 1)), pltpu.SemaphoreType.DMA((2, each, size - 1)),
            pltpu.SemaphoreType.DMA((2, each, size - 1)), pltpu.SemaphoreType.DMA((each,)),
            pltpu.SemaphoreType.DMA((3,)), pltpu.SemaphoreType.DMA((3,))],
        compiler_params=pltpu.CompilerParams(collective_id=collective_id, has_side_effects=True, vmem_limit_bytes=60 << 20),
        name="layer_backward",
    )(lengths, grad, x, gain_a, gain_f, *kept, w_attn, w_ffn, w_down)


CONV = 4
BLOCKS = (1, 2, 3, 4)
HALO = 64


def halves_of(v):
    high = low(v)
    return high, low(v - high.astype(jnp.float32))


def dot_split(a, b):
    high, rest = halves_of(a)
    return dot(high, b) + dot(rest, b)


def dot_wide(a, b):
    (ah, al), (bh, bl) = halves_of(a), halves_of(b)
    return dot(ah, bh) + dot(ah, bl) + dot(al, bh)


def block_starts(places, ends):
    start = jnp.zeros(places.shape, jnp.int32)
    for end in ends:
        start = jnp.where(places >= end, end, start)
    rel = places - start
    found = []
    for size in BLOCKS:
        if size & (size - 1) == 0:
            found.append(places - (rel & (size - 1)))
        else:
            count = jnp.floor((rel.astype(jnp.float32) + 0.5) * (1.0 / size)).astype(jnp.int32)
            found.append(start + count * size)
    return found


def valid_of(places, ends):
    return (places >= 0) & (places < ends[-1])


def tap_ids(ids, first, span, ends):
    places = first - HALO + lax.broadcasted_iota(jnp.int32, (1, span), 1)
    own = segments(places, ends)
    count = ids.shape[1] // 3
    rows = []
    for tap in range(CONV):
        theirs = places + (tap - 1)
        at = count - HALO + tap - 1
        near = ids[:, at - at % 128:at - at % 128 + span + 128]
        near = lax.slice_in_dim(near, at % 128, at % 128 + span, axis=1)
        use = valid_of(places, ends) & valid_of(theirs, ends) & (segments(theirs, ends) == own)
        rows.append(jnp.where(use, near, -1))
    return rows, valid_of(places, ends)


def one_hot(row, vocab):
    return low(jnp.where(lax.broadcasted_iota(jnp.int32, (vocab, row.shape[1]), 0) == row, 1.0, 0.0))


def mix_blocks(first, span, tokens, ends):
    keys = block_starts(first - HALO + lax.broadcasted_iota(jnp.int32, (span, tokens), 0), ends)
    found = []
    for parity in range(2):
        own = block_starts(first + 2 * lax.broadcasted_iota(jnp.int32, (1, tokens), 1) + parity, ends)
        found.append([key == mine for key, mine in zip(keys, own)])
    return found


def gbst_forward(ends, ids, first, small, conv, choice, vocab, tokens, tick=lambda: None):
    span = conv.shape[1]
    taps, valid = tap_ids(ids, first, span, ends)
    table = small[:, :vocab]
    at = vocab + CONV
    total = small[:, at:at + 1] * jnp.where(valid, 1.0, 0.0)
    for tap in range(CONV):
        total = total + dot_split(table * small[:, vocab + tap:vocab + tap + 1], one_hot(taps[tap], vocab))
        tick()
    conv[...] = total
    scored = jnp.sum(total * small[:, at + 1:at + 2], 0, keepdims=True)
    scored = jnp.broadcast_to(scored, (8, span))
    parts = []
    for _ in range(3):
        parts.append(low(scored))
        scored = scored - parts[-1].astype(jnp.float32)
    mix = jnp.zeros((span, tokens), jnp.float32)
    for parity, blocks in enumerate(mix_blocks(first, span, tokens, ends)):
        logits = []
        for size, block in zip(BLOCKS, blocks):
            ones = low(jnp.where(block, 1.0, 0.0))
            logits.append((dot(parts[0], ones) + dot(parts[1], ones) + dot(parts[2], ones))[:1] * (1.0 / size))
        top = functools.reduce(jnp.maximum, logits)
        raised = [jnp.exp(v - top) for v in logits]
        whole = functools.reduce(jnp.add, raised)
        for i, (size, block) in enumerate(zip(BLOCKS, blocks)):
            chosen = raised[i] / whole
            choice[len(BLOCKS) * parity + i:len(BLOCKS) * parity + i + 1, :] = chosen
            mix = mix + jnp.where(block, chosen * (0.5 / size), 0.0)
        tick()
    return dot_wide(total, mix)


def gbst_backward(ends, ids, first, small, conv, choice, grad_t, vocab, out):
    span, tokens = conv.shape[1], grad_t.shape[1]
    taps, valid = tap_ids(ids, first, span, ends)
    at = vocab + CONV
    total = conv[...]
    along = dot_wide(total.T, grad_t)
    mix = jnp.zeros((span, tokens), jnp.float32)
    scored = jnp.zeros((span, tokens), jnp.float32)
    for parity, blocks in enumerate(mix_blocks(first, span, tokens, ends)):
        chosen = [choice[len(BLOCKS) * parity + i:len(BLOCKS) * parity + i + 1, :] for i in range(len(BLOCKS))]
        grads = [jnp.sum(jnp.where(block, along, 0.0), 0, keepdims=True) * (0.5 / size) for size, block in zip(BLOCKS, blocks)]
        inner = functools.reduce(jnp.add, [c * g for c, g in zip(chosen, grads)])
        for i, (size, block) in enumerate(zip(BLOCKS, blocks)):
            mix = mix + jnp.where(block, chosen[i] * (0.5 / size), 0.0)
            scored = scored + jnp.where(block, chosen[i] * (grads[i] - inner) * (1.0 / size), 0.0)
    g_scored = jnp.sum(scored.T, 0, keepdims=True)
    g_conv = dot_wide(grad_t, mix.T) + small[:, at + 1:at + 2] * g_scored
    out[:, at + 1:at + 2] = jnp.sum(total * g_scored, 1, keepdims=True)
    g_conv = g_conv * jnp.where(valid, 1.0, 0.0)
    out[:, at:at + 1] = jnp.sum(g_conv, 1, keepdims=True)
    high, rest = halves_of(g_conv)
    table = small[:, :vocab]
    g_table = jnp.zeros(table.shape, jnp.float32)
    for tap in range(CONV):
        hot = one_hot(taps[tap], vocab)
        g_tap = dot_nt(high, hot) + dot_nt(rest, hot)
        g_table = g_table + g_tap * small[:, vocab + tap:vocab + tap + 1]
        out[:, vocab + tap:vocab + tap + 1] = jnp.sum(g_tap * table, 1, keepdims=True)
    out[:, :vocab] = g_table


def gbst_forward_kernel(vocab, tokens, lengths, ids, small, out, conv, choice):
    ends = ends_of(lengths)
    first = lax.axis_index("ctx") * 2 * tokens
    out[...] = gbst_forward(ends, ids, first, small, conv, choice, vocab, tokens).T


def gbst_backward_kernel(vocab, lengths, ids, small, conv, choice, grad, out):
    ends = ends_of(lengths)
    first = lax.axis_index("ctx") * 2 * grad.shape[0]
    out[...] = jnp.zeros(out.shape, jnp.float32)
    gbst_backward(ends, ids, first, small, conv, choice, grad[...].T, vocab, out)


class Keep:
    def __init__(self, sems):
        self.sems, self.count, self.flying = sems, 0, []

    def __call__(self, src, dst):
        copy = pltpu.make_async_copy(src, dst, self.sems.at[self.count])
        copy.start()
        self.count += 1
        self.flying.append(copy)

    def finish(self):
        for copy in self.flying:
            copy.wait()


def unpack(blocks, dst):
    nz, cores, ny, nx, rows, width = blocks.shape
    each = ny * nx * rows
    part = min(width, 512)

    def body(i, carry):
        for c in range(width // part):
            columns = slice(c * part, (c + 1) * part)
            found = [blocks[i // cores, i % cores, y, x, :, columns].astype(jnp.float32) for y in range(ny) for x in range(nx)]
            dst[pl.ds(pl.multiple_of(i * each, each), each), columns] = low(jnp.concatenate(found, 0))
        return carry
    lax.fori_loop(0, nz * cores, body, 0)


KEPT = ("x", "middle", "normed_t", "qkv", "lse", "att", "gate", "up", "nffn_t")


def kept_shapes(count, model, wide):
    size, each = lax.axis_size("ctx"), heads_each()
    f32, bf16 = jnp.float32, jnp.bfloat16
    return {
        "x": ((count, model), f32), "middle": ((count, model), f32), "normed_t": ((model, count), bf16),
        "qkv": ((3, each * HEAD_DIM, count * size), bf16), "lse": ((each, 1, count * size), f32),
        "att": ((each * size * HEAD_DIM, count), bf16), "gate": ((count, wide), f32), "up": ((count, wide), f32),
        "nffn_t": ((model, count), bf16)}


def named(names, refs):
    return dict(zip(names, refs, strict=True))


def forward_kernel(layers, vocab, third, names, *refs):
    r = named(names, refs)
    ends = ends_of(r["lengths"])
    size, me = lax.axis_size("ctx"), lax.axis_index("ctx")
    each = heads_each()
    keep = Keep(r["keep_sems"])
    kinds = ["small"] + [f"{kind}{l}" for l in range(layers) for kind in ("attn", "ffn", "down")]
    greet_all()
    ids, count = r["ids"], r["byte_ids"].shape[1]
    near = []
    for i, (there, at) in enumerate(((lax.rem(me + 1, size), 0), (lax.rem(me + size - 1, size), 2))):
        copy = to_group(r["byte_ids"], ids.at[:, pl.ds(at * count, count)], r["ids_sems"], (i,), there)
        copy.start()
        near.append(copy)
    ids[:, count:2 * count] = r["byte_ids"][...]
    chunks = [GatherChunk(r["shard_" + k], r["full_" + k], r["sems_" + k], r["local_sems"].at[i], third) for i, k in enumerate(kinds)]
    ticker = Ticker(chunks)
    tick = ticker.tick
    tick(2)
    tokens = count // 2
    seg_all = r["seg_all"]
    seg_all[...] = segments(2 * lax.broadcasted_iota(jnp.int32, seg_all.shape, 0), ends)
    for copy in near:
        copy.wait_recv()
    ticker.need(0)
    small = r["small_wide"]
    for z in range(r["full_small"].shape[0]):
        found = r["full_small"][z].astype(jnp.float32)
        rows = math.prod(found.shape[:-1])
        small[z * rows:(z + 1) * rows, :] = jnp.concatenate(
            [found[i, j, k] for i in range(found.shape[0]) for j in range(found.shape[1]) for k in range(found.shape[2])], 0)
    tick(2)
    stream = gbst_forward(ends, ids[...], me * count, small[...], r["conv"], r["choice"], vocab, tokens, tick).T
    at = vocab + CONV + 2
    gains = small[:, at // 128 * 128:].T
    at = at % 128
    model = stream.shape[1]
    keep(r["conv"], r["out_conv"])
    for l in range(layers):
        gain_a, gain_f = gains[at + l:at + l + 1, :], gains[at + layers + l:at + layers + l + 1, :]
        kept = {k: r[f"{k}{l}"] for k in KEPT}
        w_attn, w_ffn, w_down = r["w_attn"], r["w_ffn"], r["w_down"]
        first = 1 + 3 * l

        def fetch(i, dst, sem):
            ticker.need(i)
            copy = pltpu.make_async_copy(r["full_" + kinds[i]], dst, r["load_sems"].at[l, sem])
            copy.start()
            return copy
        load = fetch(first, r["blocks_attn"], 0)
        kept["x"][...] = stream
        normed = low(stream * inverse_rms(stream) * gain_a)
        kept["normed_t"][...] = flip(normed)
        load.wait()
        unpack(r["blocks_attn"], w_attn)
        tick()
        qkv_all = r["qkv_all"]
        for part in range(3):
            for c in range(model // CHUNK):
                columns = pl.ds(part * model + c * CHUNK, CHUNK)
                qkv_all[part, c * CHUNK:(c + 1) * CHUNK, :] = low(dot(normed, w_attn[:, columns]).T)
        qkv_copies = spread_heads(qkv_all, kept["qkv"], r["sems_qkv"].at[l], r["own_sems"].at[l], each)
        tick()
        keep(kept["x"], r[f"out_x{l}"])
        keep(kept["normed_t"], r[f"out_normed_t{l}"])
        out_copies = attention_forward(each, seg_all, ends, kept["qkv"], kept["lse"], r["out_send"], kept["att"],
                                       qkv_copies, r["sems_att"].at[l], tick)
        for copy in out_copies:
            copy.wait_recv()
        keep(kept["qkv"], r[f"out_qkv{l}"])
        keep(kept["lse"], r[f"out_lse{l}"])
        keep(kept["att"], r[f"out_att{l}"])
        attended = flip(kept["att"][:model, :])
        mid = stream + dot(attended, w_attn[:, 3 * model:])
        kept["middle"][...] = mid
        after = low(mid * inverse_rms(mid) * gain_f)
        r["nffn"][...] = after
        kept["nffn_t"][...] = flip(after)
        r["total"][...] = mid
        keep(kept["middle"], r[f"out_middle{l}"])
        keep(kept["nffn_t"], r[f"out_nffn_t{l}"])
        load = fetch(first + 1, r["blocks_ffn"], 1)
        load_down = fetch(first + 2, w_down, 2)
        load.wait()
        unpack(r["blocks_ffn"], w_ffn)
        tick()
        load_down.wait()
        nz, cores, ny, nx, rows, _ = w_down.shape
        wide, part = nz * cores * ny * nx * rows, ny * nx * rows

        def step(c, carry):
            columns = pl.ds(pl.multiple_of(c * part, part), part)
            gate = dot(r["nffn"][...], w_ffn[:, columns])
            up = dot(r["nffn"][...], w_ffn[:, pl.ds(pl.multiple_of(wide + c * part, part), part)])
            kept["gate"][:, columns] = gate
            kept["up"][:, columns] = up
            hidden = low(gelu_parts(gate)[0] * up)
            r["total"][...] += dot(hidden, w_down[c // cores, c % cores].reshape(part, model))
            return carry
        half = nz * cores // 2
        lax.fori_loop(0, half, step, 0)
        tick(2)
        lax.fori_loop(half, nz * cores, step, 0)
        keep(kept["gate"], r[f"out_gate{l}"])
        keep(kept["up"], r[f"out_up{l}"])
        stream = r["total"][...]
        for made in qkv_copies:
            for copy in made[:-1]:
                copy.wait_send()
        for copy in out_copies:
            copy.wait_send()
    r["encoded"][...] = low(stream)
    for copy in near:
        copy.wait_send()
    for i in range(len(chunks)):
        ticker.need(i)
    for chunk in chunks:
        chunk.finish()
    keep.finish()


def forward_pass(lengths, byte_ids, small, shards, layers, vocab, third, collective_id):
    nz, ny, nx = grid_of()
    size, each = lax.axis_size("ctx"), heads_each()
    model = shards[0].shape[1] // 4
    tokens = byte_ids.shape[1] // 2
    wide = shards[1].shape[1] // 2
    span = byte_ids.shape[1] + 2 * HALO
    f32, bf16 = jnp.float32, jnp.bfloat16
    made = lambda shape, dtype: jax.ShapeDtypeStruct(shape, dtype)
    whole = lambda s: (nz, CORES, ny, nx) + s.shape
    kinds = [f"{kind}{l}" for l in range(layers) for kind in ("attn", "ffn", "down")]
    inputs = {"lengths": (lengths, SMEM), "byte_ids": (byte_ids, VMEM), "shard_small": (small, ANY)}
    for k, s in zip(kinds, shards):
        inputs["shard_" + k] = (s, ANY)
    outputs = {"encoded": (made((tokens, model), bf16), VMEM), "small_wide": (made((model, small.shape[1]), f32), VMEM),
               "ids": (made((1, 3 * byte_ids.shape[1]), jnp.int32), VMEM), "choice": (made((2 * len(BLOCKS), tokens), f32), VMEM),
               "out_conv": (made((model, span), f32), ANY)}
    for k, s in zip(kinds, shards):
        outputs["full_" + k] = (made(whole(s), bf16), ANY)
    shapes = kept_shapes(tokens, model, wide)
    for l in range(layers):
        for k in KEPT:
            outputs[f"out_{k}{l}"] = (made(*shapes[k]), ANY)
    rows = each * size * HEAD_DIM
    dma = pltpu.SemaphoreType.DMA
    scratch = {"full_small": pltpu.VMEM(whole(small), bf16), "conv": pltpu.VMEM((model, span), f32),
               "w_attn": pltpu.VMEM((model, 4 * model), bf16), "w_ffn": pltpu.VMEM((model, 2 * wide), bf16),
               "w_down": pltpu.VMEM(whole(shards[2]), bf16), "blocks_attn": pltpu.VMEM(whole(shards[0]), bf16),
               "blocks_ffn": pltpu.VMEM(whole(shards[1]), bf16), "qkv_all": pltpu.VMEM((3, rows, tokens), bf16),
               "out_send": pltpu.VMEM((each, size - 1, HEAD_DIM, tokens), bf16),
               "seg_all": pltpu.VMEM((tokens * size, tokens), jnp.int32), "nffn": pltpu.VMEM((tokens, model), bf16),
               "total": pltpu.VMEM((tokens, model), f32),
               "keep_sems": dma((1 + layers * len(KEPT),)), "ids_sems": dma((2, 2)), "local_sems": dma((1 + len(kinds),)),
               "load_sems": dma((layers, 3)), "own_sems": dma((layers, each)),
               "sems_qkv": dma((layers, 2, each, size - 1)), "sems_att": dma((layers, 2, each, size - 1)),
               "sems_small": dma((2, hops(small.shape[1], third)))}
    for k, s in zip(kinds, shards):
        scratch["sems_" + k] = dma((2, hops(s.shape[1], third)))
    for l in range(layers):
        for k in KEPT:
            scratch[f"{k}{l}"] = pltpu.VMEM(*shapes[k])
    names = [*inputs, *outputs, *scratch]
    found = pl.pallas_call(
        functools.partial(forward_kernel, layers, vocab, third, names),
        out_shape=[s for s, _ in outputs.values()],
        in_specs=[s for _, s in inputs.values()],
        out_specs=[s for _, s in outputs.values()],
        scratch_shapes=list(scratch.values()),
        compiler_params=pltpu.CompilerParams(collective_id=collective_id, has_side_effects=True, vmem_limit_bytes=60 << 20),
        name="forward_pass",
    )(*[a for a, _ in inputs.values()])
    return named(outputs, found)


def packed_small(embed, conv_weight, conv_bias, scorer, norm_attn, norm_ffn):
    rows = jnp.concatenate([embed, conv_weight, conv_bias[None], scorer[None], norm_attn, norm_ffn], 0).T
    return jnp.pad(rows, ((0, 0), (0, -rows.shape[1] % 128)))


def split_small(rows, vocab, layers):
    at = vocab + CONV
    return (rows[:vocab], rows[vocab:at], rows[at], rows[at + 1], rows[at + 2 : at + 2 + layers],
            rows[at + 2 + layers : at + 2 + 2 * layers])


def separate_forward(lengths, byte_ids, shards, layer_count, vocab, model):
    ring, tokens = lax.axis_size("ctx"), byte_ids.shape[1] // 2
    up = [(i, (i + 1) % ring) for i in range(ring)]
    down = [(j, i) for i, j in up]
    ids = jnp.concatenate([lax.ppermute(byte_ids, "ctx", up), byte_ids, lax.ppermute(byte_ids, "ctx", down)], 1)
    small_full, *full = [a.reshape(-1, a.shape[-1]) for a in gather_all(shards, 0)]
    small_wide = small_full.astype(jnp.float32)
    gains = small_wide.T[vocab + CONV + 2 :]
    stream, conv, choice = pl.pallas_call(
        functools.partial(gbst_forward_kernel, vocab, tokens),
        out_shape=[
            jax.ShapeDtypeStruct((tokens, model), jnp.float32),
            jax.ShapeDtypeStruct((model, byte_ids.shape[1] + 2 * HALO), jnp.float32),
            jax.ShapeDtypeStruct((2 * len(BLOCKS), tokens), jnp.float32),
        ],
        in_specs=[SMEM, VMEM, VMEM],
        out_specs=[VMEM] * 3,
        compiler_params=pltpu.CompilerParams(vmem_limit_bytes=56 << 20),
        name="mix_bytes",
    )(lengths, ids, small_wide)
    kept = []
    for layer in range(layer_count):
        before = stream
        stream, *saved = layer_forward(
            lengths, stream, gains[layer][None], gains[layer_count + layer][None], *full[3 * layer : 3 * layer + 3], 2
        )
        kept.append((before, saved))
    return stream.astype(jnp.bfloat16), full, small_wide, ids, conv, choice, kept


def fused_forward(lengths, byte_ids, shards, layer_count, vocab, model):
    kinds = [f"{kind}{layer}" for layer in range(layer_count) for kind in ("attn", "ffn", "down")]
    fwd = forward_pass(lengths, byte_ids, shards[0], shards[1:], layer_count, vocab, THIRD, 4)
    full = [fwd["full_" + k].reshape(-1, fwd["full_" + k].shape[-1]) for k in kinds]
    kept = []
    for layer in range(layer_count):
        saved = [fwd[f"out_{k}{layer}"] for k in KEPT]
        kept.append((saved[0], saved[1:]))
    return fwd["encoded"], full, fwd["small_wide"], fwd["ids"], fwd["out_conv"], fwd["choice"], kept


def on_device(
    byte_ids,
    lengths,
    embed,
    conv_weight,
    conv_bias,
    scorer,
    norm_attn,
    query_w,
    key_w,
    value_w,
    attn_out_w,
    norm_ffn,
    gate_w,
    up_w,
    down_w,
    out_grad,
):
    ctx_count = lax.axis_size("ctx")
    ctx_place = lax.axis_index("ctx")
    layer_count = query_w.shape[0]
    vocab = embed.shape[0]
    model = query_w.shape[2]
    byte_count = byte_ids.shape[1]
    small = packed_small(embed, conv_weight, conv_bias, scorer, norm_attn, norm_ffn)
    shards = [small]
    for layer in range(layer_count):
        shards.append(jnp.concatenate([query_w[layer], key_w[layer], value_w[layer], attn_out_w[layer]], 1))
        shards.append(jnp.concatenate([gate_w[layer], up_w[layer]], 1))
        shards.append(down_w[layer])
    fused = shards[1].shape[0] % 8 == 0 and HEADS % lax.axis_size("ctx") == 0
    encoded, full, small_wide, ids, conv, choice, kept = (fused_forward if fused else separate_forward)(
        lengths, byte_ids, shards, layer_count, vocab, model
    )
    encoded = encoded[None]
    gains = small_wide.T[vocab + CONV + 2 :]
    gains_a, gains_f = gains[:layer_count], gains[layer_count : 2 * layer_count]
    grad_stream = out_grad[0].astype(jnp.float32)
    partial = []
    gains = []
    for layer in reversed(range(layer_count)):
        before, saved = kept[layer]
        weights = full[3 * layer : 3 * layer + 3]
        grad_stream, d_gain_attn, d_gain_ffn, *grads = layer_backward(
            lengths, grad_stream, before, gains_a[layer][None], gains_f[layer][None], saved, *weights, 3
        )
        partial = list(grads) + partial
        gains = [(d_gain_attn[0], d_gain_ffn[0])] + gains
    small_grad = pl.pallas_call(
        functools.partial(gbst_backward_kernel, vocab),
        out_shape=jax.ShapeDtypeStruct(small_wide.shape, jnp.float32),
        in_specs=[SMEM] + [VMEM] * 5,
        out_specs=VMEM,
        compiler_params=pltpu.CompilerParams(vmem_limit_bytes=56 << 20),
        name="mix_bytes_backward",
    )(lengths, ids, small_wide, conv, choice, grad_stream)
    columns = jnp.stack([a for a, _ in gains] + [f for _, f in gains]).T
    small_grad = lax.dynamic_update_slice(small_grad, columns, (0, vocab + CONV + 2))
    outs = scatter_all([p.astype(jnp.bfloat16) for p in [small_grad] + partial], 1)
    small_out, *rest = outs
    g_embed, g_conv, g_bias, g_scorer, g_norm_a, g_norm_f = split_small(small_out.T, vocab, layer_count)
    attn_out, ffn_out, down_out = rest[0::3], rest[1::3], rest[2::3]
    columns = [jnp.stack([a[:, i * model : (i + 1) * model] for a in attn_out]) for i in range(4)]
    wide = ffn_out[0].shape[1] // 2
    return (
        encoded,
        g_embed,
        g_conv,
        g_bias,
        g_scorer,
        g_norm_a,
        columns[0],
        columns[1],
        columns[2],
        columns[3],
        g_norm_f,
        jnp.stack([a[:, :wide] for a in ffn_out]),
        jnp.stack([a[:, wide:] for a in ffn_out]),
        jnp.stack(down_out),
    )


def solution(mesh):
    placed = (
        P("dp", "ctx"),
        P("dp", None),
        P(None, ("dp", "ctx")),
        P(None, ("dp", "ctx")),
        P(("dp", "ctx")),
        P(("dp", "ctx")),
        P(None, ("dp", "ctx")),
        P(None, ("dp", "ctx"), None),
        P(None, ("dp", "ctx"), None),
        P(None, ("dp", "ctx"), None),
        P(None, ("dp", "ctx"), None),
        P(None, ("dp", "ctx")),
        P(None, ("dp", "ctx"), None),
        P(None, ("dp", "ctx"), None),
        P(None, ("dp", "ctx"), None),
        P("dp", "ctx", None),
    )
    return jax.shard_map(
        on_device,
        mesh=mesh,
        in_specs=placed,
        out_specs=(
            P("dp", "ctx", None),
            P(None, ("dp", "ctx")),
            P(None, ("dp", "ctx")),
            P(("dp", "ctx")),
            P(("dp", "ctx")),
            P(None, ("dp", "ctx")),
            P(None, ("dp", "ctx"), None),
            P(None, ("dp", "ctx"), None),
            P(None, ("dp", "ctx"), None),
            P(None, ("dp", "ctx"), None),
            P(None, ("dp", "ctx")),
            P(None, ("dp", "ctx"), None),
            P(None, ("dp", "ctx"), None),
            P(None, ("dp", "ctx"), None),
        ),
        check_vma=False,
    )
```

```python
import functools
import types
import jax
import jax.numpy as jnp
from jax import lax
from jax.experimental import pallas as pl
from jax.experimental.pallas import tpu as pltpu
from jax.sharding import PartitionSpec as P


MESH = pl.DeviceIdType.MESH
CORES = 2
LANES = 128
THIRD = 0.1
DEPTH = 2
SPLIT = 3


def grid_of():
    dp, ctx = lax.axis_size("dp"), lax.axis_size("ctx")
    rows = 2 if ctx % 2 == 0 else 1
    return dp // CORES, rows, ctx // rows


def place_of():
    _, _, nx = grid_of()
    d, c = lax.axis_index("dp"), lax.axis_index("ctx")
    return d // CORES, d % CORES, c // nx, c % nx


def device(z, core, y, x):
    _, _, nx = grid_of()
    return (z * CORES + core, y * nx + x)


def along(axis):
    place = list(place_of())
    nz, ny, nx = grid_of()
    size = (nz, CORES, ny, nx)[axis]
    found = []
    for i in range(1, size):
        there = list(place)
        there[axis] = lax.rem(place[axis] + i, size)
        found.append((there[axis], device(*there)))
    return found


def sibling():
    z, core, y, x = place_of()
    return device(z, 1 - core, y, x)


def greet_all():
    barrier = pltpu.get_barrier_semaphore()
    targets = [target for axis in (0, 2, 3) for _, target in along(axis)] + [sibling()]
    _, ny, nx = grid_of()
    z, core, y, x = place_of()
    for i in range(1, ny):
        for j in range(1, nx):
            targets.append(device(z, core, lax.rem(y + i, ny), lax.rem(x + j, nx)))
    for target in targets:
        pl.semaphore_signal(barrier, inc=1, device_id=target, device_id_type=MESH)
    pl.semaphore_wait(barrier, len(targets))
    return targets


ORDERS = ((0, 3, 2), (0, 2, 3), (3, 2, 0))


def splits_of(width, count):
    units = width // LANES
    cuts = [units * i // count * LANES for i in range(count + 1)]
    return [(a, b - a) for a, b in zip(cuts, cuts[1:])]


def pieces_of(width, third, first=0):
    units = width // LANES
    last = int(units * third)
    left = (units - last + 1) // 2
    found, at = [], first // LANES
    for order, size in zip(ORDERS, (left, units - last - left, last)):
        if size:
            found.append((pl.ds(at * LANES, size * LANES), order))
        at += size
    return found


def hops(width, third):
    nz, ny, nx = grid_of()
    return len(pieces_of(width, third)) * (nz - 1 + ny - 1 + nx - 1) + 1


class Sender:
    def __init__(self, sems):
        self.sems, self.count, self.flying = sems, 0, []

    def send(self, src, dst, target):
        copy = pltpu.make_async_remote_copy(
            src_ref=src, dst_ref=dst, send_sem=self.sems.at[0, self.count], recv_sem=self.sems.at[1, self.count],
            device_id=target, device_id_type=MESH)
        copy.start()
        self.count += 1
        self.flying.append(copy)
        return copy

    def finish(self):
        for copy in self.flying:
            copy.wait_send()
        self.flying = []


class GatherChunk(Sender):
    phases = 4

    def __init__(self, shard, out, sems, local_sem, third):
        super().__init__(sems)
        self.shard, self.out, self.local_sem = shard, out, local_sem
        self.pieces = pieces_of(shard.shape[-1], third)
        self.waiting = []

    def stage(self, number):
        place = place_of()
        for copy in self.waiting:
            copy.wait_recv()
        self.waiting = []
        if number == 0:
            self.own = pltpu.make_async_copy(self.shard, self.out.at[place], self.local_sem)
            self.own.start()
        if number == 1:
            self.own.wait()
        if number < 3:
            for columns, order in self.pieces:
                have = order[:number]
                where = tuple(slice(None) if axis in have else place[axis] for axis in range(4)) + (slice(None), columns)
                src = self.out.at[where] if number else self.shard.at[:, columns]
                for _, target in along(order[number]):
                    self.waiting.append(self.send(src, self.out.at[where], target))
        else:
            where = (slice(None), place[1])
            self.waiting.append(self.send(self.out.at[where], self.out.at[where], sibling()))

    def arrive(self):
        for copy in self.waiting:
            copy.wait_recv()
        self.waiting = []


class Pipeline:
    def __init__(self, chunks):
        self.chunks, self.steps, self.done = chunks, [], [0] * len(chunks)
        phases = chunks[0].phases
        for t in range(len(chunks) + phases):
            for number in [0] + list(range(phases - 1, 0, -1)):
                if 0 <= t - number < len(chunks):
                    self.steps.append((t - number, number))

    def tick(self, count=1):
        for _ in range(count):
            if self.steps:
                i, number = self.steps.pop(0)
                self.chunks[i].stage(number)
                self.done[i] = number + 1

    def until(self, i):
        while self.done[i] < self.chunks[i].phases:
            self.tick()

    def need(self, i):
        self.until(i)
        self.chunks[i].arrive()


def gather_kernel(n, third, *refs):
    shards, outs, sems, local_sems = refs[:n], refs[n:2 * n], refs[2 * n:3 * n], refs[3 * n]
    greet_all()
    chunks = [GatherChunk(shards[i], outs[i], sems[i], local_sems.at[i], third) for i in range(n)]
    ticker = Pipeline(chunks)
    for i in range(n):
        ticker.need(i)
    for chunk in chunks:
        chunk.finish()


def gather_all(shards, collective_id, third=THIRD):
    nz, ny, nx = grid_of()
    n = len(shards)
    outs = pl.pallas_call(
        functools.partial(gather_kernel, n, third),
        out_shape=[jax.ShapeDtypeStruct((nz, CORES, ny, nx) + s.shape, s.dtype) for s in shards],
        in_specs=[pl.BlockSpec(memory_space=pl.ANY)] * n,
        out_specs=[pl.BlockSpec(memory_space=pl.ANY)] * n,
        scratch_shapes=[pltpu.SemaphoreType.DMA((2, hops(s.shape[-1], third))) for s in shards] + [pltpu.SemaphoreType.DMA((n,))],
        compiler_params=pltpu.CompilerParams(collective_id=collective_id, has_side_effects=True),
        name="gather_weights",
    )(*shards)
    return [o.reshape((-1,) + o.shape[5:]) for o in outs]


def add_into(dst, src, lead):
    if not lead:
        dst[...] = (dst[...].astype(jnp.float32) + src[...].astype(jnp.float32)).astype(dst.dtype)
        return

    def body(i, carry):
        add_into(dst.at[i], src.at[i], lead[1:])
        return carry
    lax.fori_loop(0, lead[0], body, 0)


class ScatterChunk(Sender):
    phases = 5

    def __init__(self, parts, out, scratch, sems, local_sem, third):
        super().__init__(sems)
        self.parts, self.out, self.local_sem = parts, out, local_sem
        self.held, self.across, *landing = scratch
        self.pieces = [(columns, order[::-1], landing[3 * i:3 * i + 3])
                       for i, (columns, order) in enumerate(pieces_of(parts.shape[-1], third))]
        self.waiting = []

    @staticmethod
    def scratch(shape, dtype, third):
        sizes = dict(zip((0, 2, 3), grid_of()))
        whole = (*sizes.values(), *shape)
        found = [whole, whole]
        for columns, order in pieces_of(shape[-1], third):
            order = order[::-1]
            for number in range(3):
                rest = [sizes[a] for a in sizes if a in order[number + 1:]]
                found.append((sizes[order[number]] - 1, *rest, shape[0], columns.size))
        return [pltpu.VMEM(s, dtype) for s in found]

    def stage(self, number):
        place = place_of()
        sizes = dict(zip((0, 2, 3), grid_of()))
        for copy in self.waiting:
            copy.wait_recv()
        self.waiting = []
        if number == 0:
            self.own = pltpu.make_async_copy(self.parts.at[:, place[1]], self.held, self.local_sem)
            self.own.start()
            self.waiting.append(self.send(self.parts.at[:, 1 - place[1]], self.across, sibling()))
            return
        if number == 1:
            self.own.wait()
            add_into(self.held, self.across, list(sizes.values()))
        for columns, order, landing in self.pieces:
            if number > 1:
                mine = order[:number - 1]
                where = tuple(place[a] if a in mine else slice(None) for a in sizes) + (slice(None), columns)
                lead = [sizes[a] for a in sizes if a not in mine]
                landed = landing[number - 2]
                if number < 4:
                    for i in range(landed.shape[0]):
                        add_into(self.held.at[where], landed.at[i], lead)
                else:
                    total = self.held[where].astype(jnp.float32)
                    for i in range(landed.shape[0]):
                        total = total + landed[i].astype(jnp.float32)
                    self.out[:, columns] = total
            if number < 4:
                axis, mine = order[number - 1], order[:number - 1]
                for i, (there, target) in enumerate(along(axis)):
                    where = tuple(there if a == axis else place[a] if a in mine else slice(None) for a in sizes)
                    src = self.held.at[where + (slice(None), columns)]
                    self.waiting.append(self.send(src, landing[number - 1].at[i], target))


def scatter_kernel(n, third, counts, *refs):
    parts, outs, rest = refs[:n], refs[n:2 * n], list(refs[2 * n:])
    greet_all()
    chunks = []
    for i in range(n):
        scratch = [rest.pop(0) for _ in range(counts[i])]
        chunks.append(ScatterChunk(parts[i], outs[i], scratch, rest.pop(0), rest.pop(0), third))
    ticker = Pipeline(chunks)
    for i in range(n):
        ticker.until(i)
    for chunk in chunks:
        chunk.finish()


def scatter_scratch(shape, dtype, third):
    scratch = ScatterChunk.scratch(shape, dtype, third)
    return scratch + [pltpu.SemaphoreType.DMA((2, hops(shape[-1], third))), pltpu.SemaphoreType.DMA]


def scatter_all(parts, collective_id, third=THIRD):
    nz, ny, nx = grid_of()
    n = len(parts)
    devices = nz * CORES * ny * nx
    parts = [p.reshape((nz, CORES, ny, nx, p.shape[0] // devices) + p.shape[1:]) for p in parts]
    scratch, counts = [], []
    for p in parts:
        made = scatter_scratch(p.shape[4:], p.dtype, third)
        counts.append(len(made) - 2)
        scratch += made
    return pl.pallas_call(
        functools.partial(scatter_kernel, n, third, counts),
        out_shape=[jax.ShapeDtypeStruct(p.shape[4:], jnp.float32) for p in parts],
        in_specs=[pl.BlockSpec(memory_space=pl.ANY)] * n,
        out_specs=[pl.BlockSpec(memory_space=pltpu.VMEM)] * n,
        scratch_shapes=scratch,
        compiler_params=pltpu.CompilerParams(collective_id=collective_id, has_side_effects=True, vmem_limit_bytes=60 << 20),
        name="scatter_grads",
    )(*parts)


HEADS = 12
HEAD_DIM = 64
CHUNK = 256
NORM_EPS = 1e-06
NEG_FILL = -1000000000.0
GELU_A = 0.7978845608028654
GELU_B = 0.044715


def dot(a, b):
    return jnp.dot(a, b, preferred_element_type=jnp.float32)


def dot_nt(a, b):
    return lax.dot_general(a, b, (((1,), (1,)), ((), ())), preferred_element_type=jnp.float32)


def low(v):
    return v.astype(jnp.bfloat16)


def flip(v):
    return low(v.astype(jnp.float32).T)


def inverse_rms(v):
    return lax.rsqrt(jnp.mean(v * v, -1, keepdims=True) + NORM_EPS)


def ends_of(lengths_ref):
    ends, total = [], 0
    for i in range(lengths_ref.shape[-1]):
        total = total + lengths_ref[0, i]
        ends.append(total)
    return ends


def segments(places, ends):
    seg = jnp.zeros(places.shape, jnp.int32)
    for end in ends:
        seg = seg + jnp.where(places >= end, 1, 0)
    return seg


def heads_each():
    return -(-HEADS // lax.axis_size("ctx"))


def others():
    size, me = lax.axis_size("ctx"), lax.axis_index("ctx")
    return [lax.rem(me + 1 + i, size) for i in range(size)]


def greet_group():
    barrier = pltpu.get_barrier_semaphore()
    peers_ = others()[:-1]
    for p in peers_:
        pl.semaphore_signal(barrier, inc=1, device_id=(lax.axis_index("dp"), p), device_id_type=MESH)
    pl.semaphore_wait(barrier, len(peers_))


def to_group(src, dst, sems, index, p):
    return pltpu.make_async_remote_copy(
        src_ref=src, dst_ref=dst, send_sem=sems.at[(0,) + index], recv_sem=sems.at[(1,) + index],
        device_id=(lax.axis_index("dp"), p), device_id_type=MESH)


def tokens_of(p, count):
    return pl.ds(pl.multiple_of(p * count, count), count)


def spread_heads(src, dst, sems, local_sem, each):
    me = lax.axis_index("ctx")
    count = src.shape[2]
    copies = []
    for h in range(each):
        rows = pl.ds(h * HEAD_DIM, HEAD_DIM)
        made = []
        for i, p in enumerate(others()):
            theirs = pl.ds(pl.multiple_of((p * each + h) * HEAD_DIM, HEAD_DIM), HEAD_DIM)
            a, b = src.at[:, theirs], dst.at[:, rows, tokens_of(me, count)]
            if i == lax.axis_size("ctx") - 1:
                copy = pltpu.make_async_copy(a, b, local_sem.at[h])
            else:
                copy = to_group(a, b, sems, (h, i), p)
            copy.start()
            made.append(copy)
        copies.append(made)
    return copies


def arrive(made):
    for copy in made[:-1]:
        copy.wait_recv()
    made[-1].wait()


def attention_forward(each, seg_all, ends, qkv, lse, out_send, att, qkv_copies, sems, tick=lambda: None):
    size, me = lax.axis_size("ctx"), lax.axis_index("ctx")
    count = att.shape[1]
    copies = []
    for h in range(each):
        arrive(qkv_copies[h])
        rows = pl.ds(h * HEAD_DIM, HEAD_DIM)
        key = flip(qkv[1, rows, :])
        value_t = qkv[2, rows, :]
        theirs = pl.ds(pl.multiple_of((me * each + h) * HEAD_DIM, HEAD_DIM), HEAD_DIM)
        for i, p in enumerate(others()):
            tokens = tokens_of(p, count)
            seg_q = segments(2 * (p * count + lax.broadcasted_iota(jnp.int32, (1, count), 1)), ends)
            scores = dot(key, qkv[0, rows, tokens])
            scores = jnp.where(seg_all[...] == seg_q, scores, NEG_FILL)
            top = jnp.max(scores, 0, keepdims=True)
            probs = jnp.exp(scores - top)
            total = jnp.sum(probs, 0, keepdims=True)
            lse[h, :, tokens] = top + jnp.log(total)
            result = low(dot(value_t, low(probs)) / total)
            if i == size - 1:
                att[theirs, :] = result
            else:
                out_send[h, i] = result
                copy = to_group(out_send.at[h, i], att.at[theirs], sems, (h, i), p)
                copy.start()
                copies.append(copy)
            tick()
    return copies


def gelu_parts(gate):
    inner = jnp.tanh(GELU_A * (gate + GELU_B * gate * gate * gate))
    half = 0.5 * (1.0 + inner)
    slope = half + 0.5 * gate * (1.0 - inner * inner) * GELU_A * (1.0 + 3.0 * GELU_B * gate * gate)
    return gate * half, slope


def layer_forward_kernel(lengths, x, gain_a, gain_f, w_attn_hbm, w_ffn_hbm, w_down_hbm,
                         out, middle, normed_t, qkv, lse, att, gate_out, up_out, nffn_t,
                         w_attn, w_ffn, w_down, qkv_all, out_send, seg_all, nffn,
                         sems_in, sems_out, local_sems, w_sems):
    each = heads_each()
    model = x.shape[1]
    loads = [pltpu.make_async_copy(a, b, w_sems.at[i]) for i, (a, b) in enumerate(
        ((w_attn_hbm, w_attn), (w_ffn_hbm, w_ffn), (w_down_hbm, w_down)))]
    for load in loads:
        load.start()
    greet_group()
    ends = ends_of(lengths)
    seg_all[...] = segments(2 * lax.broadcasted_iota(jnp.int32, seg_all.shape, 0), ends)
    stream = x[...]
    normed = low(stream * inverse_rms(stream) * gain_a[...])
    normed_t[...] = flip(normed)
    if qkv_all.shape[1] > model:
        qkv_all[:, model:, :] = jnp.zeros((3, qkv_all.shape[1] - model, qkv_all.shape[2]), jnp.bfloat16)
    loads[0].wait()
    for part in range(3):
        for c in range(model // CHUNK):
            columns = pl.ds(part * model + c * CHUNK, CHUNK)
            qkv_all[part, c * CHUNK:(c + 1) * CHUNK, :] = low(dot(normed, w_attn[:, columns]).T)
    qkv_copies = spread_heads(qkv_all, qkv, sems_in, local_sems, each)
    out_copies = attention_forward(each, seg_all, ends, qkv, lse, out_send, att, qkv_copies, sems_out)
    for copy in out_copies:
        copy.wait_recv()
    attended = flip(att[:model, :])
    mid = stream + dot(attended, w_attn[:, 3 * model:])
    middle[...] = mid
    after = low(mid * inverse_rms(mid) * gain_f[...])
    nffn[...] = after
    nffn_t[...] = flip(after)
    out[...] = mid
    loads[1].wait()
    loads[2].wait()
    hidden_count = w_down.shape[0]

    def step(c, carry):
        columns = pl.ds(pl.multiple_of(c * CHUNK, CHUNK), CHUNK)
        gate = dot(nffn[...], w_ffn[:, columns])
        up = dot(nffn[...], w_ffn[:, pl.ds(pl.multiple_of(hidden_count + c * CHUNK, CHUNK), CHUNK)])
        gate_out[:, columns] = gate
        up_out[:, columns] = up
        hidden = low(gelu_parts(gate)[0] * up)
        out[...] += dot(hidden, w_down[columns, :])
        return carry
    lax.fori_loop(0, hidden_count // CHUNK, step, 0)
    for made in qkv_copies:
        for copy in made[:-1]:
            copy.wait_send()
    for copy in out_copies:
        copy.wait_send()


VMEM = pl.BlockSpec(memory_space=pltpu.VMEM)
ANY = pl.BlockSpec(memory_space=pl.ANY)
SMEM = pl.BlockSpec(memory_space=pltpu.SMEM)


def layer_forward(lengths, x, gain_a, gain_f, w_attn, w_ffn, w_down, collective_id):
    size, each = lax.axis_size("ctx"), heads_each()
    count, model = x.shape
    wide = w_down.shape[0]
    group = count * size
    rows = each * size * HEAD_DIM
    f32, bf16 = jnp.float32, jnp.bfloat16
    made = lambda shape, dtype: jax.ShapeDtypeStruct(shape, dtype)
    return pl.pallas_call(
        layer_forward_kernel,
        out_shape=[made((count, model), f32), made((count, model), f32), made((model, count), bf16),
                   made((3, each * HEAD_DIM, group), bf16), made((each, 1, group), f32), made((rows, count), bf16),
                   made((count, wide), f32), made((count, wide), f32), made((model, count), bf16)],
        in_specs=[SMEM, VMEM, VMEM, VMEM, ANY, ANY, ANY],
        out_specs=[VMEM] * 9,
        scratch_shapes=[
            pltpu.VMEM(w_attn.shape, bf16), pltpu.VMEM(w_ffn.shape, bf16), pltpu.VMEM(w_down.shape, bf16),
            pltpu.VMEM((3, rows, count), bf16), pltpu.VMEM((each, size - 1, HEAD_DIM, count), bf16),
            pltpu.VMEM((group, count), jnp.int32), pltpu.VMEM((count, model), bf16),
            pltpu.SemaphoreType.DMA((2, each, size - 1)), pltpu.SemaphoreType.DMA((2, each, size - 1)),
            pltpu.SemaphoreType.DMA((each,)), pltpu.SemaphoreType.DMA((3,))],
        compiler_params=pltpu.CompilerParams(collective_id=collective_id, has_side_effects=True, vmem_limit_bytes=56 << 20),
        name="layer_forward",
    )(lengths, x, gain_a, gain_f, w_attn, w_ffn, w_down)


def layer_backward_kernel(lengths, grad, x, gain_a, gain_f, middle, normed_t, qkv, lse, att, gate_in, up_in, nffn_t,
                          w_attn_hbm, w_ffn_hbm, w_down_hbm,
                          grad_in, d_gain_a, d_gain_f, d_attn_hbm, d_ffn_hbm, d_down_hbm,
                          w_attn, w_ffn, w_down, d_attn, d_ffn, d_down, go_all, go, dqkv, q_send, kv_send, seg_all, total,
                          grad_low, mid_low, sems_in, sems_q, sems_kv, local_sems, w_sems, d_sems):
    each = heads_each()
    size, me = lax.axis_size("ctx"), lax.axis_index("ctx")
    count, model = x.shape
    wide = w_down.shape[0]
    loads = [pltpu.make_async_copy(a, b, w_sems.at[i]) for i, (a, b) in enumerate(
        ((w_down_hbm, w_down), (w_ffn_hbm, w_ffn), (w_attn_hbm, w_attn)))]
    for load in loads:
        load.start()
    greet_group()
    ends = ends_of(lengths)
    seg_all[...] = segments(2 * lax.broadcasted_iota(jnp.int32, seg_all.shape, 0), ends)
    grad_low[...] = low(grad[...])
    total[...] = jnp.zeros(total.shape, jnp.float32)
    loads[0].wait()
    loads[1].wait()

    def step(c, carry):
        columns = pl.ds(pl.multiple_of(c * CHUNK, CHUNK), CHUNK)
        later = pl.ds(pl.multiple_of(wide + c * CHUNK, CHUNK), CHUNK)
        g_hidden = dot_nt(grad_low[...], w_down[columns, :])
        up = up_in[:, columns]
        act, slope = gelu_parts(gate_in[:, columns])
        g_gate = low(g_hidden * up * slope)
        g_up = low(g_hidden * act)
        d_down[columns, :] = low(dot(low((act * up).T), grad_low[...]))
        d_ffn[:, columns] = low(dot(nffn_t[...], g_gate))
        d_ffn[:, later] = low(dot(nffn_t[...], g_up))
        total[...] += dot_nt(g_gate, w_ffn[:, columns]) + dot_nt(g_up, w_ffn[:, later])
        return carry
    lax.fori_loop(0, wide // CHUNK, step, 0)
    saves = [pltpu.make_async_copy(d_ffn, d_ffn_hbm, d_sems.at[0]), pltpu.make_async_copy(d_down, d_down_hbm, d_sems.at[1])]
    for save in saves:
        save.start()

    def norm_back(values, gain, upstream):
        scale = inverse_rms(values)
        scaled = upstream * gain
        along = jnp.mean(values * scaled, -1, keepdims=True)
        return scale * scaled - values * (scale * scale * scale * along), jnp.sum(upstream * values * scale, 0, keepdims=True)

    back, d_gain = norm_back(middle[...], gain_f[...], total[...])
    d_gain_f[...] = d_gain
    grad_in[...] = grad[...] + back
    mid_low[...] = low(grad_in[...])
    if go_all.shape[1] > model:
        go_all[:, model:, :] = jnp.zeros((1, go_all.shape[1] - model, count), jnp.bfloat16)
    loads[2].wait()
    for c in range(model // CHUNK):
        rows = slice(c * CHUNK, (c + 1) * CHUNK)
        go_all[0, rows, :] = low(dot_nt(mid_low[...], w_attn[rows, 3 * model:]).T)
    go_copies = spread_heads(go_all, go, sems_in, local_sems, each)
    for c in range(model // CHUNK):
        rows = slice(c * CHUNK, (c + 1) * CHUNK)
        d_attn[rows, 3 * model:] = low(dot(att[rows, :], mid_low[...]))
    sent = []
    for h in range(each):
        arrive(go_copies[h])
        rows = pl.ds(h * HEAD_DIM, HEAD_DIM)
        theirs = pl.ds(pl.multiple_of((me * each + h) * HEAD_DIM, HEAD_DIM), HEAD_DIM)
        key_t = qkv[1, rows, :]
        key, value = flip(key_t), flip(qkv[2, rows, :])
        g_key = jnp.zeros((HEAD_DIM, count * size), jnp.float32)
        g_value = jnp.zeros((HEAD_DIM, count * size), jnp.float32)
        for i, p in enumerate(others()):
            tokens = tokens_of(p, count)
            seg_q = segments(2 * (p * count + lax.broadcasted_iota(jnp.int32, (1, count), 1)), ends)
            query_t, go_t = qkv[0, rows, tokens], go[0, rows, tokens]
            scores = jnp.where(seg_all[...] == seg_q, dot(key, query_t), NEG_FILL)
            probs = jnp.exp(scores - lse[h, :, tokens])
            g_probs = dot(value, go_t)
            inner = jnp.sum(probs * g_probs, 0, keepdims=True)
            g_scores = low(probs * (g_probs - inner))
            g_query = low(dot(key_t, g_scores))
            g_key = g_key + dot_nt(query_t, g_scores)
            g_value = g_value + dot_nt(go_t, low(probs))
            if i == size - 1:
                dqkv[0, theirs, :] = g_query
            else:
                q_send[h, i] = g_query
                copy = to_group(q_send.at[h, i], dqkv.at[0, theirs], sems_q, (h, i), p)
                copy.start()
                sent.append(copy)
        kv_send[h, 0] = low(g_key)
        kv_send[h, 1] = low(g_value)
        for i, p in enumerate(others()):
            if i == size - 1:
                dqkv[1:, theirs, :] = kv_send[h, :, :, tokens_of(me, count)]
            else:
                copy = to_group(kv_send.at[h, :, :, tokens_of(p, count)], dqkv.at[pl.ds(1, 2), theirs], sems_kv, (h, i), p)
                copy.start()
                sent.append(copy)
    for copy in sent:
        copy.wait_recv()
    summed = jnp.zeros((model, count), jnp.float32)
    for part in range(3):
        for c in range(model // CHUNK):
            rows = slice(c * CHUNK, (c + 1) * CHUNK)
            columns = slice(part * model + c * CHUNK, part * model + (c + 1) * CHUNK)
            d_attn[:, columns] = low(dot_nt(normed_t[...], dqkv[part, rows, :]))
        summed = summed + dot(w_attn[:, part * model:(part + 1) * model], dqkv[part, :model, :])
    saves.append(pltpu.make_async_copy(d_attn, d_attn_hbm, d_sems.at[2]))
    saves[-1].start()
    back, d_gain = norm_back(x[...], gain_a[...], summed.T)
    d_gain_a[...] = d_gain
    grad_in[...] += back
    for made in go_copies:
        for copy in made[:-1]:
            copy.wait_send()
    for copy in sent:
        copy.wait_send()
    for save in saves:
        save.wait()


def layer_backward(lengths, grad, x, gain_a, gain_f, kept, w_attn, w_ffn, w_down, collective_id):
    size, each = lax.axis_size("ctx"), heads_each()
    count, model = x.shape
    wide = w_down.shape[0]
    group = count * size
    rows = each * size * HEAD_DIM
    f32, bf16 = jnp.float32, jnp.bfloat16
    made = lambda shape, dtype: jax.ShapeDtypeStruct(shape, dtype)
    return pl.pallas_call(
        layer_backward_kernel,
        out_shape=[made((count, model), f32), made((1, model), f32), made((1, model), f32),
                   made(w_attn.shape, bf16), made(w_ffn.shape, bf16), made(w_down.shape, bf16)],
        in_specs=[SMEM] + [VMEM] * 12 + [ANY] * 3,
        out_specs=[VMEM] * 3 + [ANY] * 3,
        scratch_shapes=[
            pltpu.VMEM(w_attn.shape, bf16), pltpu.VMEM(w_ffn.shape, bf16), pltpu.VMEM(w_down.shape, bf16),
            pltpu.VMEM(w_attn.shape, bf16), pltpu.VMEM(w_ffn.shape, bf16), pltpu.VMEM(w_down.shape, bf16),
            pltpu.VMEM((1, rows, count), bf16), pltpu.VMEM((1, each * HEAD_DIM, group), bf16),
            pltpu.VMEM((3, rows, count), bf16), pltpu.VMEM((each, size - 1, HEAD_DIM, count), bf16),
            pltpu.VMEM((each, 2, HEAD_DIM, group), bf16), pltpu.VMEM((group, count), jnp.int32),
            pltpu.VMEM((count, model), f32), pltpu.VMEM((count, model), bf16), pltpu.VMEM((count, model), bf16),
            pltpu.SemaphoreType.DMA((2, each, size - 1)), pltpu.SemaphoreType.DMA((2, each, size - 1)),
            pltpu.SemaphoreType.DMA((2, each, size - 1)), pltpu.SemaphoreType.DMA((each,)),
            pltpu.SemaphoreType.DMA((3,)), pltpu.SemaphoreType.DMA((3,))],
        compiler_params=pltpu.CompilerParams(collective_id=collective_id, has_side_effects=True, vmem_limit_bytes=60 << 20),
        name="layer_backward",
    )(lengths, grad, x, gain_a, gain_f, *kept, w_attn, w_ffn, w_down)


CONV = 4
BLOCKS = (1, 2, 3, 4)
HALO = 64


def halves_of(v):
    high = low(v)
    return high, low(v - high.astype(jnp.float32))


def dot_split(a, b):
    high, rest = halves_of(a)
    return dot(high, b) + dot(rest, b)


def dot_wide(a, b):
    (ah, al), (bh, bl) = halves_of(a), halves_of(b)
    return dot(ah, bh) + dot(ah, bl) + dot(al, bh)


def block_starts(places, ends):
    start = jnp.zeros(places.shape, jnp.int32)
    for end in ends:
        start = jnp.where(places >= end, end, start)
    rel = places - start
    found = []
    for size in BLOCKS:
        if size & (size - 1) == 0:
            found.append(places - (rel & (size - 1)))
        else:
            count = jnp.floor((rel.astype(jnp.float32) + 0.5) * (1.0 / size)).astype(jnp.int32)
            found.append(start + count * size)
    return found


def valid_of(places, ends):
    return (places >= 0) & (places < ends[-1])


def tap_ids(ids, first, span, ends):
    places = first - HALO + lax.broadcasted_iota(jnp.int32, (1, span), 1)
    own = segments(places, ends)
    count = ids.shape[1] // 3
    rows = []
    for tap in range(CONV):
        theirs = places + (tap - 1)
        at = count - HALO + tap - 1
        near = ids[:, at - at % 128:at - at % 128 + span + 128]
        near = lax.slice_in_dim(near, at % 128, at % 128 + span, axis=1)
        use = valid_of(places, ends) & valid_of(theirs, ends) & (segments(theirs, ends) == own)
        rows.append(jnp.where(use, near, -1))
    return rows, valid_of(places, ends)


def one_hot(row, vocab):
    return low(jnp.where(lax.broadcasted_iota(jnp.int32, (vocab, row.shape[1]), 0) == row, 1.0, 0.0))


def mix_blocks(first, span, tokens, ends):
    keys = block_starts(first - HALO + lax.broadcasted_iota(jnp.int32, (span, tokens), 0), ends)
    found = []
    for parity in range(2):
        own = block_starts(first + 2 * lax.broadcasted_iota(jnp.int32, (1, tokens), 1) + parity, ends)
        found.append([key == mine for key, mine in zip(keys, own)])
    return found


def gbst_forward(ends, ids, first, small, conv, choice, vocab, tokens, tick=lambda: None):
    span = conv.shape[1]
    taps, valid = tap_ids(ids, first, span, ends)
    table = small[:, :vocab]
    at = vocab + CONV
    total = small[:, at:at + 1] * jnp.where(valid, 1.0, 0.0)
    for tap in range(CONV):
        total = total + dot_split(table * small[:, vocab + tap:vocab + tap + 1], one_hot(taps[tap], vocab))
        tick()
    conv[...] = total
    scored = jnp.sum(total * small[:, at + 1:at + 2], 0, keepdims=True)
    scored = jnp.broadcast_to(scored, (8, span))
    parts = []
    for _ in range(3):
        parts.append(low(scored))
        scored = scored - parts[-1].astype(jnp.float32)
    mix = jnp.zeros((span, tokens), jnp.float32)
    for parity, blocks in enumerate(mix_blocks(first, span, tokens, ends)):
        logits = []
        for size, block in zip(BLOCKS, blocks):
            ones = low(jnp.where(block, 1.0, 0.0))
            logits.append((dot(parts[0], ones) + dot(parts[1], ones) + dot(parts[2], ones))[:1] * (1.0 / size))
        top = functools.reduce(jnp.maximum, logits)
        raised = [jnp.exp(v - top) for v in logits]
        whole = functools.reduce(jnp.add, raised)
        for i, (size, block) in enumerate(zip(BLOCKS, blocks)):
            chosen = raised[i] / whole
            choice[len(BLOCKS) * parity + i:len(BLOCKS) * parity + i + 1, :] = chosen
            mix = mix + jnp.where(block, chosen * (0.5 / size), 0.0)
        tick()
    return dot_wide(total, mix)


def gbst_backward(ends, ids, first, small, conv, choice, grad_t, vocab, out, tick=lambda: None):
    span, tokens = conv.shape[1], grad_t.shape[1]
    taps, valid = tap_ids(ids, first, span, ends)
    at = vocab + CONV
    total = conv[...]
    along = dot_wide(total.T, grad_t)
    mix = jnp.zeros((span, tokens), jnp.float32)
    scored = jnp.zeros((span, tokens), jnp.float32)
    for parity, blocks in enumerate(mix_blocks(first, span, tokens, ends)):
        chosen = [choice[len(BLOCKS) * parity + i:len(BLOCKS) * parity + i + 1, :] for i in range(len(BLOCKS))]
        grads = [jnp.sum(jnp.where(block, along, 0.0), 0, keepdims=True) * (0.5 / size) for size, block in zip(BLOCKS, blocks)]
        inner = functools.reduce(jnp.add, [c * g for c, g in zip(chosen, grads)])
        for i, (size, block) in enumerate(zip(BLOCKS, blocks)):
            mix = mix + jnp.where(block, chosen[i] * (0.5 / size), 0.0)
            scored = scored + jnp.where(block, chosen[i] * (grads[i] - inner) * (1.0 / size), 0.0)
    g_scored = jnp.sum(scored.T, 0, keepdims=True)
    g_conv = dot_wide(grad_t, mix.T) + small[:, at + 1:at + 2] * g_scored
    out[:, at + 1:at + 2] = jnp.sum(total * g_scored, 1, keepdims=True)
    g_conv = g_conv * jnp.where(valid, 1.0, 0.0)
    out[:, at:at + 1] = jnp.sum(g_conv, 1, keepdims=True)
    high, rest = halves_of(g_conv)
    table = small[:, :vocab]
    g_table = jnp.zeros(table.shape, jnp.float32)
    for tap in range(CONV):
        hot = one_hot(taps[tap], vocab)
        g_tap = dot_nt(high, hot) + dot_nt(rest, hot)
        g_table = g_table + g_tap * small[:, vocab + tap:vocab + tap + 1]
        out[:, vocab + tap:vocab + tap + 1] = jnp.sum(g_tap * table, 1, keepdims=True)
        tick()
    out[:, :vocab] = g_table


def gbst_forward_kernel(vocab, tokens, lengths, ids, small, out, conv, choice):
    ends = ends_of(lengths)
    first = lax.axis_index("ctx") * 2 * tokens
    out[...] = gbst_forward(ends, ids, first, small, conv, choice, vocab, tokens).T


def gbst_backward_kernel(vocab, lengths, ids, small, conv, choice, grad, out):
    ends = ends_of(lengths)
    first = lax.axis_index("ctx") * 2 * grad.shape[0]
    out[...] = jnp.zeros(out.shape, jnp.float32)
    gbst_backward(ends, ids, first, small, conv, choice, grad[...].T, vocab, out)


class Gather(Sender):
    phases = 4

    def __init__(self, sources, out, sems, local_sems, first=0, width=None):
        super().__init__(sems)
        self.out = out
        self.columns = pl.ds(first, width or out.shape[-1])
        self.pieces = pieces_of(self.columns.size, THIRD, first)
        self.waiting = []
        self.own = []
        for i, (source, at) in enumerate(sources):
            a, b = max(first, at), min(first + (width or out.shape[-1]), at + source.shape[-1])
            if a < b:
                there = out.at[place_of() + (slice(None), pl.ds(a, b - a))]
                copy = pltpu.make_async_copy(source.at[:, pl.ds(a - at, b - a)], there, local_sems.at[i])
                copy.start()
                self.own.append(copy)

    def stage(self, number):
        place = place_of()
        self.arrive()
        if number == 0:
            for copy in self.own:
                copy.wait()
        if number < 3:
            for columns, order in self.pieces:
                have = order[:number]
                where = tuple(slice(None) if axis in have else place[axis] for axis in range(4)) + (slice(None), columns)
                for _, target in along(order[number]):
                    self.waiting.append(self.send(self.out.at[where], self.out.at[where], target))
        else:
            where = (slice(None), place[1]) + (slice(None),) * 3 + (self.columns,)
            self.waiting.append(self.send(self.out.at[where], self.out.at[where], sibling()))

    def arrive(self):
        for copy in self.waiting:
            copy.wait_recv()
        self.waiting = []


class GatherHeads(Sender):
    phases = 3

    def __init__(self, shard, out, sems, local_sem):
        super().__init__(sems)
        self.shard, self.out = shard, out
        self.waiting = []
        self.own = pltpu.make_async_copy(shard.at[lax.axis_index("ctx")], out.at[place_of()], local_sem)
        self.own.start()

    def stage(self, number):
        z, core, y, x = place_of()
        self.arrive()
        if number == 0:
            for p in others()[:-1]:
                target = (lax.axis_index("dp"), p)
                self.waiting.append(self.send(self.shard.at[p], self.out.at[z, core, y, x], target))
        elif number == 1:
            self.own.wait()
            for _, target in along(0):
                self.waiting.append(self.send(self.out.at[z, core], self.out.at[z, core], target))
        else:
            where = (slice(None), core)
            self.waiting.append(self.send(self.out.at[where], self.out.at[where], sibling()))

    arrive = Gather.arrive


class Ticker:
    def __init__(self):
        self.chunks, self.steps = [], []

    def pipeline(self, chunks):
        self.chunks = chunks
        self.done = [0] * len(chunks)
        for t in range(len(chunks) + 4 * DEPTH):
            for number in (0, 3, 2, 1):
                i = t - DEPTH * number
                if 0 <= i < len(chunks) and number < chunks[i].phases:
                    self.steps.append((i, number))

    def tick(self, count=1):
        for _ in range(count):
            if self.steps:
                i, number = self.steps.pop(0)
                self.chunks[i].stage(number)
                self.done[i] = number + 1

    def need(self, i):
        while self.done[i] < self.chunks[i].phases:
            self.tick()
        self.chunks[i].arrive()


class Scatter(Sender):
    phases = 5

    def __init__(self, parts, emit, scratch, sems, local_sem, before=None, credit=None, final=True, first=0):
        super().__init__(sems)
        self.parts, self.emit, self.local_sem, self.first = parts, emit, local_sem, first
        self.held, self.across, *landing = scratch
        self.pieces = [(columns, order[::-1], landing[3 * i:3 * i + 3])
                       for i, (columns, order) in enumerate(pieces_of(self.held.shape[-1], THIRD))]
        self.waiting, self.before, self.credit, self.final = [], before, credit, final

    @staticmethod
    def scratch(shape, dtype):
        sizes = dict(zip((0, 2, 3), grid_of()))
        whole = (*sizes.values(), *shape)
        found = [whole, whole]
        for columns, order in pieces_of(shape[-1], THIRD):
            order = order[::-1]
            for number in range(3):
                rest = [sizes[a] for a in sizes if a in order[number + 1:]]
                found.append((sizes[order[number]] - 1, *rest, shape[0], columns.size))
        return [pltpu.VMEM(s, dtype) for s in found]

    def targets(self):
        return [target for axis in (0, 2, 3) for _, target in along(axis)] + [sibling()]

    def open(self):
        if self.before is not None:
            self.before.finish()
            pl.semaphore_wait(self.credit, len(self.targets()))

    def close(self):
        if not self.final:
            for target in self.targets():
                pl.semaphore_signal(self.credit, inc=1, device_id=target, device_id_type=MESH)

    arrive = Gather.arrive

    def stage(self, number):
        place = place_of()
        sizes = dict(zip((0, 2, 3), grid_of()))
        self.arrive()
        if number == 0:
            self.open()
            columns = (slice(None),) * 3 + (pl.ds(self.first, self.held.shape[-1]),)
            self.own = pltpu.make_async_copy(self.parts.at[(slice(None), place[1]) + columns], self.held, self.local_sem)
            self.own.start()
            self.waiting.append(self.send(self.parts.at[(slice(None), 1 - place[1]) + columns], self.across, sibling()))
            return
        if number == 1:
            self.own.wait()
            add_into(self.held, self.across, list(sizes.values()))
        for columns, order, landing in self.pieces:
            if number > 1:
                mine = order[:number - 1]
                where = tuple(place[a] if a in mine else slice(None) for a in sizes) + (slice(None), columns)
                lead = [sizes[a] for a in sizes if a not in mine]
                landed = landing[number - 2]
                if number < 4:
                    for i in range(landed.shape[0]):
                        add_into(self.held.at[where], landed.at[i], lead)
                else:
                    total = self.held[where].astype(jnp.float32)
                    for i in range(landed.shape[0]):
                        total = total + landed[i].astype(jnp.float32)
                    self.emit(pl.ds(self.first + columns.start, columns.size), total)
            if number < 4:
                axis, mine = order[number - 1], order[:number - 1]
                for i, (there, target) in enumerate(along(axis)):
                    where = tuple(there if a == axis else place[a] if a in mine else slice(None) for a in sizes)
                    src = self.held.at[where + (slice(None), columns)]
                    self.waiting.append(self.send(src, landing[number - 1].at[i], target))
        if number == 4:
            self.close()


class ScatterHeads(Scatter):
    phases = 4

    def __init__(self, parts, out, scratch, sems, local_sem, before=None, credit=None, final=True):
        Sender.__init__(self, sems)
        self.parts, self.out, self.local_sem = parts, out, local_sem
        self.across, self.landed, self.sums = scratch
        self.waiting, self.before, self.credit, self.final = [], before, credit, final

    def targets(self):
        return [target for _, target in along(0)] + [sibling()]

    def stage(self, number):
        nz, ny, nx = grid_of()
        z, core, y, x = place_of()
        me = lax.axis_index("ctx")
        self.arrive()
        if number == 0:
            if self.before is not None:
                pl.semaphore_wait(self.credit, len(self.targets()))
            self.waiting.append(self.send(self.parts.at[:, 1 - core], self.across, sibling()))
        elif number == 1:
            add_into(self.parts.at[:, core], self.across, [nz, ny, nx])
            for i, (there, target) in enumerate(along(0)):
                self.waiting.append(self.send(self.parts.at[there, core], self.landed.at[i], target))
        elif number == 2:
            for j in range(ny):
                for k in range(nx):
                    total = self.parts[z, core, j, k].astype(jnp.float32)
                    for i in range(nz - 1):
                        total = total + self.landed[i, j, k].astype(jnp.float32)
                    self.sums[j * nx + k] = total
            self.close()
            for p in others()[:-1]:
                self.waiting.append(self.send(self.sums.at[p], self.out.at[me], (lax.axis_index("dp"), p)))
            self.own = pltpu.make_async_copy(self.sums.at[me], self.out.at[me], self.local_sem)
            self.own.start()

    def finish(self):
        self.arrive()
        for copy in self.flying:
            copy.wait_send()
        self.flying = []
        if self.own is not None:
            self.own.wait()
        self.own = None


class Rota:
    def __init__(self):
        self.queue = []

    def add(self, chunk):
        chunk.stage(0)
        self.queue.append([chunk, 1])

    def tick(self, count=1):
        for _ in range(count):
            if not self.queue:
                return
            item = self.queue.pop(0)
            item[0].stage(item[1])
            item[1] += 1
            if item[1] < item[0].phases:
                self.queue.append(item)

    def close(self, chunk):
        while any(item[0] is chunk for item in self.queue):
            self.tick()


def run_kernel(body, inputs, outputs, scratch, collective_id, name):
    def leaves(value):
        return [v for part in value for v in leaves(part)] if isinstance(value, list) else [value]

    def again(value, refs):
        return [again(v, refs) for v in value] if isinstance(value, list) else next(refs)

    def flat(group):
        return leaves(list(group.values()))

    def rebuilt(group, refs):
        return {k: again(value, refs) for k, value in group.items()}

    def kernel(*refs):
        refs = iter(refs)
        body(types.SimpleNamespace(**rebuilt(inputs, refs), **rebuilt(outputs, refs), **rebuilt(scratch, refs)))
    found = pl.pallas_call(
        kernel,
        out_shape=[s for s, _ in flat(outputs)],
        in_specs=[s for _, s in flat(inputs)],
        out_specs=[s for _, s in flat(outputs)],
        scratch_shapes=flat(scratch),
        compiler_params=pltpu.CompilerParams(collective_id=collective_id, has_side_effects=True, vmem_limit_bytes=60 << 20),
        name=name,
    )(*[a for a, _ in flat(inputs)])
    return types.SimpleNamespace(**rebuilt(outputs, iter(found)))


class Keep:
    def __init__(self, sems):
        self.sems, self.count, self.flying = sems, 0, []

    def __call__(self, src, dst):
        copy = pltpu.make_async_copy(src, dst, self.sems.at[self.count])
        copy.start()
        self.count += 1
        self.flying.append(copy)
        return copy

    def finish(self):
        for copy in self.flying:
            copy.wait()


def unpack(blocks, dst):
    nz, cores, ny, nx, rows, width = blocks.shape
    each = ny * nx * rows
    part = next(p for p in (512, 256, 128) if width % p == 0)

    def body(i, carry):
        for c in range(width // part):
            columns = slice(c * part, (c + 1) * part)
            found = [blocks[i // cores, i % cores, y, x, :, columns].astype(jnp.float32) for y in range(ny) for x in range(nx)]
            dst[pl.ds(pl.multiple_of(i * each, each), each), columns] = low(jnp.concatenate(found, 0))
        return carry
    lax.fori_loop(0, nz * cores, body, 0)


def to_blocks(dst, columns, values):
    nz, cores, ny, nx, rows, _ = dst.shape
    for b in range(nz * cores * ny * nx):
        g, k = divmod(b, ny * nx)
        dst[g // cores, g % cores, k // nx, k % nx, :, columns] = low(values[b * rows:(b + 1) * rows])


def norm_back(values, gain, upstream):
    scale = inverse_rms(values)
    scaled = upstream * gain
    mean = jnp.mean(values * scaled, -1, keepdims=True)
    return scale * scaled - values * (scale * scale * scale * mean), jnp.sum(upstream * values * scale, 0, keepdims=True)


def from_slot(i):
    size, me = lax.axis_size("ctx"), lax.axis_index("ctx")
    return lax.rem(me + size - 1 - i, size)


def gain_rows(small, vocab, layers):
    at = vocab + CONV + 2
    rows = small[:, at // LANES * LANES:].T
    at = at % LANES
    return [rows[at + l:at + l + 1, :] for l in range(2 * layers)]


def forward_body(vocab, layers, r):
    ends = ends_of(r.lengths)
    size, me = lax.axis_size("ctx"), lax.axis_index("ctx")
    each = heads_each()
    base = each * HEAD_DIM
    keep = Keep(r.keep_sems)
    greet_all()
    ids, count = r.ids, r.byte_ids.shape[1]
    near = []
    for i, (there, at) in enumerate(((lax.rem(me + 1, size), 0), (lax.rem(me + size - 1, size), 2))):
        copy = to_group(r.byte_ids, ids.at[:, pl.ds(at * count, count)], r.ids_sems, (i,), there)
        copy.start()
        near.append(copy)
    ids[:, count:2 * count] = r.byte_ids[...]
    chunks = [Gather([(r.small, 0)], r.full_small, r.small_sems, r.local_sems.at[0])]
    model = r.encoded.shape[1]
    wide = r.gate_w.shape[2]
    for l in range(layers):
        chunks.append(GatherHeads(r.heads_w.at[l], r.full_heads[l], r.heads_sems.at[l], r.more_sems.at[l, 1]))
        sources = [(r.gate_w.at[l], 0), (r.up_w.at[l], wide), (r.out_w.at[l], 2 * wide)]
        for k, (at, part) in enumerate(splits_of(r.full_ffn[l].shape[-1], SPLIT)):
            chunks.append(Gather(sources, r.full_ffn[l], r.ffn_sems.at[l, k], r.local_sems.at[1 + l * SPLIT + k], at, part))
        chunks.append(Gather([(r.down_w.at[l], 0)], r.full_down[l], r.down_sems.at[l], r.more_sems.at[l]))
    ticker = Ticker()
    ticker.pipeline(chunks)
    tick = ticker.tick
    tick(2)
    tokens = count // 2
    seg_all = r.seg_all
    seg_all[...] = segments(2 * lax.broadcasted_iota(jnp.int32, seg_all.shape, 0), ends)
    for copy in near:
        copy.wait_recv()
    ticker.need(0)
    small = r.small_wide
    nz, cores, ny, nx, rows, _ = r.full_small.shape
    for b in range(nz * cores * ny * nx):
        place = (b // (cores * ny * nx), b // (ny * nx) % cores, b // nx % ny, b % nx)
        small[b * rows:(b + 1) * rows, :] = r.full_small[place].astype(jnp.float32)
    tick()
    stream = gbst_forward(ends, ids[...], me * count, small[...], r.conv, r.choice, vocab, tokens, tick).T
    gains = gain_rows(small, vocab, layers)
    keep(r.conv, r.out_conv)
    for l in range(layers):
        base_chunk = 1 + (2 + SPLIT) * l
        nrm, qkv, att = r.nrm[l], r.qkv[l], r.att[l]
        r.x[l][...] = stream
        r.mine[...] = flip(low(stream * inverse_rms(stream) * gains[l]))
        spread = []
        for i, p in enumerate(others()[:-1]):
            copy = to_group(r.mine, nrm.at[:, tokens_of(me, tokens)], r.nrm_sems.at[l], (i,), p)
            copy.start()
            spread.append(copy)
        nrm[:, tokens_of(me, tokens)] = r.mine[...]
        keep(r.x[l], r.out_x[l])
        ticker.need(base_chunk)
        unpack(r.full_heads[l], r.w_heads[l])
        keep(r.w_heads[l], r.out_w_heads[l])
        r.w_turned[...] = flip(r.w_heads[l][...])
        for i in range(-1, size - 1):
            if i >= 0:
                spread[i].wait_recv()
            theirs = tokens_of(me if i < 0 else from_slot(i), tokens)
            qkv[:, theirs] = low(dot(r.w_turned[...], nrm[:, theirs]))
            tick()
        keep(nrm, r.out_nrm[l])
        keep(qkv, r.out_qkv[l])
        copies = []
        for h in range(each):
            query = pl.ds(h * HEAD_DIM, HEAD_DIM)
            key = flip(qkv[base + h * HEAD_DIM:base + (h + 1) * HEAD_DIM, :])
            value_t = qkv[2 * base + h * HEAD_DIM:2 * base + (h + 1) * HEAD_DIM, :]
            rows = pl.ds(pl.multiple_of((me * each + h) * HEAD_DIM, HEAD_DIM), HEAD_DIM)
            for i, p in enumerate(others()):
                theirs = tokens_of(p, tokens)
                seg_q = segments(2 * (p * tokens + lax.broadcasted_iota(jnp.int32, (1, tokens), 1)), ends)
                scores = jnp.where(seg_all[...] == seg_q, dot(key, qkv[query, theirs]), NEG_FILL)
                top = jnp.max(scores, 0, keepdims=True)
                probs = jnp.exp(scores - top)
                total = jnp.sum(probs, 0, keepdims=True)
                r.lse[l][h, :, theirs] = top + jnp.log(total)
                result = low(dot(value_t, low(probs)) / total)
                if i == size - 1:
                    att[rows, :] = result
                else:
                    r.att_send[h, i] = result
                    copy = to_group(r.att_send.at[h, i], att.at[rows], r.att_sems.at[l], (h, i), p)
                    copy.start()
                    copies.append(copy)
                tick()
        keep(r.lse[l], r.out_lse[l])
        for k in range(SPLIT):
            ticker.need(base_chunk + 1 + k)
        load = pltpu.make_async_copy(r.full_ffn[l], r.blocks, r.load_sems.at[l, 0])
        load.start()
        for copy in copies:
            copy.wait_recv()
        keep(att, r.out_att[l])
        load.wait()
        unpack(r.blocks, r.w_ffn)
        mid = stream + dot(flip(att[...]), r.w_ffn[:, 2 * wide:])
        r.middle[l][...] = mid
        after = low(mid * inverse_rms(mid) * gains[layers + l])
        r.nffn[...] = after
        r.nffn_t[l][...] = flip(after)
        r.total[...] = mid
        keep(r.middle[l], r.out_middle[l])
        keep(r.nffn_t[l], r.out_nffn_t[l])
        ticker.need(base_chunk + 1 + SPLIT)
        load = pltpu.make_async_copy(r.full_down[l], r.w_down, r.load_sems.at[l, 1])
        load.start()
        load.wait()
        part = wide // (nz * cores)

        def step(c, carry):
            columns = pl.ds(pl.multiple_of(c * part, part), part)
            gate = dot(r.nffn[...], r.w_ffn[:, columns])
            up = dot(r.nffn[...], r.w_ffn[:, pl.ds(pl.multiple_of(wide + c * part, part), part)])
            hidden = low(gelu_parts(gate)[0] * up)
            r.total[...] += dot(hidden, r.w_down[c // cores, c % cores].reshape(part, model))
            return carry
        half = nz * cores // 2
        lax.fori_loop(0, half, step, 0)
        tick(2)
        lax.fori_loop(half, nz * cores, step, 0)
        stream = r.total[...]
        for copy in spread + copies:
            copy.wait_send()
    r.encoded[...] = low(stream)
    for copy in near:
        copy.wait_send()
    for i, chunk in enumerate(chunks):
        ticker.need(i)
        chunk.finish()
    keep.finish()


def like(shape, dtype):
    return jax.ShapeDtypeStruct(shape, dtype)


def kept_shapes(tokens, model):
    size, each = lax.axis_size("ctx"), heads_each()
    f32, bf16 = jnp.float32, jnp.bfloat16
    turned = -(-3 * each * HEAD_DIM // LANES) * LANES
    return dict(x=((tokens, model), f32), middle=((tokens, model), f32), nrm=((model, tokens * size), bf16),
                qkv=((turned, tokens * size), bf16), lse=((each, 1, tokens * size), f32),
                att=((each * size * HEAD_DIM, tokens), bf16), nffn_t=((model, tokens), bf16))


def forward_pass(lengths, byte_ids, small, heads_w, out_w, gate_w, up_w, down_w, vocab):
    nz, ny, nx = grid_of()
    size, each = lax.axis_size("ctx"), heads_each()
    layers, _, model = out_w.shape
    wide = gate_w.shape[2]
    tokens = byte_ids.shape[1] // 2
    span = byte_ids.shape[1] + 2 * HALO
    f32, bf16 = jnp.float32, jnp.bfloat16
    dma, vmem = pltpu.SemaphoreType.DMA, pltpu.VMEM
    blocks = lambda rows, width: (nz, CORES, ny, nx, rows, width)
    shapes = kept_shapes(tokens, model)
    per_layer = lambda made: [made] * layers
    ffn = blocks(gate_w.shape[1], 2 * wide + model)
    down = blocks(*down_w.shape[1:])
    heads = blocks(*heads_w.shape[2:])
    inputs = dict(lengths=(lengths, SMEM), byte_ids=(byte_ids, VMEM), small=(small, ANY), heads_w=(heads_w, ANY),
                  out_w=(out_w, ANY), gate_w=(gate_w, ANY), up_w=(up_w, ANY), down_w=(down_w, ANY))
    outputs = dict(
        encoded=(like((tokens, model), bf16), VMEM), small_wide=(like((model, small.shape[1]), f32), VMEM),
        ids=(like((1, 3 * byte_ids.shape[1]), jnp.int32), VMEM), choice=(like((2 * len(BLOCKS), tokens), f32), VMEM),
        out_conv=(like((model, span), f32), ANY), full_ffn=per_layer((like(ffn, bf16), ANY)),
        full_down=per_layer((like(down, bf16), ANY)), out_w_heads=per_layer((like((model, heads[-1]), bf16), ANY)),
        out_x=per_layer((like(*shapes["x"]), ANY)), out_middle=per_layer((like(*shapes["middle"]), ANY)),
        out_nrm=per_layer((like(*shapes["nrm"]), ANY)), out_qkv=per_layer((like(*shapes["qkv"]), ANY)),
        out_lse=per_layer((like(*shapes["lse"]), ANY)), out_att=per_layer((like(*shapes["att"]), ANY)),
        out_nffn_t=per_layer((like(*shapes["nffn_t"]), ANY)))
    scratch = {k: per_layer(vmem(*v)) for k, v in shapes.items()}
    scratch.update(
        full_small=vmem(blocks(*small.shape), bf16), conv=vmem((model, span), f32), full_heads=per_layer(vmem(heads, bf16)),
        w_heads=per_layer(vmem((model, heads[-1]), bf16)), w_turned=vmem((heads[-1], model), bf16), w_ffn=vmem((model, ffn[-1]), bf16),
        w_down=vmem(down, bf16), blocks=vmem(ffn, bf16), mine=vmem((model, tokens), bf16),
        att_send=vmem((each, size - 1, HEAD_DIM, tokens), bf16), seg_all=vmem((tokens * size, tokens), jnp.int32),
        nffn=vmem((tokens, model), bf16), total=vmem((tokens, model), f32),
        keep_sems=dma((1 + 8 * layers,)), ids_sems=dma((2, 2)), local_sems=dma((1 + layers * SPLIT, 3)), more_sems=dma((layers, 2)),
        load_sems=dma((layers, 2)), nrm_sems=dma((layers, 2, size - 1)), att_sems=dma((layers, 2, each, size - 1)),
        small_sems=dma((2, hops(small.shape[1], THIRD))), heads_sems=dma((layers, 2, size + nz - 1)),
        ffn_sems=dma((layers, SPLIT, 2, hops(ffn[-1], THIRD))), down_sems=dma((layers, 2, hops(model, THIRD))))
    return run_kernel(functools.partial(forward_body, vocab, layers), inputs, outputs, scratch, 4, "forward_pass")


def backward_body(vocab, layers, r):
    ends = ends_of(r.lengths)
    size, me = lax.axis_size("ctx"), lax.axis_index("ctx")
    each = heads_each()
    base = each * HEAD_DIM
    tokens, model = r.out_grad.shape
    wide = r.w_down.shape[0]
    nz, cores, ny, nx, rows, _ = r.block_ffn.shape[1:]
    part = wide // (nz * cores)
    loads = {}

    def load(key, src, dst, sem):
        loads[key] = pltpu.make_async_copy(src, dst, sem)
        loads[key].start()

    def load_ffn(l):
        sems = r.load_sems.at[l]
        load(0, r.in_nffn_t[l], r.nffn_t, sems.at[0])
        load(1, r.in_w_down[l], r.w_down, sems.at[1])
        load(2, r.in_w_ffn[l], r.w_ffn, sems.at[2])
        load(3, r.in_middle[l], r.middle, sems.at[3])
        load(4, r.in_att[l], r.att, sems.at[4])

    def load_attention(l):
        sems = r.load_sems.at[l]
        load(5, r.in_qkv[l], r.qkv, sems.at[5])
        load(6, r.in_lse[l], r.lse, sems.at[6])
        load(7, r.in_w_heads[l], r.w_heads, sems.at[7])
        load(8, r.in_nrm[l], r.nrm, sems.at[8])
        load(9, r.in_x[l], r.x, sems.at[9])
    load_ffn(layers - 1)
    load_attention(layers - 1)
    greet_all()
    gains = gain_rows(r.small_wide, vocab, layers)
    d_gains = [None] * (2 * layers)
    seg_all = r.seg_all
    seg_all[...] = segments(2 * lax.broadcasted_iota(jnp.int32, seg_all.shape, 0), ends)
    r.dqkv[...] = jnp.zeros(r.dqkv.shape, jnp.bfloat16)
    r.grad[...] = r.out_grad[...].astype(jnp.float32)
    rota = Rota()
    tick = rota.tick
    before = [None] * (2 + SPLIT)
    made = []

    def begin(kind, chunk):
        made.append(chunk)
        before[kind] = chunk
        rota.add(chunk)
    for l in reversed(range(layers)):
        r.grad_low[...] = low(r.grad[...])
        r.total[...] = jnp.zeros(r.total.shape, jnp.float32)
        for key in range(3):
            loads[key].wait()
        r.nffn[...] = flip(r.nffn_t[...])

        def saves(c, slot):
            sems = r.save_sems.at[slot]
            columns = pl.ds(pl.multiple_of(c * part, part), part)
            later = pl.ds(pl.multiple_of(wide + c * part, part), part)
            where = (slice(None),) * 5
            return [pltpu.make_async_copy(r.block_down.at[slot], r.parts_down[l].at[c // cores, c % cores], sems.at[0]),
                    pltpu.make_async_copy(r.block_ffn.at[slot, :, :, :, :, :, pl.ds(0, part)], r.parts_ffn[l].at[where + (columns,)], sems.at[1]),
                    pltpu.make_async_copy(r.block_ffn.at[slot, :, :, :, :, :, pl.ds(part, part)], r.parts_ffn[l].at[where + (later,)], sems.at[2])]

        def step(c, carry):
            columns = pl.ds(pl.multiple_of(c * part, part), part)
            later = pl.ds(pl.multiple_of(wide + c * part, part), part)
            slot = lax.rem(c, 2)

            @pl.when(c >= 2)
            def _():
                for copy in saves(c - 2, slot):
                    copy.wait()
            gate = dot(r.nffn[...], r.w_ffn[:, columns])
            up = dot(r.nffn[...], r.w_ffn[:, later])
            g_hidden = dot_nt(r.grad_low[...], r.w_down[columns, :])
            act, slope = gelu_parts(gate)
            g_gate = low(g_hidden * up * slope)
            g_up = low(g_hidden * act)
            d_down = low(dot(low((act * up).T), r.grad_low[...]))
            r.block_down[slot] = d_down.reshape(r.block_down.shape[1:])
            to_blocks(r.block_ffn.at[slot], slice(0, part), dot(r.nffn_t[...], g_gate))
            to_blocks(r.block_ffn.at[slot], slice(part, 2 * part), dot(r.nffn_t[...], g_up))
            for copy in saves(c, slot):
                copy.start()
            r.total[...] += dot_nt(g_gate, r.w_ffn[:, columns]) + dot_nt(g_up, r.w_ffn[:, later])
            return carry
        for c in range(0, nz * cores, 2):
            lax.fori_loop(c, c + 2, step, 0)
            tick()
        for c in (nz * cores - 2, nz * cores - 1):
            for copy in saves(c, c % 2):
                copy.wait()

        def emit_down(columns, total, l=l):
            r.d_down[l, :, columns] = total

        def emit_ffn(columns, total, l=l):
            first, last = columns.start, columns.start + columns.size
            for out, start in ((r.d_gate, 0), (r.d_up, wide), (r.d_out, 2 * wide)):
                a, b = max(first, start), min(last, start + out.shape[2])
                if a < b:
                    out[l, :, a - start:b - start] = total[:, a - first:b - first]
        if before[0] is not None:
            rota.close(before[0])
        begin(0, Scatter(r.parts_down[l], emit_down, r.down_scratch, r.down_sems.at[l], r.own_sems.at[l, 0], before[0], r.credits.at[0], l == 0))
        loads[3].wait()
        loads[4].wait()
        back, d_gains[layers + l] = norm_back(r.middle[...], gains[layers + l], r.total[...])
        r.grad[...] += back
        r.grad_low[...] = low(r.grad[...])
        r.go_all[0] = flip(dot_nt(r.grad_low[...], r.w_ffn[:, 2 * wide:]))
        go_copies = spread_heads(r.go_all, r.go, r.go_sems.at[l], r.go_own.at[l], each)
        to_blocks(r.block_out, slice(0, model), dot(r.att[...], r.grad_low[...]))
        save = pltpu.make_async_copy(r.block_out, r.parts_ffn[l].at[(slice(None),) * 5 + (pl.ds(2 * wide, model),)], r.own_sems.at[l, 3])
        save.start()
        save.wait()
        for k, (at, _) in enumerate(splits_of(r.parts_ffn[l].shape[-1], SPLIT)):
            if before[2 + k] is not None:
                rota.close(before[2 + k])
            begin(2 + k, Scatter(r.parts_ffn[l], emit_ffn, r.ffn_scratch[k], r.ffn_sems.at[l, k], r.ffn_own.at[l, k],
                                 before[2 + k], r.credits.at[2 + k], l == 0, at))
        if l:
            load_ffn(l - 1)
        for key in range(5, 8):
            loads[key].wait()
        for h in range(each):
            arrive(go_copies[h])
            rows_h = [slice(k * base + h * HEAD_DIM, k * base + (h + 1) * HEAD_DIM) for k in range(3)]
            key_t = r.qkv[rows_h[1], :]
            key, value = flip(key_t), flip(r.qkv[rows_h[2], :])
            g_key = jnp.zeros((HEAD_DIM, tokens * size), jnp.float32)
            g_value = jnp.zeros((HEAD_DIM, tokens * size), jnp.float32)
            for p in range(size):
                theirs = slice(p * tokens, (p + 1) * tokens)
                seg_q = segments(2 * (p * tokens + lax.broadcasted_iota(jnp.int32, (1, tokens), 1)), ends)
                query_t, go_t = r.qkv[rows_h[0], theirs], r.go[0, h * HEAD_DIM:(h + 1) * HEAD_DIM, theirs]
                scores = jnp.where(seg_all[...] == seg_q, dot(key, query_t), NEG_FILL)
                probs = jnp.exp(scores - r.lse[h, :, theirs])
                g_probs = dot(value, go_t)
                inner = jnp.sum(probs * g_probs, 0, keepdims=True)
                g_scores = low(probs * (g_probs - inner))
                r.dqkv[rows_h[0], theirs] = low(dot(key_t, g_scores))
                g_key = g_key + dot_nt(query_t, g_scores)
                g_value = g_value + dot_nt(go_t, low(probs))
                tick()
            r.dqkv[rows_h[1], :] = low(g_key)
            r.dqkv[rows_h[2], :] = low(g_value)
        spread = []
        for i, p in enumerate(others()):
            mine = dot(r.w_heads[...], r.dqkv[:, tokens_of(p, tokens)])
            if i == size - 1:
                r.summed[...] = mine
            else:
                r.sum_send[i] = low(mine)
                copy = to_group(r.sum_send.at[i], r.sum_land.at[i], r.sum_sems.at[l], (i,), p)
                copy.start()
                spread.append(copy)
        for key in (8, 9):
            loads[key].wait()
        if before[1] is not None:
            rota.close(before[1])
            before[1].finish()

        def heads_step(i, carry):
            each_rows = ny * nx * rows
            found = dot_nt(r.nrm[pl.ds(pl.multiple_of(i * each_rows, each_rows), each_rows), :], r.dqkv[...])
            for k in range(ny * nx):
                r.block_heads[i // cores, i % cores, k // nx, k % nx] = low(found[k * rows:(k + 1) * rows])
            return carry
        lax.fori_loop(0, nz * cores, heads_step, 0)
        begin(1, ScatterHeads(r.block_heads, r.d_heads[l], r.heads_scratch, r.heads_sems.at[l], r.own_sems.at[l, 2], before[1], r.credits.at[1], l == 0))
        tick()
        for i, copy in enumerate(spread):
            copy.wait_recv()
            r.summed[...] += r.sum_land[i].astype(jnp.float32)
        back, d_gains[l] = norm_back(r.x[...], gains[l], r.summed[...].T)
        r.grad[...] += back
        if l:
            load_attention(l - 1)
        for copies in go_copies:
            for copy in copies[:-1]:
                copy.wait_send()
        for copy in spread:
            copy.wait_send()
    out = r.small_grad
    out[...] = jnp.zeros(out.shape, jnp.float32)
    gbst_backward(ends, r.ids[...], me * 2 * tokens, r.small_wide[...], r.conv, r.choice, r.grad[...].T, vocab, out, tick)
    at = vocab + CONV + 2
    turned = jnp.concatenate(d_gains + [jnp.zeros((-2 * layers % 8, model), jnp.float32)], 0).T
    for i in range(2 * layers):
        out[:, at + i:at + i + 1] = turned[:, i:i + 1]
    to_blocks(r.block_small, slice(None), out[...])

    def emit_small(columns, total):
        r.d_small[:, columns] = total
    begin(0, Scatter(r.block_small, emit_small, r.small_scratch, r.small_sems, r.own_sems.at[layers, 0]))
    while rota.queue:
        tick()
    for chunk in made:
        chunk.finish()


def backward_pass(lengths, out_grad, fwd, vocab, heads_width):
    nz, ny, nx = grid_of()
    size, each = lax.axis_size("ctx"), heads_each()
    tokens, model = out_grad.shape
    layers = len(fwd.full_ffn)
    w_ffn = [w.reshape(-1, w.shape[-1]) for w in fwd.full_ffn]
    w_down = [w.reshape(-1, w.shape[-1]) for w in fwd.full_down]
    wide = w_down[0].shape[0]
    part = wide // (nz * CORES)
    f32, bf16 = jnp.float32, jnp.bfloat16
    dma, vmem = pltpu.SemaphoreType.DMA, pltpu.VMEM
    shapes = kept_shapes(tokens, model)
    per_layer = lambda found: [found] * layers
    ffn, down = fwd.full_ffn[0].shape, fwd.full_down[0].shape
    heads = ffn[:5] + (heads_width,)
    small = ffn[:5] + (fwd.small_wide.shape[1],)
    anywhere = lambda arrays: [(a, ANY) for a in arrays]
    inputs = dict(
        lengths=(lengths, SMEM), out_grad=(out_grad, VMEM), small_wide=(fwd.small_wide, VMEM), ids=(fwd.ids, VMEM),
        choice=(fwd.choice, VMEM), conv=(fwd.out_conv, VMEM), in_w_heads=anywhere(fwd.out_w_heads), in_w_ffn=anywhere(w_ffn),
        in_w_down=anywhere(w_down), in_x=anywhere(fwd.out_x), in_middle=anywhere(fwd.out_middle), in_nrm=anywhere(fwd.out_nrm),
        in_qkv=anywhere(fwd.out_qkv), in_lse=anywhere(fwd.out_lse), in_att=anywhere(fwd.out_att), in_nffn_t=anywhere(fwd.out_nffn_t))
    outputs = dict(
        d_small=(like(small[4:], f32), VMEM), d_heads=per_layer((like((size,) + heads[4:], f32), ANY)),
        d_gate=(like((layers, ffn[4], wide), f32), VMEM), d_up=(like((layers, ffn[4], wide), f32), VMEM),
        d_out=(like((layers, ffn[4], model), f32), VMEM), d_down=(like((layers,) + down[4:], f32), VMEM),
        parts_ffn=per_layer((like(ffn, bf16), ANY)), parts_down=per_layer((like(down, bf16), ANY)))
    scratch = {k: vmem(*v) for k, v in shapes.items()}
    scratch.update(
        grad=vmem((tokens, model), f32), total=vmem((tokens, model), f32), grad_low=vmem((tokens, model), bf16),
        nffn=vmem((tokens, model), bf16), w_heads=vmem((model, heads_width), bf16), w_ffn=vmem(w_ffn[0].shape, bf16),
        w_down=vmem(w_down[0].shape, bf16), block_ffn=vmem((2,) + ffn[:5] + (2 * part,), bf16), block_down=vmem((2,) + down[2:], bf16),
        block_out=vmem(ffn[:5] + (model,), bf16), block_heads=vmem(heads, bf16), block_small=vmem(small, bf16),
        go_all=vmem((1,) + shapes["att"][0], bf16), go=vmem((1, each * HEAD_DIM, tokens * size), bf16), dqkv=vmem(*shapes["qkv"]),
        summed=vmem((model, tokens), f32), sum_send=vmem((size - 1, model, tokens), bf16),
        sum_land=vmem((size - 1, model, tokens), bf16),
        seg_all=vmem((tokens * size, tokens), jnp.int32), small_grad=vmem(fwd.small_wide.shape, f32),
        down_scratch=Scatter.scratch(down[4:], bf16), ffn_scratch=[Scatter.scratch((ffn[4], w), bf16) for _, w in splits_of(ffn[-1], SPLIT)], ffn_own=dma((layers, SPLIT)),
        small_scratch=Scatter.scratch(small[4:], bf16),
        heads_scratch=[vmem((nz, ny, nx) + heads[4:], bf16), vmem((nz - 1, ny, nx) + heads[4:], bf16), vmem((size,) + heads[4:], f32)],
        load_sems=dma((layers, 10)), save_sems=dma((2, 3)), own_sems=dma((layers + 1, 4)), go_own=dma((layers, each)),
        go_sems=dma((layers, 2, each, size - 1)), sum_sems=dma((layers, 2, size - 1)), heads_sems=dma((layers, 2, size + nz - 1)),
        ffn_sems=dma((layers, SPLIT, 2, hops(ffn[-1], THIRD))), down_sems=dma((layers, 2, hops(model, THIRD))),
        small_sems=dma((2, hops(small[-1], THIRD))), credits=pltpu.SemaphoreType.REGULAR((2 + SPLIT,)))
    return run_kernel(functools.partial(backward_body, vocab, layers), inputs, outputs, scratch, 5, "backward_pass")


def packed_small(embed, conv_weight, conv_bias, scorer, norm_attn, norm_ffn):
    rows = jnp.concatenate([embed, conv_weight, conv_bias[None], scorer[None], norm_attn, norm_ffn], 0).T
    return jnp.pad(rows, ((0, 0), (0, -rows.shape[1] % 128)))


def split_small(rows, vocab, layers):
    at = vocab + CONV
    return (rows[:vocab], rows[vocab:at], rows[at], rows[at + 1], rows[at + 2 : at + 2 + layers],
            rows[at + 2 + layers : at + 2 + 2 * layers])


def separate_forward(lengths, byte_ids, shards, layer_count, vocab, model):
    ring, tokens = lax.axis_size("ctx"), byte_ids.shape[1] // 2
    up = [(i, (i + 1) % ring) for i in range(ring)]
    down = [(j, i) for i, j in up]
    ids = jnp.concatenate([lax.ppermute(byte_ids, "ctx", up), byte_ids, lax.ppermute(byte_ids, "ctx", down)], 1)
    small_full, *full = [a.reshape(-1, a.shape[-1]) for a in gather_all(shards, 0)]
    small_wide = small_full.astype(jnp.float32)
    gains = small_wide.T[vocab + CONV + 2 :]
    stream, conv, choice = pl.pallas_call(
        functools.partial(gbst_forward_kernel, vocab, tokens),
        out_shape=[
            jax.ShapeDtypeStruct((tokens, model), jnp.float32),
            jax.ShapeDtypeStruct((model, byte_ids.shape[1] + 2 * HALO), jnp.float32),
            jax.ShapeDtypeStruct((2 * len(BLOCKS), tokens), jnp.float32),
        ],
        in_specs=[SMEM, VMEM, VMEM],
        out_specs=[VMEM] * 3,
        compiler_params=pltpu.CompilerParams(vmem_limit_bytes=56 << 20),
        name="mix_bytes",
    )(lengths, ids, small_wide)
    kept = []
    for layer in range(layer_count):
        before = stream
        stream, *saved = layer_forward(
            lengths, stream, gains[layer][None], gains[layer_count + layer][None], *full[3 * layer : 3 * layer + 3], 2
        )
        kept.append((before, saved))
    return stream.astype(jnp.bfloat16), full, small_wide, ids, conv, choice, kept


def head_columns(query_w, key_w, value_w):
    layers, rows, model = query_w.shape
    size = lax.axis_size("ctx")
    found = [w.reshape(layers, rows, size, model // size).transpose(0, 2, 1, 3) for w in (query_w, key_w, value_w)]
    found = jnp.concatenate(found, 3)
    return jnp.pad(found, ((0, 0),) * 3 + ((0, -found.shape[3] % LANES),))


def fused_step(lengths, byte_ids, small, heads_w, out_w, gate_w, up_w, down_w, out_grad, vocab):
    fwd = forward_pass(lengths, byte_ids, small, heads_w, out_w, gate_w, up_w, down_w, vocab)
    back = backward_pass(lengths, out_grad, fwd, vocab, heads_w.shape[3])
    layers, rows, model = out_w.shape
    each = model // lax.axis_size("ctx")
    heads = jnp.stack(back.d_heads)
    columns = [heads[..., i * each : (i + 1) * each].transpose(0, 2, 1, 3).reshape(layers, rows, model) for i in range(3)]
    return fwd.encoded, back.d_small, (*columns, back.d_out, back.d_gate, back.d_up, back.d_down)


def separate_step(lengths, byte_ids, small, query_w, key_w, value_w, out_w, gate_w, up_w, down_w, out_grad, vocab):
    layer_count, _, model = query_w.shape
    shards = [small]
    for layer in range(layer_count):
        shards.append(jnp.concatenate([w[layer] for w in (query_w, key_w, value_w, out_w)], 1))
        shards.append(jnp.concatenate([gate_w[layer], up_w[layer]], 1))
        shards.append(down_w[layer])
    encoded, full, small_wide, ids, conv, choice, kept = separate_forward(lengths, byte_ids, shards, layer_count, vocab, model)
    gains = small_wide.T[vocab + CONV + 2 :]
    gains_a, gains_f = gains[:layer_count], gains[layer_count : 2 * layer_count]
    grad_stream = out_grad.astype(jnp.float32)
    partial = []
    gains = []
    for layer in reversed(range(layer_count)):
        before, saved = kept[layer]
        weights = full[3 * layer : 3 * layer + 3]
        grad_stream, d_gain_attn, d_gain_ffn, *grads = layer_backward(
            lengths, grad_stream, before, gains_a[layer][None], gains_f[layer][None], saved, *weights, 3
        )
        partial = list(grads) + partial
        gains = [(d_gain_attn[0], d_gain_ffn[0])] + gains
    small_grad = pl.pallas_call(
        functools.partial(gbst_backward_kernel, vocab),
        out_shape=jax.ShapeDtypeStruct(small_wide.shape, jnp.float32),
        in_specs=[SMEM] + [VMEM] * 5,
        out_specs=VMEM,
        compiler_params=pltpu.CompilerParams(vmem_limit_bytes=56 << 20),
        name="mix_bytes_backward",
    )(lengths, ids, small_wide, conv, choice, grad_stream)
    columns = jnp.stack([a for a, _ in gains] + [f for _, f in gains]).T
    small_grad = lax.dynamic_update_slice(small_grad, columns, (0, vocab + CONV + 2))
    outs = scatter_all([p.astype(jnp.bfloat16) for p in [small_grad] + partial], 1)
    small_out, *rest = outs
    attn_out, ffn_out, down_out = rest[0::3], rest[1::3], rest[2::3]
    columns = [jnp.stack([a[:, i * model : (i + 1) * model] for a in attn_out]) for i in range(4)]
    wide = ffn_out[0].shape[1] // 2
    halves_out = [jnp.stack([a[:, :wide] for a in ffn_out]), jnp.stack([a[:, wide:] for a in ffn_out])]
    return encoded, small_out, (*columns, *halves_out, jnp.stack(down_out))


def on_device(
    byte_ids,
    lengths,
    embed,
    conv_weight,
    conv_bias,
    scorer,
    norm_attn,
    query_w,
    key_w,
    value_w,
    attn_out_w,
    norm_ffn,
    gate_w,
    up_w,
    down_w,
    out_grad,
):
    layers, vocab = query_w.shape[0], embed.shape[0]
    small = packed_small(embed, conv_weight, conv_bias, scorer, norm_attn, norm_ffn)
    if query_w.shape[1] % 8 == 0 and HEADS % lax.axis_size("ctx") == 0:
        heads_w = head_columns(query_w, key_w, value_w)
        encoded, small_out, wide_grads = fused_step(
            lengths, byte_ids, small, heads_w, attn_out_w, gate_w, up_w, down_w, out_grad[0], vocab
        )
    else:
        encoded, small_out, wide_grads = separate_step(
            lengths, byte_ids, small, query_w, key_w, value_w, attn_out_w, gate_w, up_w, down_w, out_grad[0], vocab
        )
    d_query, d_key, d_value, d_out, d_gate, d_up, d_down = wide_grads
    d_embed, d_conv, d_bias, d_scorer, d_norm_attn, d_norm_ffn = split_small(small_out.T, vocab, layers)
    return (encoded[None], d_embed, d_conv, d_bias, d_scorer, d_norm_attn, d_query, d_key, d_value, d_out, d_norm_ffn,
            d_gate, d_up, d_down)


def solution(mesh):
    placed = (
        P("dp", "ctx"),
        P("dp", None),
        P(None, ("dp", "ctx")),
        P(None, ("dp", "ctx")),
        P(("dp", "ctx")),
        P(("dp", "ctx")),
        P(None, ("dp", "ctx")),
        P(None, ("dp", "ctx"), None),
        P(None, ("dp", "ctx"), None),
        P(None, ("dp", "ctx"), None),
        P(None, ("dp", "ctx"), None),
        P(None, ("dp", "ctx")),
        P(None, ("dp", "ctx"), None),
        P(None, ("dp", "ctx"), None),
        P(None, ("dp", "ctx"), None),
        P("dp", "ctx", None),
    )
    return jax.shard_map(
        on_device,
        mesh=mesh,
        in_specs=placed,
        out_specs=(
            P("dp", "ctx", None),
            P(None, ("dp", "ctx")),
            P(None, ("dp", "ctx")),
            P(("dp", "ctx")),
            P(("dp", "ctx")),
            P(None, ("dp", "ctx")),
            P(None, ("dp", "ctx"), None),
            P(None, ("dp", "ctx"), None),
            P(None, ("dp", "ctx"), None),
            P(None, ("dp", "ctx"), None),
            P(None, ("dp", "ctx")),
            P(None, ("dp", "ctx"), None),
            P(None, ("dp", "ctx"), None),
            P(None, ("dp", "ctx"), None),
        ),
        check_vma=False,
    )
```

```python
import functools
import types
import jax
import jax.numpy as jnp
from jax import lax
from jax.experimental import pallas as pl
from jax.experimental.pallas import tpu as pltpu
from jax.sharding import PartitionSpec as P


MESH = pl.DeviceIdType.MESH
CORES = 2
LANES = 128
THIRD = 0.1
DEPTH = 2
SPLIT = 3
LAG = 1


def grid_of():
    dp, ctx = lax.axis_size("dp"), lax.axis_size("ctx")
    rows = 2 if ctx % 2 == 0 else 1
    return dp // CORES, rows, ctx // rows


def place_of():
    _, _, nx = grid_of()
    d, c = lax.axis_index("dp"), lax.axis_index("ctx")
    return d // CORES, d % CORES, c // nx, c % nx


def device(z, core, y, x):
    _, _, nx = grid_of()
    return (z * CORES + core, y * nx + x)


def along(axis):
    place = list(place_of())
    nz, ny, nx = grid_of()
    size = (nz, CORES, ny, nx)[axis]
    found = []
    for i in range(1, size):
        there = list(place)
        there[axis] = lax.rem(place[axis] + i, size)
        found.append((there[axis], device(*there)))
    return found


def sibling():
    z, core, y, x = place_of()
    return device(z, 1 - core, y, x)


def greet_all():
    barrier = pltpu.get_barrier_semaphore()
    targets = [target for axis in (0, 2, 3) for _, target in along(axis)] + [sibling()]
    _, ny, nx = grid_of()
    z, core, y, x = place_of()
    for i in range(1, ny):
        for j in range(1, nx):
            targets.append(device(z, core, lax.rem(y + i, ny), lax.rem(x + j, nx)))
    for target in targets:
        pl.semaphore_signal(barrier, inc=1, device_id=target, device_id_type=MESH)
    pl.semaphore_wait(barrier, len(targets))
    return targets


ORDERS = ((0, 3, 2), (0, 2, 3), (3, 2, 0))


def splits_of(width, count):
    units = width // LANES
    cuts = [units * i // count * LANES for i in range(count + 1)]
    return [(a, b - a) for a, b in zip(cuts, cuts[1:])]


def pieces_of(width, third, first=0):
    units = width // LANES
    last = int(units * third)
    left = (units - last + 1) // 2
    found, at = [], first // LANES
    for order, size in zip(ORDERS, (left, units - last - left, last)):
        if size:
            found.append((pl.ds(at * LANES, size * LANES), order))
        at += size
    return found


def hops(width, third):
    nz, ny, nx = grid_of()
    return len(pieces_of(width, third)) * (nz - 1 + ny - 1 + nx - 1) + 1


class Sender:
    def __init__(self, sems):
        self.sems, self.count, self.flying = sems, 0, []

    def send(self, src, dst, target):
        copy = pltpu.make_async_remote_copy(
            src_ref=src, dst_ref=dst, send_sem=self.sems.at[0, self.count], recv_sem=self.sems.at[1, self.count],
            device_id=target, device_id_type=MESH)
        copy.start()
        self.count += 1
        self.flying.append(copy)
        return copy

    def finish(self):
        for copy in self.flying:
            copy.wait_send()
        self.flying = []


class GatherChunk(Sender):
    phases = 4

    def __init__(self, shard, out, sems, local_sem, third):
        super().__init__(sems)
        self.shard, self.out, self.local_sem = shard, out, local_sem
        self.pieces = pieces_of(shard.shape[-1], third)
        self.waiting = []

    def stage(self, number):
        place = place_of()
        for copy in self.waiting:
            copy.wait_recv()
        self.waiting = []
        if number == 0:
            self.own = pltpu.make_async_copy(self.shard, self.out.at[place], self.local_sem)
            self.own.start()
        if number == 1:
            self.own.wait()
        if number < 3:
            for columns, order in self.pieces:
                have = order[:number]
                where = tuple(slice(None) if axis in have else place[axis] for axis in range(4)) + (slice(None), columns)
                src = self.out.at[where] if number else self.shard.at[:, columns]
                for _, target in along(order[number]):
                    self.waiting.append(self.send(src, self.out.at[where], target))
        else:
            where = (slice(None), place[1])
            self.waiting.append(self.send(self.out.at[where], self.out.at[where], sibling()))

    def arrive(self):
        for copy in self.waiting:
            copy.wait_recv()
        self.waiting = []


class Pipeline:
    def __init__(self, chunks):
        self.chunks, self.steps, self.done = chunks, [], [0] * len(chunks)
        phases = chunks[0].phases
        for t in range(len(chunks) + phases):
            for number in [0] + list(range(phases - 1, 0, -1)):
                if 0 <= t - number < len(chunks):
                    self.steps.append((t - number, number))

    def tick(self, count=1):
        for _ in range(count):
            if self.steps:
                i, number = self.steps.pop(0)
                self.chunks[i].stage(number)
                self.done[i] = number + 1

    def until(self, i):
        while self.done[i] < self.chunks[i].phases:
            self.tick()

    def need(self, i):
        self.until(i)
        self.chunks[i].arrive()


def gather_kernel(n, third, *refs):
    shards, outs, sems, local_sems = refs[:n], refs[n:2 * n], refs[2 * n:3 * n], refs[3 * n]
    greet_all()
    chunks = [GatherChunk(shards[i], outs[i], sems[i], local_sems.at[i], third) for i in range(n)]
    ticker = Pipeline(chunks)
    for i in range(n):
        ticker.need(i)
    for chunk in chunks:
        chunk.finish()


def gather_all(shards, collective_id, third=THIRD):
    nz, ny, nx = grid_of()
    n = len(shards)
    outs = pl.pallas_call(
        functools.partial(gather_kernel, n, third),
        out_shape=[jax.ShapeDtypeStruct((nz, CORES, ny, nx) + s.shape, s.dtype) for s in shards],
        in_specs=[pl.BlockSpec(memory_space=pl.ANY)] * n,
        out_specs=[pl.BlockSpec(memory_space=pl.ANY)] * n,
        scratch_shapes=[pltpu.SemaphoreType.DMA((2, hops(s.shape[-1], third))) for s in shards] + [pltpu.SemaphoreType.DMA((n,))],
        compiler_params=pltpu.CompilerParams(collective_id=collective_id, has_side_effects=True),
        name="gather_weights",
    )(*shards)
    return [o.reshape((-1,) + o.shape[5:]) for o in outs]


def add_into(dst, src, lead):
    if not lead:
        dst[...] = (dst[...].astype(jnp.float32) + src[...].astype(jnp.float32)).astype(dst.dtype)
        return

    def body(i, carry):
        add_into(dst.at[i], src.at[i], lead[1:])
        return carry
    lax.fori_loop(0, lead[0], body, 0)


class ScatterChunk(Sender):
    phases = 5

    def __init__(self, parts, out, scratch, sems, local_sem, third):
        super().__init__(sems)
        self.parts, self.out, self.local_sem = parts, out, local_sem
        self.held, self.across, *landing = scratch
        self.pieces = [(columns, order[::-1], landing[3 * i:3 * i + 3])
                       for i, (columns, order) in enumerate(pieces_of(parts.shape[-1], third))]
        self.waiting = []

    @staticmethod
    def scratch(shape, dtype, third):
        sizes = dict(zip((0, 2, 3), grid_of()))
        whole = (*sizes.values(), *shape)
        found = [whole, whole]
        for columns, order in pieces_of(shape[-1], third):
            order = order[::-1]
            for number in range(3):
                rest = [sizes[a] for a in sizes if a in order[number + 1:]]
                found.append((sizes[order[number]] - 1, *rest, shape[0], columns.size))
        return [pltpu.VMEM(s, dtype) for s in found]

    def stage(self, number):
        place = place_of()
        sizes = dict(zip((0, 2, 3), grid_of()))
        for copy in self.waiting:
            copy.wait_recv()
        self.waiting = []
        if number == 0:
            self.own = pltpu.make_async_copy(self.parts.at[:, place[1]], self.held, self.local_sem)
            self.own.start()
            self.waiting.append(self.send(self.parts.at[:, 1 - place[1]], self.across, sibling()))
            return
        if number == 1:
            self.own.wait()
            add_into(self.held, self.across, list(sizes.values()))
        for columns, order, landing in self.pieces:
            if number > 1:
                mine = order[:number - 1]
                where = tuple(place[a] if a in mine else slice(None) for a in sizes) + (slice(None), columns)
                lead = [sizes[a] for a in sizes if a not in mine]
                landed = landing[number - 2]
                if number < 4:
                    for i in range(landed.shape[0]):
                        add_into(self.held.at[where], landed.at[i], lead)
                else:
                    total = self.held[where].astype(jnp.float32)
                    for i in range(landed.shape[0]):
                        total = total + landed[i].astype(jnp.float32)
                    self.out[:, columns] = total
            if number < 4:
                axis, mine = order[number - 1], order[:number - 1]
                for i, (there, target) in enumerate(along(axis)):
                    where = tuple(there if a == axis else place[a] if a in mine else slice(None) for a in sizes)
                    src = self.held.at[where + (slice(None), columns)]
                    self.waiting.append(self.send(src, landing[number - 1].at[i], target))


def scatter_kernel(n, third, counts, *refs):
    parts, outs, rest = refs[:n], refs[n:2 * n], list(refs[2 * n:])
    greet_all()
    chunks = []
    for i in range(n):
        scratch = [rest.pop(0) for _ in range(counts[i])]
        chunks.append(ScatterChunk(parts[i], outs[i], scratch, rest.pop(0), rest.pop(0), third))
    ticker = Pipeline(chunks)
    for i in range(n):
        ticker.until(i)
    for chunk in chunks:
        chunk.finish()


def scatter_scratch(shape, dtype, third):
    scratch = ScatterChunk.scratch(shape, dtype, third)
    return scratch + [pltpu.SemaphoreType.DMA((2, hops(shape[-1], third))), pltpu.SemaphoreType.DMA]


def scatter_all(parts, collective_id, third=THIRD):
    nz, ny, nx = grid_of()
    n = len(parts)
    devices = nz * CORES * ny * nx
    parts = [p.reshape((nz, CORES, ny, nx, p.shape[0] // devices) + p.shape[1:]) for p in parts]
    scratch, counts = [], []
    for p in parts:
        made = scatter_scratch(p.shape[4:], p.dtype, third)
        counts.append(len(made) - 2)
        scratch += made
    return pl.pallas_call(
        functools.partial(scatter_kernel, n, third, counts),
        out_shape=[jax.ShapeDtypeStruct(p.shape[4:], jnp.float32) for p in parts],
        in_specs=[pl.BlockSpec(memory_space=pl.ANY)] * n,
        out_specs=[pl.BlockSpec(memory_space=pltpu.VMEM)] * n,
        scratch_shapes=scratch,
        compiler_params=pltpu.CompilerParams(collective_id=collective_id, has_side_effects=True, vmem_limit_bytes=60 << 20),
        name="scatter_grads",
    )(*parts)


HEADS = 12
HEAD_DIM = 64
CHUNK = 256
NORM_EPS = 1e-06
NEG_FILL = -1000000000.0
GELU_A = 0.7978845608028654
GELU_B = 0.044715


def dot(a, b):
    return jnp.dot(a, b, preferred_element_type=jnp.float32)


def dot_nt(a, b):
    return lax.dot_general(a, b, (((1,), (1,)), ((), ())), preferred_element_type=jnp.float32)


def low(v):
    return v.astype(jnp.bfloat16)


def flip(v):
    return low(v.astype(jnp.float32).T)


def inverse_rms(v):
    return lax.rsqrt(jnp.mean(v * v, -1, keepdims=True) + NORM_EPS)


def ends_of(lengths_ref):
    ends, total = [], 0
    for i in range(lengths_ref.shape[-1]):
        total = total + lengths_ref[0, i]
        ends.append(total)
    return ends


def segments(places, ends):
    seg = jnp.zeros(places.shape, jnp.int32)
    for end in ends:
        seg = seg + jnp.where(places >= end, 1, 0)
    return seg


def heads_each():
    return -(-HEADS // lax.axis_size("ctx"))


def others():
    size, me = lax.axis_size("ctx"), lax.axis_index("ctx")
    return [lax.rem(me + 1 + i, size) for i in range(size)]


def greet_group():
    barrier = pltpu.get_barrier_semaphore()
    peers_ = others()[:-1]
    for p in peers_:
        pl.semaphore_signal(barrier, inc=1, device_id=(lax.axis_index("dp"), p), device_id_type=MESH)
    pl.semaphore_wait(barrier, len(peers_))


def to_group(src, dst, sems, index, p):
    return pltpu.make_async_remote_copy(
        src_ref=src, dst_ref=dst, send_sem=sems.at[(0,) + index], recv_sem=sems.at[(1,) + index],
        device_id=(lax.axis_index("dp"), p), device_id_type=MESH)


def tokens_of(p, count):
    return pl.ds(pl.multiple_of(p * count, count), count)


def spread_heads(src, dst, sems, local_sem, each):
    me = lax.axis_index("ctx")
    count = src.shape[2]
    copies = []
    for h in range(each):
        rows = pl.ds(h * HEAD_DIM, HEAD_DIM)
        made = []
        for i, p in enumerate(others()):
            theirs = pl.ds(pl.multiple_of((p * each + h) * HEAD_DIM, HEAD_DIM), HEAD_DIM)
            a, b = src.at[:, theirs], dst.at[:, rows, tokens_of(me, count)]
            if i == lax.axis_size("ctx") - 1:
                copy = pltpu.make_async_copy(a, b, local_sem.at[h])
            else:
                copy = to_group(a, b, sems, (h, i), p)
            copy.start()
            made.append(copy)
        copies.append(made)
    return copies


def arrive(made):
    for copy in made[:-1]:
        copy.wait_recv()
    made[-1].wait()


def attention_forward(each, seg_all, ends, qkv, lse, out_send, att, qkv_copies, sems, tick=lambda: None):
    size, me = lax.axis_size("ctx"), lax.axis_index("ctx")
    count = att.shape[1]
    copies = []
    for h in range(each):
        arrive(qkv_copies[h])
        rows = pl.ds(h * HEAD_DIM, HEAD_DIM)
        key = flip(qkv[1, rows, :])
        value_t = qkv[2, rows, :]
        theirs = pl.ds(pl.multiple_of((me * each + h) * HEAD_DIM, HEAD_DIM), HEAD_DIM)
        for i, p in enumerate(others()):
            tokens = tokens_of(p, count)
            seg_q = segments(2 * (p * count + lax.broadcasted_iota(jnp.int32, (1, count), 1)), ends)
            scores = dot(key, qkv[0, rows, tokens])
            scores = jnp.where(seg_all[...] == seg_q, scores, NEG_FILL)
            top = jnp.max(scores, 0, keepdims=True)
            probs = jnp.exp(scores - top)
            total = jnp.sum(probs, 0, keepdims=True)
            lse[h, :, tokens] = top + jnp.log(total)
            result = low(dot(value_t, low(probs)) / total)
            if i == size - 1:
                att[theirs, :] = result
            else:
                out_send[h, i] = result
                copy = to_group(out_send.at[h, i], att.at[theirs], sems, (h, i), p)
                copy.start()
                copies.append(copy)
            tick()
    return copies


def gelu_parts(gate):
    inner = jnp.tanh(GELU_A * (gate + GELU_B * gate * gate * gate))
    half = 0.5 * (1.0 + inner)
    slope = half + 0.5 * gate * (1.0 - inner * inner) * GELU_A * (1.0 + 3.0 * GELU_B * gate * gate)
    return gate * half, slope


def layer_forward_kernel(lengths, x, gain_a, gain_f, w_attn_hbm, w_ffn_hbm, w_down_hbm,
                         out, middle, normed_t, qkv, lse, att, gate_out, up_out, nffn_t,
                         w_attn, w_ffn, w_down, qkv_all, out_send, seg_all, nffn,
                         sems_in, sems_out, local_sems, w_sems):
    each = heads_each()
    model = x.shape[1]
    loads = [pltpu.make_async_copy(a, b, w_sems.at[i]) for i, (a, b) in enumerate(
        ((w_attn_hbm, w_attn), (w_ffn_hbm, w_ffn), (w_down_hbm, w_down)))]
    for load in loads:
        load.start()
    greet_group()
    ends = ends_of(lengths)
    seg_all[...] = segments(2 * lax.broadcasted_iota(jnp.int32, seg_all.shape, 0), ends)
    stream = x[...]
    normed = low(stream * inverse_rms(stream) * gain_a[...])
    normed_t[...] = flip(normed)
    if qkv_all.shape[1] > model:
        qkv_all[:, model:, :] = jnp.zeros((3, qkv_all.shape[1] - model, qkv_all.shape[2]), jnp.bfloat16)
    loads[0].wait()
    for part in range(3):
        for c in range(model // CHUNK):
            columns = pl.ds(part * model + c * CHUNK, CHUNK)
            qkv_all[part, c * CHUNK:(c + 1) * CHUNK, :] = low(dot(normed, w_attn[:, columns]).T)
    qkv_copies = spread_heads(qkv_all, qkv, sems_in, local_sems, each)
    out_copies = attention_forward(each, seg_all, ends, qkv, lse, out_send, att, qkv_copies, sems_out)
    for copy in out_copies:
        copy.wait_recv()
    attended = flip(att[:model, :])
    mid = stream + dot(attended, w_attn[:, 3 * model:])
    middle[...] = mid
    after = low(mid * inverse_rms(mid) * gain_f[...])
    nffn[...] = after
    nffn_t[...] = flip(after)
    out[...] = mid
    loads[1].wait()
    loads[2].wait()
    hidden_count = w_down.shape[0]

    def step(c, carry):
        columns = pl.ds(pl.multiple_of(c * CHUNK, CHUNK), CHUNK)
        gate = dot(nffn[...], w_ffn[:, columns])
        up = dot(nffn[...], w_ffn[:, pl.ds(pl.multiple_of(hidden_count + c * CHUNK, CHUNK), CHUNK)])
        gate_out[:, columns] = gate
        up_out[:, columns] = up
        hidden = low(gelu_parts(gate)[0] * up)
        out[...] += dot(hidden, w_down[columns, :])
        return carry
    lax.fori_loop(0, hidden_count // CHUNK, step, 0)
    for made in qkv_copies:
        for copy in made[:-1]:
            copy.wait_send()
    for copy in out_copies:
        copy.wait_send()


VMEM = pl.BlockSpec(memory_space=pltpu.VMEM)
ANY = pl.BlockSpec(memory_space=pl.ANY)
SMEM = pl.BlockSpec(memory_space=pltpu.SMEM)


def layer_forward(lengths, x, gain_a, gain_f, w_attn, w_ffn, w_down, collective_id):
    size, each = lax.axis_size("ctx"), heads_each()
    count, model = x.shape
    wide = w_down.shape[0]
    group = count * size
    rows = each * size * HEAD_DIM
    f32, bf16 = jnp.float32, jnp.bfloat16
    made = lambda shape, dtype: jax.ShapeDtypeStruct(shape, dtype)
    return pl.pallas_call(
        layer_forward_kernel,
        out_shape=[made((count, model), f32), made((count, model), f32), made((model, count), bf16),
                   made((3, each * HEAD_DIM, group), bf16), made((each, 1, group), f32), made((rows, count), bf16),
                   made((count, wide), f32), made((count, wide), f32), made((model, count), bf16)],
        in_specs=[SMEM, VMEM, VMEM, VMEM, ANY, ANY, ANY],
        out_specs=[VMEM] * 9,
        scratch_shapes=[
            pltpu.VMEM(w_attn.shape, bf16), pltpu.VMEM(w_ffn.shape, bf16), pltpu.VMEM(w_down.shape, bf16),
            pltpu.VMEM((3, rows, count), bf16), pltpu.VMEM((each, size - 1, HEAD_DIM, count), bf16),
            pltpu.VMEM((group, count), jnp.int32), pltpu.VMEM((count, model), bf16),
            pltpu.SemaphoreType.DMA((2, each, size - 1)), pltpu.SemaphoreType.DMA((2, each, size - 1)),
            pltpu.SemaphoreType.DMA((each,)), pltpu.SemaphoreType.DMA((3,))],
        compiler_params=pltpu.CompilerParams(collective_id=collective_id, has_side_effects=True, vmem_limit_bytes=56 << 20),
        name="layer_forward",
    )(lengths, x, gain_a, gain_f, w_attn, w_ffn, w_down)


def layer_backward_kernel(lengths, grad, x, gain_a, gain_f, middle, normed_t, qkv, lse, att, gate_in, up_in, nffn_t,
                          w_attn_hbm, w_ffn_hbm, w_down_hbm,
                          grad_in, d_gain_a, d_gain_f, d_attn_hbm, d_ffn_hbm, d_down_hbm,
                          w_attn, w_ffn, w_down, d_attn, d_ffn, d_down, go_all, go, dqkv, q_send, kv_send, seg_all, total,
                          grad_low, mid_low, sems_in, sems_q, sems_kv, local_sems, w_sems, d_sems):
    each = heads_each()
    size, me = lax.axis_size("ctx"), lax.axis_index("ctx")
    count, model = x.shape
    wide = w_down.shape[0]
    loads = [pltpu.make_async_copy(a, b, w_sems.at[i]) for i, (a, b) in enumerate(
        ((w_down_hbm, w_down), (w_ffn_hbm, w_ffn), (w_attn_hbm, w_attn)))]
    for load in loads:
        load.start()
    greet_group()
    ends = ends_of(lengths)
    seg_all[...] = segments(2 * lax.broadcasted_iota(jnp.int32, seg_all.shape, 0), ends)
    grad_low[...] = low(grad[...])
    total[...] = jnp.zeros(total.shape, jnp.float32)
    loads[0].wait()
    loads[1].wait()

    def step(c, carry):
        columns = pl.ds(pl.multiple_of(c * CHUNK, CHUNK), CHUNK)
        later = pl.ds(pl.multiple_of(wide + c * CHUNK, CHUNK), CHUNK)
        g_hidden = dot_nt(grad_low[...], w_down[columns, :])
        up = up_in[:, columns]
        act, slope = gelu_parts(gate_in[:, columns])
        g_gate = low(g_hidden * up * slope)
        g_up = low(g_hidden * act)
        d_down[columns, :] = low(dot(low((act * up).T), grad_low[...]))
        d_ffn[:, columns] = low(dot(nffn_t[...], g_gate))
        d_ffn[:, later] = low(dot(nffn_t[...], g_up))
        total[...] += dot_nt(g_gate, w_ffn[:, columns]) + dot_nt(g_up, w_ffn[:, later])
        return carry
    lax.fori_loop(0, wide // CHUNK, step, 0)
    saves = [pltpu.make_async_copy(d_ffn, d_ffn_hbm, d_sems.at[0]), pltpu.make_async_copy(d_down, d_down_hbm, d_sems.at[1])]
    for save in saves:
        save.start()

    def norm_back(values, gain, upstream):
        scale = inverse_rms(values)
        scaled = upstream * gain
        along = jnp.mean(values * scaled, -1, keepdims=True)
        return scale * scaled - values * (scale * scale * scale * along), jnp.sum(upstream * values * scale, 0, keepdims=True)

    back, d_gain = norm_back(middle[...], gain_f[...], total[...])
    d_gain_f[...] = d_gain
    grad_in[...] = grad[...] + back
    mid_low[...] = low(grad_in[...])
    if go_all.shape[1] > model:
        go_all[:, model:, :] = jnp.zeros((1, go_all.shape[1] - model, count), jnp.bfloat16)
    loads[2].wait()
    for c in range(model // CHUNK):
        rows = slice(c * CHUNK, (c + 1) * CHUNK)
        go_all[0, rows, :] = low(dot_nt(mid_low[...], w_attn[rows, 3 * model:]).T)
    go_copies = spread_heads(go_all, go, sems_in, local_sems, each)
    for c in range(model // CHUNK):
        rows = slice(c * CHUNK, (c + 1) * CHUNK)
        d_attn[rows, 3 * model:] = low(dot(att[rows, :], mid_low[...]))
    sent = []
    for h in range(each):
        arrive(go_copies[h])
        rows = pl.ds(h * HEAD_DIM, HEAD_DIM)
        theirs = pl.ds(pl.multiple_of((me * each + h) * HEAD_DIM, HEAD_DIM), HEAD_DIM)
        key_t = qkv[1, rows, :]
        key, value = flip(key_t), flip(qkv[2, rows, :])
        g_key = jnp.zeros((HEAD_DIM, count * size), jnp.float32)
        g_value = jnp.zeros((HEAD_DIM, count * size), jnp.float32)
        for i, p in enumerate(others()):
            tokens = tokens_of(p, count)
            seg_q = segments(2 * (p * count + lax.broadcasted_iota(jnp.int32, (1, count), 1)), ends)
            query_t, go_t = qkv[0, rows, tokens], go[0, rows, tokens]
            scores = jnp.where(seg_all[...] == seg_q, dot(key, query_t), NEG_FILL)
            probs = jnp.exp(scores - lse[h, :, tokens])
            g_probs = dot(value, go_t)
            inner = jnp.sum(probs * g_probs, 0, keepdims=True)
            g_scores = low(probs * (g_probs - inner))
            g_query = low(dot(key_t, g_scores))
            g_key = g_key + dot_nt(query_t, g_scores)
            g_value = g_value + dot_nt(go_t, low(probs))
            if i == size - 1:
                dqkv[0, theirs, :] = g_query
            else:
                q_send[h, i] = g_query
                copy = to_group(q_send.at[h, i], dqkv.at[0, theirs], sems_q, (h, i), p)
                copy.start()
                sent.append(copy)
        kv_send[h, 0] = low(g_key)
        kv_send[h, 1] = low(g_value)
        for i, p in enumerate(others()):
            if i == size - 1:
                dqkv[1:, theirs, :] = kv_send[h, :, :, tokens_of(me, count)]
            else:
                copy = to_group(kv_send.at[h, :, :, tokens_of(p, count)], dqkv.at[pl.ds(1, 2), theirs], sems_kv, (h, i), p)
                copy.start()
                sent.append(copy)
    for copy in sent:
        copy.wait_recv()
    summed = jnp.zeros((model, count), jnp.float32)
    for part in range(3):
        for c in range(model // CHUNK):
            rows = slice(c * CHUNK, (c + 1) * CHUNK)
            columns = slice(part * model + c * CHUNK, part * model + (c + 1) * CHUNK)
            d_attn[:, columns] = low(dot_nt(normed_t[...], dqkv[part, rows, :]))
        summed = summed + dot(w_attn[:, part * model:(part + 1) * model], dqkv[part, :model, :])
    saves.append(pltpu.make_async_copy(d_attn, d_attn_hbm, d_sems.at[2]))
    saves[-1].start()
    back, d_gain = norm_back(x[...], gain_a[...], summed.T)
    d_gain_a[...] = d_gain
    grad_in[...] += back
    for made in go_copies:
        for copy in made[:-1]:
            copy.wait_send()
    for copy in sent:
        copy.wait_send()
    for save in saves:
        save.wait()


def layer_backward(lengths, grad, x, gain_a, gain_f, kept, w_attn, w_ffn, w_down, collective_id):
    size, each = lax.axis_size("ctx"), heads_each()
    count, model = x.shape
    wide = w_down.shape[0]
    group = count * size
    rows = each * size * HEAD_DIM
    f32, bf16 = jnp.float32, jnp.bfloat16
    made = lambda shape, dtype: jax.ShapeDtypeStruct(shape, dtype)
    return pl.pallas_call(
        layer_backward_kernel,
        out_shape=[made((count, model), f32), made((1, model), f32), made((1, model), f32),
                   made(w_attn.shape, bf16), made(w_ffn.shape, bf16), made(w_down.shape, bf16)],
        in_specs=[SMEM] + [VMEM] * 12 + [ANY] * 3,
        out_specs=[VMEM] * 3 + [ANY] * 3,
        scratch_shapes=[
            pltpu.VMEM(w_attn.shape, bf16), pltpu.VMEM(w_ffn.shape, bf16), pltpu.VMEM(w_down.shape, bf16),
            pltpu.VMEM(w_attn.shape, bf16), pltpu.VMEM(w_ffn.shape, bf16), pltpu.VMEM(w_down.shape, bf16),
            pltpu.VMEM((1, rows, count), bf16), pltpu.VMEM((1, each * HEAD_DIM, group), bf16),
            pltpu.VMEM((3, rows, count), bf16), pltpu.VMEM((each, size - 1, HEAD_DIM, count), bf16),
            pltpu.VMEM((each, 2, HEAD_DIM, group), bf16), pltpu.VMEM((group, count), jnp.int32),
            pltpu.VMEM((count, model), f32), pltpu.VMEM((count, model), bf16), pltpu.VMEM((count, model), bf16),
            pltpu.SemaphoreType.DMA((2, each, size - 1)), pltpu.SemaphoreType.DMA((2, each, size - 1)),
            pltpu.SemaphoreType.DMA((2, each, size - 1)), pltpu.SemaphoreType.DMA((each,)),
            pltpu.SemaphoreType.DMA((3,)), pltpu.SemaphoreType.DMA((3,))],
        compiler_params=pltpu.CompilerParams(collective_id=collective_id, has_side_effects=True, vmem_limit_bytes=60 << 20),
        name="layer_backward",
    )(lengths, grad, x, gain_a, gain_f, *kept, w_attn, w_ffn, w_down)


CONV = 4
BLOCKS = (1, 2, 3, 4)
HALO = 64


def halves_of(v):
    high = low(v)
    return high, low(v - high.astype(jnp.float32))


def dot_split(a, b):
    high, rest = halves_of(a)
    return dot(high, b) + dot(rest, b)


def dot_wide(a, b):
    (ah, al), (bh, bl) = halves_of(a), halves_of(b)
    return dot(ah, bh) + dot(ah, bl) + dot(al, bh)


def block_starts(places, ends):
    start = jnp.zeros(places.shape, jnp.int32)
    for end in ends:
        start = jnp.where(places >= end, end, start)
    rel = places - start
    found = []
    for size in BLOCKS:
        if size & (size - 1) == 0:
            found.append(places - (rel & (size - 1)))
        else:
            count = jnp.floor((rel.astype(jnp.float32) + 0.5) * (1.0 / size)).astype(jnp.int32)
            found.append(start + count * size)
    return found


def valid_of(places, ends):
    return (places >= 0) & (places < ends[-1])


def tap_ids(ids, first, span, ends):
    places = first - HALO + lax.broadcasted_iota(jnp.int32, (1, span), 1)
    own = segments(places, ends)
    count = ids.shape[1] // 3
    rows = []
    for tap in range(CONV):
        theirs = places + (tap - 1)
        at = count - HALO + tap - 1
        near = ids[:, at - at % 128:at - at % 128 + span + 128]
        near = lax.slice_in_dim(near, at % 128, at % 128 + span, axis=1)
        use = valid_of(places, ends) & valid_of(theirs, ends) & (segments(theirs, ends) == own)
        rows.append(jnp.where(use, near, -1))
    return rows, valid_of(places, ends)


def one_hot(row, vocab):
    return low(jnp.where(lax.broadcasted_iota(jnp.int32, (vocab, row.shape[1]), 0) == row, 1.0, 0.0))


def mix_blocks(first, span, tokens, ends):
    keys = block_starts(first - HALO + lax.broadcasted_iota(jnp.int32, (span, tokens), 0), ends)
    found = []
    for parity in range(2):
        own = block_starts(first + 2 * lax.broadcasted_iota(jnp.int32, (1, tokens), 1) + parity, ends)
        found.append([key == mine for key, mine in zip(keys, own)])
    return found


def gbst_forward(ends, ids, first, small, conv, choice, vocab, tokens, tick=lambda: None):
    span = conv.shape[1]
    taps, valid = tap_ids(ids, first, span, ends)
    table = small[:, :vocab]
    at = vocab + CONV
    total = small[:, at:at + 1] * jnp.where(valid, 1.0, 0.0)
    for tap in range(CONV):
        total = total + dot_split(table * small[:, vocab + tap:vocab + tap + 1], one_hot(taps[tap], vocab))
        tick()
    conv[...] = total
    scored = jnp.sum(total * small[:, at + 1:at + 2], 0, keepdims=True)
    scored = jnp.broadcast_to(scored, (8, span))
    parts = []
    for _ in range(3):
        parts.append(low(scored))
        scored = scored - parts[-1].astype(jnp.float32)
    mix = jnp.zeros((span, tokens), jnp.float32)
    for parity, blocks in enumerate(mix_blocks(first, span, tokens, ends)):
        logits = []
        for size, block in zip(BLOCKS, blocks):
            ones = low(jnp.where(block, 1.0, 0.0))
            logits.append((dot(parts[0], ones) + dot(parts[1], ones) + dot(parts[2], ones))[:1] * (1.0 / size))
        top = functools.reduce(jnp.maximum, logits)
        raised = [jnp.exp(v - top) for v in logits]
        whole = functools.reduce(jnp.add, raised)
        for i, (size, block) in enumerate(zip(BLOCKS, blocks)):
            chosen = raised[i] / whole
            choice[len(BLOCKS) * parity + i:len(BLOCKS) * parity + i + 1, :] = chosen
            mix = mix + jnp.where(block, chosen * (0.5 / size), 0.0)
        tick()
    return dot_wide(total, mix)


def gbst_backward(ends, ids, first, small, conv, choice, grad_t, vocab, out, tick=lambda: None):
    span, tokens = conv.shape[1], grad_t.shape[1]
    taps, valid = tap_ids(ids, first, span, ends)
    at = vocab + CONV
    total = conv[...]
    along = dot_wide(total.T, grad_t)
    mix = jnp.zeros((span, tokens), jnp.float32)
    scored = jnp.zeros((span, tokens), jnp.float32)
    for parity, blocks in enumerate(mix_blocks(first, span, tokens, ends)):
        chosen = [choice[len(BLOCKS) * parity + i:len(BLOCKS) * parity + i + 1, :] for i in range(len(BLOCKS))]
        grads = [jnp.sum(jnp.where(block, along, 0.0), 0, keepdims=True) * (0.5 / size) for size, block in zip(BLOCKS, blocks)]
        inner = functools.reduce(jnp.add, [c * g for c, g in zip(chosen, grads)])
        for i, (size, block) in enumerate(zip(BLOCKS, blocks)):
            mix = mix + jnp.where(block, chosen[i] * (0.5 / size), 0.0)
            scored = scored + jnp.where(block, chosen[i] * (grads[i] - inner) * (1.0 / size), 0.0)
    g_scored = jnp.sum(scored.T, 0, keepdims=True)
    g_conv = dot_wide(grad_t, mix.T) + small[:, at + 1:at + 2] * g_scored
    out[:, at + 1:at + 2] = jnp.sum(total * g_scored, 1, keepdims=True)
    g_conv = g_conv * jnp.where(valid, 1.0, 0.0)
    out[:, at:at + 1] = jnp.sum(g_conv, 1, keepdims=True)
    high, rest = halves_of(g_conv)
    table = small[:, :vocab]
    g_table = jnp.zeros(table.shape, jnp.float32)
    for tap in range(CONV):
        hot = one_hot(taps[tap], vocab)
        g_tap = dot_nt(high, hot) + dot_nt(rest, hot)
        g_table = g_table + g_tap * small[:, vocab + tap:vocab + tap + 1]
        out[:, vocab + tap:vocab + tap + 1] = jnp.sum(g_tap * table, 1, keepdims=True)
        tick()
    out[:, :vocab] = g_table


def gbst_forward_kernel(vocab, tokens, lengths, ids, small, out, conv, choice):
    ends = ends_of(lengths)
    first = lax.axis_index("ctx") * 2 * tokens
    out[...] = gbst_forward(ends, ids, first, small, conv, choice, vocab, tokens).T


def gbst_backward_kernel(vocab, lengths, ids, small, conv, choice, grad, out):
    ends = ends_of(lengths)
    first = lax.axis_index("ctx") * 2 * grad.shape[0]
    out[...] = jnp.zeros(out.shape, jnp.float32)
    gbst_backward(ends, ids, first, small, conv, choice, grad[...].T, vocab, out)


class Gather(Sender):
    phases = 4

    def __init__(self, sources, out, sems, local_sems, first=0, width=None):
        super().__init__(sems)
        self.out = out
        self.columns = pl.ds(first, width or out.shape[-1])
        self.pieces = pieces_of(self.columns.size, THIRD, first)
        self.waiting = []
        self.own = []
        for i, (source, at) in enumerate(sources):
            a, b = max(first, at), min(first + (width or out.shape[-1]), at + source.shape[-1])
            if a < b:
                there = out.at[place_of() + (slice(None), pl.ds(a, b - a))]
                copy = pltpu.make_async_copy(source.at[:, pl.ds(a - at, b - a)], there, local_sems.at[i])
                copy.start()
                self.own.append(copy)

    def stage(self, number):
        place = place_of()
        self.arrive()
        if number == 0:
            for copy in self.own:
                copy.wait()
        if number < 3:
            for columns, order in self.pieces:
                have = order[:number]
                where = tuple(slice(None) if axis in have else place[axis] for axis in range(4)) + (slice(None), columns)
                for _, target in along(order[number]):
                    self.waiting.append(self.send(self.out.at[where], self.out.at[where], target))
        else:
            where = (slice(None), place[1]) + (slice(None),) * 3 + (self.columns,)
            self.waiting.append(self.send(self.out.at[where], self.out.at[where], sibling()))

    def arrive(self):
        for copy in self.waiting:
            copy.wait_recv()
        self.waiting = []


class GatherHeads(Sender):
    phases = 3

    def __init__(self, shard, out, sems, local_sem):
        super().__init__(sems)
        self.shard, self.out = shard, out
        self.waiting = []
        self.own = pltpu.make_async_copy(shard.at[lax.axis_index("ctx")], out.at[place_of()], local_sem)
        self.own.start()

    def stage(self, number):
        z, core, y, x = place_of()
        self.arrive()
        if number == 0:
            for p in others()[:-1]:
                target = (lax.axis_index("dp"), p)
                self.waiting.append(self.send(self.shard.at[p], self.out.at[z, core, y, x], target))
        elif number == 1:
            self.own.wait()
            for _, target in along(0):
                self.waiting.append(self.send(self.out.at[z, core], self.out.at[z, core], target))
        else:
            where = (slice(None), core)
            self.waiting.append(self.send(self.out.at[where], self.out.at[where], sibling()))

    arrive = Gather.arrive


class Ticker:
    def __init__(self):
        self.chunks, self.steps = [], []

    def pipeline(self, chunks):
        self.chunks = chunks
        self.done = [0] * len(chunks)
        for t in range(len(chunks) + 4 * DEPTH):
            for number in (0, 3, 2, 1):
                i = t - DEPTH * number
                if 0 <= i < len(chunks) and number < chunks[i].phases:
                    self.steps.append((i, number))

    def tick(self, count=1):
        for _ in range(count):
            if self.steps:
                i, number = self.steps.pop(0)
                self.chunks[i].stage(number)
                self.done[i] = number + 1

    def need(self, i):
        while self.done[i] < self.chunks[i].phases:
            self.tick()
        self.chunks[i].arrive()


class Scatter(Sender):
    phases = 5

    def __init__(self, parts, emit, scratch, sems, local_sem, before=None, credit=None, final=True, first=0):
        super().__init__(sems)
        self.parts, self.emit, self.local_sem, self.first = parts, emit, local_sem, first
        self.held, self.across, *landing = scratch
        self.pieces = [(columns, order[::-1], landing[3 * i:3 * i + 3])
                       for i, (columns, order) in enumerate(pieces_of(self.held.shape[-1], THIRD))]
        self.waiting, self.before, self.credit, self.final = [], before, credit, final

    @staticmethod
    def scratch(shape, dtype):
        sizes = dict(zip((0, 2, 3), grid_of()))
        whole = (*sizes.values(), *shape)
        found = [whole, whole]
        for columns, order in pieces_of(shape[-1], THIRD):
            order = order[::-1]
            for number in range(3):
                rest = [sizes[a] for a in sizes if a in order[number + 1:]]
                found.append((sizes[order[number]] - 1, *rest, shape[0], columns.size))
        return [pltpu.VMEM(s, dtype) for s in found]

    def targets(self):
        return [target for axis in (0, 2, 3) for _, target in along(axis)] + [sibling()]

    def open(self):
        if self.before is not None:
            self.before.finish()
            pl.semaphore_wait(self.credit, len(self.targets()))

    def close(self):
        if not self.final:
            for target in self.targets():
                pl.semaphore_signal(self.credit, inc=1, device_id=target, device_id_type=MESH)

    arrive = Gather.arrive

    def stage(self, number):
        place = place_of()
        sizes = dict(zip((0, 2, 3), grid_of()))
        self.arrive()
        if number == 0:
            self.open()
            columns = (slice(None),) * 3 + (pl.ds(self.first, self.held.shape[-1]),)
            self.own = pltpu.make_async_copy(self.parts.at[(slice(None), place[1]) + columns], self.held, self.local_sem)
            self.own.start()
            self.waiting.append(self.send(self.parts.at[(slice(None), 1 - place[1]) + columns], self.across, sibling()))
            return
        if number == 1:
            self.own.wait()
            add_into(self.held, self.across, list(sizes.values()))
        for columns, order, landing in self.pieces:
            if number > 1:
                mine = order[:number - 1]
                where = tuple(place[a] if a in mine else slice(None) for a in sizes) + (slice(None), columns)
                lead = [sizes[a] for a in sizes if a not in mine]
                landed = landing[number - 2]
                if number < 4:
                    for i in range(landed.shape[0]):
                        add_into(self.held.at[where], landed.at[i], lead)
                else:
                    total = self.held[where].astype(jnp.float32)
                    for i in range(landed.shape[0]):
                        total = total + landed[i].astype(jnp.float32)
                    self.emit(pl.ds(self.first + columns.start, columns.size), total)
            if number < 4:
                axis, mine = order[number - 1], order[:number - 1]
                for i, (there, target) in enumerate(along(axis)):
                    where = tuple(there if a == axis else place[a] if a in mine else slice(None) for a in sizes)
                    src = self.held.at[where + (slice(None), columns)]
                    self.waiting.append(self.send(src, landing[number - 1].at[i], target))
        if number == 4:
            self.close()


class ScatterHeads(Scatter):
    phases = 4

    def __init__(self, parts, out, scratch, sems, local_sem, before=None, credit=None, final=True):
        Sender.__init__(self, sems)
        self.parts, self.out, self.local_sem = parts, out, local_sem
        self.across, self.landed, self.sums = scratch
        self.waiting, self.before, self.credit, self.final = [], before, credit, final

    def targets(self):
        return [target for _, target in along(0)] + [sibling()]

    def stage(self, number):
        nz, ny, nx = grid_of()
        z, core, y, x = place_of()
        me = lax.axis_index("ctx")
        self.arrive()
        if number == 0:
            if self.before is not None:
                pl.semaphore_wait(self.credit, len(self.targets()))
            self.waiting.append(self.send(self.parts.at[:, 1 - core], self.across, sibling()))
        elif number == 1:
            add_into(self.parts.at[:, core], self.across, [nz, ny, nx])
            for i, (there, target) in enumerate(along(0)):
                self.waiting.append(self.send(self.parts.at[there, core], self.landed.at[i], target))
        elif number == 2:
            for j in range(ny):
                for k in range(nx):
                    total = self.parts[z, core, j, k].astype(jnp.float32)
                    for i in range(nz - 1):
                        total = total + self.landed[i, j, k].astype(jnp.float32)
                    self.sums[j * nx + k] = total
            self.close()
            for p in others()[:-1]:
                self.waiting.append(self.send(self.sums.at[p], self.out.at[me], (lax.axis_index("dp"), p)))
            self.own = pltpu.make_async_copy(self.sums.at[me], self.out.at[me], self.local_sem)
            self.own.start()

    def finish(self):
        self.arrive()
        for copy in self.flying:
            copy.wait_send()
        self.flying = []
        if self.own is not None:
            self.own.wait()
        self.own = None


class Rota:
    def __init__(self):
        self.queue, self.count = [], 0

    def add(self, chunk):
        chunk.stage(0)
        self.queue.append([LAG + self.count, chunk, 1])
        self.count += 1

    def tick(self, count=1):
        for _ in range(count):
            if not self.queue:
                return
            item = min(self.queue, key=lambda found: found[0])
            item[1].stage(item[2])
            item[0] += LAG
            item[2] += 1
            if item[2] == item[1].phases:
                self.queue.remove(item)

    def close(self, chunk):
        while any(item[1] is chunk for item in self.queue):
            self.tick()


def run_kernel(body, inputs, outputs, scratch, collective_id, name):
    def leaves(value):
        return [v for part in value for v in leaves(part)] if isinstance(value, list) else [value]

    def again(value, refs):
        return [again(v, refs) for v in value] if isinstance(value, list) else next(refs)

    def flat(group):
        return leaves(list(group.values()))

    def rebuilt(group, refs):
        return {k: again(value, refs) for k, value in group.items()}

    def kernel(*refs):
        refs = iter(refs)
        body(types.SimpleNamespace(**rebuilt(inputs, refs), **rebuilt(outputs, refs), **rebuilt(scratch, refs)))
    found = pl.pallas_call(
        kernel,
        out_shape=[s for s, _ in flat(outputs)],
        in_specs=[s for _, s in flat(inputs)],
        out_specs=[s for _, s in flat(outputs)],
        scratch_shapes=flat(scratch),
        compiler_params=pltpu.CompilerParams(collective_id=collective_id, has_side_effects=True, vmem_limit_bytes=60 << 20),
        name=name,
    )(*[a for a, _ in flat(inputs)])
    return types.SimpleNamespace(**rebuilt(outputs, iter(found)))


class Keep:
    def __init__(self, sems):
        self.sems, self.count, self.flying = sems, 0, []

    def __call__(self, src, dst):
        copy = pltpu.make_async_copy(src, dst, self.sems.at[self.count])
        copy.start()
        self.count += 1
        self.flying.append(copy)
        return copy

    def finish(self):
        for copy in self.flying:
            copy.wait()


def unpack(blocks, dst):
    nz, cores, ny, nx, rows, width = blocks.shape
    each = ny * nx * rows
    part = next(p for p in (512, 256, 128) if width % p == 0)

    def body(i, carry):
        for c in range(width // part):
            columns = slice(c * part, (c + 1) * part)
            found = [blocks[i // cores, i % cores, y, x, :, columns].astype(jnp.float32) for y in range(ny) for x in range(nx)]
            dst[pl.ds(pl.multiple_of(i * each, each), each), columns] = low(jnp.concatenate(found, 0))
        return carry
    lax.fori_loop(0, nz * cores, body, 0)


def to_blocks(dst, columns, values):
    nz, cores, ny, nx, rows, _ = dst.shape
    for b in range(nz * cores * ny * nx):
        g, k = divmod(b, ny * nx)
        dst[g // cores, g % cores, k // nx, k % nx, :, columns] = low(values[b * rows:(b + 1) * rows])


def norm_back(values, gain, upstream):
    scale = inverse_rms(values)
    scaled = upstream * gain
    mean = jnp.mean(values * scaled, -1, keepdims=True)
    return scale * scaled - values * (scale * scale * scale * mean), jnp.sum(upstream * values * scale, 0, keepdims=True)


def from_slot(i):
    size, me = lax.axis_size("ctx"), lax.axis_index("ctx")
    return lax.rem(me + size - 1 - i, size)


def gain_rows(small, vocab, layers):
    at = vocab + CONV + 2
    rows = small[:, at // LANES * LANES:].T
    at = at % LANES
    return [rows[at + l:at + l + 1, :] for l in range(2 * layers)]


def head_columns(query_w, key_w, value_w, dst):
    layers, size, rows, width = dst.shape
    each = query_w.shape[2] // size
    rest = [jnp.zeros((rows, width - 3 * each), jnp.float32)] if width > 3 * each else []
    for l in range(layers):
        whole = [w[l].astype(jnp.float32) for w in (query_w, key_w, value_w)]
        for p in range(size):
            dst[l, p] = low(jnp.concatenate([w[:, p * each:(p + 1) * each] for w in whole] + rest, 1))


def forward_body(vocab, layers, r):
    ends = ends_of(r.lengths)
    size, me = lax.axis_size("ctx"), lax.axis_index("ctx")
    each = heads_each()
    base = each * HEAD_DIM
    keep = Keep(r.keep_sems)
    greet_all()
    ids, count = r.ids, r.byte_ids.shape[1]
    near = []
    for i, (there, at) in enumerate(((lax.rem(me + 1, size), 0), (lax.rem(me + size - 1, size), 2))):
        copy = to_group(r.byte_ids, ids.at[:, pl.ds(at * count, count)], r.ids_sems, (i,), there)
        copy.start()
        near.append(copy)
    ids[:, count:2 * count] = r.byte_ids[...]
    head_columns(r.query_w, r.key_w, r.value_w, r.heads_w)
    chunks = [Gather([(r.small, 0)], r.full_small, r.small_sems, r.local_sems.at[0])]
    model = r.encoded.shape[1]
    wide = r.gate_w.shape[2]
    for l in range(layers):
        chunks.append(GatherHeads(r.heads_w.at[l], r.full_heads[l], r.heads_sems.at[l], r.more_sems.at[l, 1]))
        sources = [(r.gate_w.at[l], 0), (r.up_w.at[l], wide), (r.out_w.at[l], 2 * wide)]
        for k, (at, part) in enumerate(splits_of(r.full_ffn[l].shape[-1], SPLIT)):
            chunks.append(Gather(sources, r.full_ffn[l], r.ffn_sems.at[l, k], r.local_sems.at[1 + l * SPLIT + k], at, part))
        chunks.append(Gather([(r.down_w.at[l], 0)], r.full_down[l], r.down_sems.at[l], r.more_sems.at[l]))
    ticker = Ticker()
    ticker.pipeline(chunks)
    tick = ticker.tick
    tick(2)
    tokens = count // 2
    seg_all = r.seg_all
    seg_all[...] = segments(2 * lax.broadcasted_iota(jnp.int32, seg_all.shape, 0), ends)
    for copy in near:
        copy.wait_recv()
    ticker.need(0)
    small = r.small_wide
    nz, cores, ny, nx, rows, _ = r.full_small.shape
    for b in range(nz * cores * ny * nx):
        place = (b // (cores * ny * nx), b // (ny * nx) % cores, b // nx % ny, b % nx)
        small[b * rows:(b + 1) * rows, :] = r.full_small[place].astype(jnp.float32)
    tick()
    stream = gbst_forward(ends, ids[...], me * count, small[...], r.conv, r.choice, vocab, tokens, tick).T
    gains = gain_rows(small, vocab, layers)
    keep(r.conv, r.out_conv)
    for l in range(layers):
        base_chunk = 1 + (2 + SPLIT) * l
        nrm, qkv, att = r.nrm[l], r.qkv[l], r.att[l]
        r.x[l][...] = stream
        r.mine[...] = flip(low(stream * inverse_rms(stream) * gains[l]))
        spread = []
        for i, p in enumerate(others()[:-1]):
            copy = to_group(r.mine, nrm.at[:, tokens_of(me, tokens)], r.nrm_sems.at[l], (i,), p)
            copy.start()
            spread.append(copy)
        nrm[:, tokens_of(me, tokens)] = r.mine[...]
        keep(r.x[l], r.out_x[l])
        ticker.need(base_chunk)
        unpack(r.full_heads[l], r.w_heads[l])
        keep(r.w_heads[l], r.out_w_heads[l])
        r.w_turned[...] = flip(r.w_heads[l][...])
        for i in range(-1, size - 1):
            if i >= 0:
                spread[i].wait_recv()
            theirs = tokens_of(me if i < 0 else from_slot(i), tokens)
            qkv[:, theirs] = low(dot(r.w_turned[...], nrm[:, theirs]))
            tick()
        keep(nrm, r.out_nrm[l])
        keep(qkv, r.out_qkv[l])
        copies = []
        for h in range(each):
            query = pl.ds(h * HEAD_DIM, HEAD_DIM)
            key = flip(qkv[base + h * HEAD_DIM:base + (h + 1) * HEAD_DIM, :])
            value_t = qkv[2 * base + h * HEAD_DIM:2 * base + (h + 1) * HEAD_DIM, :]
            rows = pl.ds(pl.multiple_of((me * each + h) * HEAD_DIM, HEAD_DIM), HEAD_DIM)
            for i, p in enumerate(others()):
                theirs = tokens_of(p, tokens)
                seg_q = segments(2 * (p * tokens + lax.broadcasted_iota(jnp.int32, (1, tokens), 1)), ends)
                scores = jnp.where(seg_all[...] == seg_q, dot(key, qkv[query, theirs]), NEG_FILL)
                top = jnp.max(scores, 0, keepdims=True)
                probs = jnp.exp(scores - top)
                total = jnp.sum(probs, 0, keepdims=True)
                r.lse[l][h, :, theirs] = top + jnp.log(total)
                result = low(dot(value_t, low(probs)) / total)
                if i == size - 1:
                    att[rows, :] = result
                else:
                    r.att_send[h, i] = result
                    copy = to_group(r.att_send.at[h, i], att.at[rows], r.att_sems.at[l], (h, i), p)
                    copy.start()
                    copies.append(copy)
                tick(i != 3)
        keep(r.lse[l], r.out_lse[l])
        for k in range(SPLIT):
            ticker.need(base_chunk + 1 + k)
        load = pltpu.make_async_copy(r.full_ffn[l], r.blocks, r.load_sems.at[l, 0])
        load.start()
        tick()
        for copy in copies:
            copy.wait_recv()
        keep(att, r.out_att[l])
        load.wait()
        unpack(r.blocks, r.w_ffn)
        mid = stream + dot(flip(att[...]), r.w_ffn[:, 2 * wide:])
        r.middle[l][...] = mid
        after = low(mid * inverse_rms(mid) * gains[layers + l])
        r.nffn[...] = after
        r.nffn_t[l][...] = flip(after)
        r.total[...] = mid
        keep(r.middle[l], r.out_middle[l])
        keep(r.nffn_t[l], r.out_nffn_t[l])
        ticker.need(base_chunk + 1 + SPLIT)
        load = pltpu.make_async_copy(r.full_down[l], r.w_down, r.load_sems.at[l, 1])
        load.start()
        load.wait()
        part = wide // (nz * cores)

        def step(c, carry):
            columns = pl.ds(pl.multiple_of(c * part, part), part)
            gate = dot(r.nffn[...], r.w_ffn[:, columns])
            up = dot(r.nffn[...], r.w_ffn[:, pl.ds(pl.multiple_of(wide + c * part, part), part)])
            hidden = low(gelu_parts(gate)[0] * up)
            r.total[...] += dot(hidden, r.w_down[c // cores, c % cores].reshape(part, model))
            return carry
        half = nz * cores // 2
        lax.fori_loop(0, half, step, 0)
        tick(2)
        lax.fori_loop(half, nz * cores, step, 0)
        stream = r.total[...]
        for copy in spread + copies:
            copy.wait_send()
    r.encoded[...] = low(stream)
    for copy in near:
        copy.wait_send()
    for i, chunk in enumerate(chunks):
        ticker.need(i)
        chunk.finish()
    keep.finish()


def like(shape, dtype):
    return jax.ShapeDtypeStruct(shape, dtype)


def kept_shapes(tokens, model):
    size, each = lax.axis_size("ctx"), heads_each()
    f32, bf16 = jnp.float32, jnp.bfloat16
    turned = -(-3 * each * HEAD_DIM // LANES) * LANES
    return dict(x=((tokens, model), f32), middle=((tokens, model), f32), nrm=((model, tokens * size), bf16),
                qkv=((turned, tokens * size), bf16), lse=((each, 1, tokens * size), f32),
                att=((each * size * HEAD_DIM, tokens), bf16), nffn_t=((model, tokens), bf16))


def forward_pass(lengths, byte_ids, small, query_w, key_w, value_w, out_w, gate_w, up_w, down_w, vocab):
    nz, ny, nx = grid_of()
    size, each = lax.axis_size("ctx"), heads_each()
    layers, _, model = out_w.shape
    wide = gate_w.shape[2]
    tokens = byte_ids.shape[1] // 2
    span = byte_ids.shape[1] + 2 * HALO
    f32, bf16 = jnp.float32, jnp.bfloat16
    dma, vmem = pltpu.SemaphoreType.DMA, pltpu.VMEM
    blocks = lambda rows, width: (nz, CORES, ny, nx, rows, width)
    shapes = kept_shapes(tokens, model)
    per_layer = lambda made: [made] * layers
    ffn = blocks(gate_w.shape[1], 2 * wide + model)
    down = blocks(*down_w.shape[1:])
    heads = blocks(query_w.shape[1], shapes["qkv"][0][0])
    inputs = dict(lengths=(lengths, SMEM), byte_ids=(byte_ids, VMEM), small=(small, ANY), query_w=(query_w, VMEM), key_w=(key_w, VMEM),
                  value_w=(value_w, VMEM), out_w=(out_w, ANY), gate_w=(gate_w, ANY), up_w=(up_w, ANY), down_w=(down_w, ANY))
    outputs = dict(
        encoded=(like((tokens, model), bf16), VMEM), small_wide=(like((model, small.shape[1]), f32), VMEM),
        ids=(like((1, 3 * byte_ids.shape[1]), jnp.int32), VMEM), choice=(like((2 * len(BLOCKS), tokens), f32), VMEM),
        out_conv=(like((model, span), f32), ANY), full_ffn=per_layer((like(ffn, bf16), ANY)),
        full_down=per_layer((like(down, bf16), ANY)), out_w_heads=per_layer((like((model, heads[-1]), bf16), ANY)),
        out_x=per_layer((like(*shapes["x"]), ANY)), out_middle=per_layer((like(*shapes["middle"]), ANY)),
        out_nrm=per_layer((like(*shapes["nrm"]), ANY)), out_qkv=per_layer((like(*shapes["qkv"]), ANY)),
        out_lse=per_layer((like(*shapes["lse"]), ANY)), out_att=per_layer((like(*shapes["att"]), ANY)),
        out_nffn_t=per_layer((like(*shapes["nffn_t"]), ANY)))
    scratch = {k: per_layer(vmem(*v)) for k, v in shapes.items()}
    scratch.update(
        heads_w=vmem((layers, size) + heads[4:], bf16), full_small=vmem(blocks(*small.shape), bf16), conv=vmem((model, span), f32), full_heads=per_layer(vmem(heads, bf16)),
        w_heads=per_layer(vmem((model, heads[-1]), bf16)), w_turned=vmem((heads[-1], model), bf16), w_ffn=vmem((model, ffn[-1]), bf16),
        w_down=vmem(down, bf16), blocks=vmem(ffn, bf16), mine=vmem((model, tokens), bf16),
        att_send=vmem((each, size - 1, HEAD_DIM, tokens), bf16), seg_all=vmem((tokens * size, tokens), jnp.int32),
        nffn=vmem((tokens, model), bf16), total=vmem((tokens, model), f32),
        keep_sems=dma((1 + 8 * layers,)), ids_sems=dma((2, 2)), local_sems=dma((1 + layers * SPLIT, 3)), more_sems=dma((layers, 2)),
        load_sems=dma((layers, 2)), nrm_sems=dma((layers, 2, size - 1)), att_sems=dma((layers, 2, each, size - 1)),
        small_sems=dma((2, hops(small.shape[1], THIRD))), heads_sems=dma((layers, 2, size + nz - 1)),
        ffn_sems=dma((layers, SPLIT, 2, hops(ffn[-1], THIRD))), down_sems=dma((layers, 2, hops(model, THIRD))))
    return run_kernel(functools.partial(forward_body, vocab, layers), inputs, outputs, scratch, 4, "forward_pass")


def backward_body(vocab, layers, r):
    ends = ends_of(r.lengths)
    size, me = lax.axis_size("ctx"), lax.axis_index("ctx")
    each = heads_each()
    base = each * HEAD_DIM
    tokens, model = r.out_grad.shape
    wide = r.w_down.shape[0]
    nz, cores, ny, nx, rows, _ = r.block_ffn.shape[1:]
    part = wide // (nz * cores)
    loads = {}

    def load(key, src, dst, sem):
        loads[key] = pltpu.make_async_copy(src, dst, sem)
        loads[key].start()

    def load_ffn(l):
        sems = r.load_sems.at[l]
        load(0, r.in_nffn_t[l], r.nffn_t, sems.at[0])
        load(1, r.in_w_down[l], r.w_down, sems.at[1])
        load(2, r.in_w_ffn[l], r.w_ffn, sems.at[2])
        load(3, r.in_middle[l], r.middle, sems.at[3])
        load(4, r.in_att[l], r.att, sems.at[4])

    def load_attention(l):
        sems = r.load_sems.at[l]
        load(5, r.in_qkv[l], r.qkv, sems.at[5])
        load(6, r.in_lse[l], r.lse, sems.at[6])
        load(7, r.in_w_heads[l], r.w_heads, sems.at[7])
        load(8, r.in_nrm[l], r.nrm, sems.at[8])
        load(9, r.in_x[l], r.x, sems.at[9])
    load_ffn(layers - 1)
    load_attention(layers - 1)
    greet_all()
    gains = gain_rows(r.small_wide, vocab, layers)
    d_gains = [None] * (2 * layers)
    seg_all = r.seg_all
    seg_all[...] = segments(2 * lax.broadcasted_iota(jnp.int32, seg_all.shape, 0), ends)
    r.dqkv[...] = jnp.zeros(r.dqkv.shape, jnp.bfloat16)
    r.grad[...] = r.out_grad[...].astype(jnp.float32)
    rota = Rota()
    tick = rota.tick
    before = [None] * (2 + SPLIT)
    made = []

    def begin(kind, chunk):
        made.append(chunk)
        before[kind] = chunk
        rota.add(chunk)
    for l in reversed(range(layers)):
        r.grad_low[...] = low(r.grad[...])
        r.total[...] = jnp.zeros(r.total.shape, jnp.float32)
        for key in range(3):
            loads[key].wait()
        r.nffn[...] = flip(r.nffn_t[...])

        def saves(c, slot):
            sems = r.save_sems.at[slot]
            columns = pl.ds(pl.multiple_of(c * part, part), part)
            later = pl.ds(pl.multiple_of(wide + c * part, part), part)
            where = (slice(None),) * 5
            return [pltpu.make_async_copy(r.block_down.at[slot], r.parts_down[l].at[c // cores, c % cores], sems.at[0]),
                    pltpu.make_async_copy(r.block_ffn.at[slot, :, :, :, :, :, pl.ds(0, part)], r.parts_ffn[l].at[where + (columns,)], sems.at[1]),
                    pltpu.make_async_copy(r.block_ffn.at[slot, :, :, :, :, :, pl.ds(part, part)], r.parts_ffn[l].at[where + (later,)], sems.at[2])]

        def step(c, carry):
            columns = pl.ds(pl.multiple_of(c * part, part), part)
            later = pl.ds(pl.multiple_of(wide + c * part, part), part)
            slot = lax.rem(c, 2)

            @pl.when(c >= 2)
            def _():
                for copy in saves(c - 2, slot):
                    copy.wait()
            gate = dot(r.nffn[...], r.w_ffn[:, columns])
            up = dot(r.nffn[...], r.w_ffn[:, later])
            g_hidden = dot_nt(r.grad_low[...], r.w_down[columns, :])
            act, slope = gelu_parts(gate)
            g_gate = low(g_hidden * up * slope)
            g_up = low(g_hidden * act)
            d_down = low(dot(low((act * up).T), r.grad_low[...]))
            r.block_down[slot] = d_down.reshape(r.block_down.shape[1:])
            to_blocks(r.block_ffn.at[slot], slice(0, part), dot(r.nffn_t[...], g_gate))
            to_blocks(r.block_ffn.at[slot], slice(part, 2 * part), dot(r.nffn_t[...], g_up))
            for copy in saves(c, slot):
                copy.start()
            r.total[...] += dot_nt(g_gate, r.w_ffn[:, columns]) + dot_nt(g_up, r.w_ffn[:, later])
            return carry
        for c in range(0, nz * cores, 2):
            lax.fori_loop(c, c + 2, step, 0)
            tick()
        for c in (nz * cores - 2, nz * cores - 1):
            for copy in saves(c, c % 2):
                copy.wait()

        def emit_down(columns, total, l=l):
            r.d_down[l, :, columns] = total

        def emit_ffn(columns, total, l=l):
            first, last = columns.start, columns.start + columns.size
            for out, start in ((r.d_gate, 0), (r.d_up, wide), (r.d_out, 2 * wide)):
                a, b = max(first, start), min(last, start + out.shape[2])
                if a < b:
                    out[l, :, a - start:b - start] = total[:, a - first:b - first]
        if before[0] is not None:
            rota.close(before[0])
        begin(0, Scatter(r.parts_down[l], emit_down, r.down_scratch, r.down_sems.at[l], r.own_sems.at[l, 0], before[0], r.credits.at[0], l == 0))
        loads[3].wait()
        loads[4].wait()
        back, d_gains[layers + l] = norm_back(r.middle[...], gains[layers + l], r.total[...])
        r.grad[...] += back
        r.grad_low[...] = low(r.grad[...])
        r.go_all[0] = flip(dot_nt(r.grad_low[...], r.w_ffn[:, 2 * wide:]))
        go_copies = spread_heads(r.go_all, r.go, r.go_sems.at[l], r.go_own.at[l], each)
        to_blocks(r.block_out, slice(0, model), dot(r.att[...], r.grad_low[...]))
        save = pltpu.make_async_copy(r.block_out, r.parts_ffn[l].at[(slice(None),) * 5 + (pl.ds(2 * wide, model),)], r.own_sems.at[l, 3])
        save.start()
        save.wait()
        for k, (at, _) in enumerate(splits_of(r.parts_ffn[l].shape[-1], SPLIT)):
            if before[2 + k] is not None:
                rota.close(before[2 + k])
            begin(2 + k, Scatter(r.parts_ffn[l], emit_ffn, r.ffn_scratch[k], r.ffn_sems.at[l, k], r.ffn_own.at[l, k],
                                 before[2 + k], r.credits.at[2 + k], l == 0, at))
        if l:
            load_ffn(l - 1)
        for key in range(5, 8):
            loads[key].wait()
        for h in range(each):
            arrive(go_copies[h])
            rows_h = [slice(k * base + h * HEAD_DIM, k * base + (h + 1) * HEAD_DIM) for k in range(3)]
            key_t = r.qkv[rows_h[1], :]
            key, value = flip(key_t), flip(r.qkv[rows_h[2], :])
            g_key = jnp.zeros((HEAD_DIM, tokens * size), jnp.float32)
            g_value = jnp.zeros((HEAD_DIM, tokens * size), jnp.float32)
            for p in range(size):
                theirs = slice(p * tokens, (p + 1) * tokens)
                seg_q = segments(2 * (p * tokens + lax.broadcasted_iota(jnp.int32, (1, tokens), 1)), ends)
                query_t, go_t = r.qkv[rows_h[0], theirs], r.go[0, h * HEAD_DIM:(h + 1) * HEAD_DIM, theirs]
                scores = jnp.where(seg_all[...] == seg_q, dot(key, query_t), NEG_FILL)
                probs = jnp.exp(scores - r.lse[h, :, theirs])
                g_probs = dot(value, go_t)
                inner = jnp.sum(probs * g_probs, 0, keepdims=True)
                g_scores = low(probs * (g_probs - inner))
                r.dqkv[rows_h[0], theirs] = low(dot(key_t, g_scores))
                g_key = g_key + dot_nt(query_t, g_scores)
                g_value = g_value + dot_nt(go_t, low(probs))
                tick(p != 3)
            r.dqkv[rows_h[1], :] = low(g_key)
            r.dqkv[rows_h[2], :] = low(g_value)
        spread = []
        for i, p in enumerate(others()):
            mine = dot(r.w_heads[...], r.dqkv[:, tokens_of(p, tokens)])
            if i == size - 1:
                r.small_grad[:, :tokens] = mine
            else:
                r.sum_send[i] = low(mine)
                copy = to_group(r.sum_send.at[i], r.sum_land.at[i], r.sum_sems.at[l], (i,), p)
                copy.start()
                spread.append(copy)
        for key in (8, 9):
            loads[key].wait()
        if before[1] is not None:
            rota.close(before[1])
            before[1].finish()

        def heads_step(i, carry):
            each_rows = ny * nx * rows
            found = dot_nt(r.nrm[pl.ds(pl.multiple_of(i * each_rows, each_rows), each_rows), :], r.dqkv[...])
            for k in range(ny * nx):
                r.block_heads[i // cores, i % cores, k // nx, k % nx] = low(found[k * rows:(k + 1) * rows])
            return carry
        lax.fori_loop(0, nz * cores, heads_step, 0)
        begin(1, ScatterHeads(r.block_heads, r.d_heads[l], r.heads_scratch, r.heads_sems.at[l], r.own_sems.at[l, 2], before[1], r.credits.at[1], l == 0))
        tick()
        for i, copy in enumerate(spread):
            copy.wait_recv()
            r.small_grad[:, :tokens] += r.sum_land[i].astype(jnp.float32)
        back, d_gains[l] = norm_back(r.x[...], gains[l], r.small_grad[:, :tokens].T)
        r.grad[...] += back
        if l:
            load_attention(l - 1)
        for copies in go_copies:
            for copy in copies[:-1]:
                copy.wait_send()
        for copy in spread:
            copy.wait_send()
    out = r.small_grad
    out[...] = jnp.zeros(out.shape, jnp.float32)
    gbst_backward(ends, r.ids[...], me * 2 * tokens, r.small_wide[...], r.conv, r.choice, r.grad[...].T, vocab, out, tick)
    at = vocab + CONV + 2
    turned = jnp.concatenate(d_gains + [jnp.zeros((-2 * layers % 8, model), jnp.float32)], 0).T
    for i in range(2 * layers):
        out[:, at + i:at + i + 1] = turned[:, i:i + 1]
    to_blocks(r.block_small, slice(None), out[...])

    def emit_small(columns, total):
        r.d_small[:, columns] = total
    begin(0, Scatter(r.block_small, emit_small, r.small_scratch, r.small_sems, r.own_sems.at[layers, 0]))
    while rota.queue:
        tick()
    for chunk in made:
        chunk.finish()
    for l in range(layers):
        for k, found in enumerate((r.d_query, r.d_key, r.d_value)):
            found[l] = jnp.concatenate([r.d_heads[l][p, :, k * base:(k + 1) * base] for p in range(size)], 1)


def backward_pass(lengths, out_grad, fwd, vocab):
    nz, ny, nx = grid_of()
    size, each = lax.axis_size("ctx"), heads_each()
    tokens, model = out_grad.shape
    layers = len(fwd.full_ffn)
    w_ffn = [w.reshape(-1, w.shape[-1]) for w in fwd.full_ffn]
    w_down = [w.reshape(-1, w.shape[-1]) for w in fwd.full_down]
    wide = w_down[0].shape[0]
    part = wide // (nz * CORES)
    f32, bf16 = jnp.float32, jnp.bfloat16
    dma, vmem = pltpu.SemaphoreType.DMA, pltpu.VMEM
    shapes = kept_shapes(tokens, model)
    per_layer = lambda found: [found] * layers
    heads_width = fwd.out_w_heads[0].shape[1]
    ffn, down = fwd.full_ffn[0].shape, fwd.full_down[0].shape
    heads = ffn[:5] + (heads_width,)
    small = ffn[:5] + (fwd.small_wide.shape[1],)
    anywhere = lambda arrays: [(a, ANY) for a in arrays]
    inputs = dict(
        lengths=(lengths, SMEM), out_grad=(out_grad, VMEM), small_wide=(fwd.small_wide, VMEM), ids=(fwd.ids, VMEM),
        choice=(fwd.choice, VMEM), conv=(fwd.out_conv, VMEM), in_w_heads=anywhere(fwd.out_w_heads), in_w_ffn=anywhere(w_ffn),
        in_w_down=anywhere(w_down), in_x=anywhere(fwd.out_x), in_middle=anywhere(fwd.out_middle), in_nrm=anywhere(fwd.out_nrm),
        in_qkv=anywhere(fwd.out_qkv), in_lse=anywhere(fwd.out_lse), in_att=anywhere(fwd.out_att), in_nffn_t=anywhere(fwd.out_nffn_t))
    outputs = dict(
        d_small=(like(small[4:], f32), VMEM), d_query=(like((layers, ffn[4], model), f32), VMEM),
        d_key=(like((layers, ffn[4], model), f32), VMEM), d_value=(like((layers, ffn[4], model), f32), VMEM),
        d_gate=(like((layers, ffn[4], wide), f32), VMEM), d_up=(like((layers, ffn[4], wide), f32), VMEM),
        d_out=(like((layers, ffn[4], model), f32), VMEM), d_down=(like((layers,) + down[4:], f32), VMEM),
        parts_ffn=per_layer((like(ffn, bf16), ANY)), parts_down=per_layer((like(down, bf16), ANY)))
    scratch = {k: vmem(*v) for k, v in shapes.items()}
    scratch.update(
        grad=vmem((tokens, model), f32), total=vmem((tokens, model), f32), grad_low=vmem((tokens, model), bf16),
        nffn=vmem((tokens, model), bf16), w_heads=vmem((model, heads_width), bf16), w_ffn=vmem(w_ffn[0].shape, bf16),
        w_down=vmem(w_down[0].shape, bf16), block_ffn=vmem((2,) + ffn[:5] + (2 * part,), bf16), block_down=vmem((2,) + down[2:], bf16),
        block_out=vmem(ffn[:5] + (model,), bf16), block_heads=vmem(heads, bf16), block_small=vmem(small, bf16),
        go_all=vmem((1,) + shapes["att"][0], bf16), go=vmem((1, each * HEAD_DIM, tokens * size), bf16), dqkv=vmem(*shapes["qkv"]),
        sum_send=vmem((size - 1, model, tokens), bf16),
        sum_land=vmem((size - 1, model, tokens), bf16),
        seg_all=vmem((tokens * size, tokens), jnp.int32), small_grad=vmem(fwd.small_wide.shape, f32),
        down_scratch=Scatter.scratch(down[4:], bf16), ffn_scratch=[Scatter.scratch((ffn[4], w), bf16) for _, w in splits_of(ffn[-1], SPLIT)], ffn_own=dma((layers, SPLIT)),
        small_scratch=Scatter.scratch(small[4:], bf16),
        d_heads=per_layer(vmem((size,) + heads[4:], f32)), heads_scratch=[vmem((nz, ny, nx) + heads[4:], bf16), vmem((nz - 1, ny, nx) + heads[4:], bf16), vmem((size,) + heads[4:], f32)],
        load_sems=dma((layers, 10)), save_sems=dma((2, 3)), own_sems=dma((layers + 1, 4)), go_own=dma((layers, each)),
        go_sems=dma((layers, 2, each, size - 1)), sum_sems=dma((layers, 2, size - 1)), heads_sems=dma((layers, 2, size + nz - 1)),
        ffn_sems=dma((layers, SPLIT, 2, hops(ffn[-1], THIRD))), down_sems=dma((layers, 2, hops(model, THIRD))),
        small_sems=dma((2, hops(small[-1], THIRD))), credits=pltpu.SemaphoreType.REGULAR((2 + SPLIT,)))
    return run_kernel(functools.partial(backward_body, vocab, layers), inputs, outputs, scratch, 5, "backward_pass")


def packed_small(embed, conv_weight, conv_bias, scorer, norm_attn, norm_ffn):
    rows = jnp.concatenate([embed, conv_weight, conv_bias[None], scorer[None], norm_attn, norm_ffn], 0).T
    return jnp.pad(rows, ((0, 0), (0, -rows.shape[1] % 128)))


def split_small(rows, vocab, layers):
    at = vocab + CONV
    return (rows[:vocab], rows[vocab:at], rows[at], rows[at + 1], rows[at + 2 : at + 2 + layers],
            rows[at + 2 + layers : at + 2 + 2 * layers])


def separate_forward(lengths, byte_ids, shards, layer_count, vocab, model):
    ring, tokens = lax.axis_size("ctx"), byte_ids.shape[1] // 2
    up = [(i, (i + 1) % ring) for i in range(ring)]
    down = [(j, i) for i, j in up]
    ids = jnp.concatenate([lax.ppermute(byte_ids, "ctx", up), byte_ids, lax.ppermute(byte_ids, "ctx", down)], 1)
    small_full, *full = [a.reshape(-1, a.shape[-1]) for a in gather_all(shards, 0)]
    small_wide = small_full.astype(jnp.float32)
    gains = small_wide.T[vocab + CONV + 2 :]
    stream, conv, choice = pl.pallas_call(
        functools.partial(gbst_forward_kernel, vocab, tokens),
        out_shape=[
            jax.ShapeDtypeStruct((tokens, model), jnp.float32),
            jax.ShapeDtypeStruct((model, byte_ids.shape[1] + 2 * HALO), jnp.float32),
            jax.ShapeDtypeStruct((2 * len(BLOCKS), tokens), jnp.float32),
        ],
        in_specs=[SMEM, VMEM, VMEM],
        out_specs=[VMEM] * 3,
        compiler_params=pltpu.CompilerParams(vmem_limit_bytes=56 << 20),
        name="mix_bytes",
    )(lengths, ids, small_wide)
    kept = []
    for layer in range(layer_count):
        before = stream
        stream, *saved = layer_forward(
            lengths, stream, gains[layer][None], gains[layer_count + layer][None], *full[3 * layer : 3 * layer + 3], 2
        )
        kept.append((before, saved))
    return stream.astype(jnp.bfloat16), full, small_wide, ids, conv, choice, kept


def fused_step(lengths, byte_ids, small, query_w, key_w, value_w, out_w, gate_w, up_w, down_w, out_grad, vocab):
    fwd = forward_pass(lengths, byte_ids, small, query_w, key_w, value_w, out_w, gate_w, up_w, down_w, vocab)
    back = backward_pass(lengths, out_grad, fwd, vocab)
    grads = (back.d_query, back.d_key, back.d_value, back.d_out, back.d_gate, back.d_up, back.d_down)
    return fwd.encoded, back.d_small, grads


def separate_step(lengths, byte_ids, small, query_w, key_w, value_w, out_w, gate_w, up_w, down_w, out_grad, vocab):
    layer_count, _, model = query_w.shape
    shards = [small]
    for layer in range(layer_count):
        shards.append(jnp.concatenate([w[layer] for w in (query_w, key_w, value_w, out_w)], 1))
        shards.append(jnp.concatenate([gate_w[layer], up_w[layer]], 1))
        shards.append(down_w[layer])
    encoded, full, small_wide, ids, conv, choice, kept = separate_forward(lengths, byte_ids, shards, layer_count, vocab, model)
    gains = small_wide.T[vocab + CONV + 2 :]
    gains_a, gains_f = gains[:layer_count], gains[layer_count : 2 * layer_count]
    grad_stream = out_grad.astype(jnp.float32)
    partial = []
    gains = []
    for layer in reversed(range(layer_count)):
        before, saved = kept[layer]
        weights = full[3 * layer : 3 * layer + 3]
        grad_stream, d_gain_attn, d_gain_ffn, *grads = layer_backward(
            lengths, grad_stream, before, gains_a[layer][None], gains_f[layer][None], saved, *weights, 3
        )
        partial = list(grads) + partial
        gains = [(d_gain_attn[0], d_gain_ffn[0])] + gains
    small_grad = pl.pallas_call(
        functools.partial(gbst_backward_kernel, vocab),
        out_shape=jax.ShapeDtypeStruct(small_wide.shape, jnp.float32),
        in_specs=[SMEM] + [VMEM] * 5,
        out_specs=VMEM,
        compiler_params=pltpu.CompilerParams(vmem_limit_bytes=56 << 20),
        name="mix_bytes_backward",
    )(lengths, ids, small_wide, conv, choice, grad_stream)
    columns = jnp.stack([a for a, _ in gains] + [f for _, f in gains]).T
    small_grad = lax.dynamic_update_slice(small_grad, columns, (0, vocab + CONV + 2))
    outs = scatter_all([p.astype(jnp.bfloat16) for p in [small_grad] + partial], 1)
    small_out, *rest = outs
    attn_out, ffn_out, down_out = rest[0::3], rest[1::3], rest[2::3]
    columns = [jnp.stack([a[:, i * model : (i + 1) * model] for a in attn_out]) for i in range(4)]
    wide = ffn_out[0].shape[1] // 2
    halves_out = [jnp.stack([a[:, :wide] for a in ffn_out]), jnp.stack([a[:, wide:] for a in ffn_out])]
    return encoded, small_out, (*columns, *halves_out, jnp.stack(down_out))


def on_device(
    byte_ids,
    lengths,
    embed,
    conv_weight,
    conv_bias,
    scorer,
    norm_attn,
    query_w,
    key_w,
    value_w,
    attn_out_w,
    norm_ffn,
    gate_w,
    up_w,
    down_w,
    out_grad,
):
    layers, vocab = query_w.shape[0], embed.shape[0]
    small = packed_small(embed, conv_weight, conv_bias, scorer, norm_attn, norm_ffn)
    if query_w.shape[1] % 8 == 0 and HEADS % lax.axis_size("ctx") == 0:
        step = fused_step
    else:
        step = separate_step
    encoded, small_out, wide_grads = step(
        lengths, byte_ids, small, query_w, key_w, value_w, attn_out_w, gate_w, up_w, down_w, out_grad[0], vocab
    )
    d_query, d_key, d_value, d_out, d_gate, d_up, d_down = wide_grads
    d_embed, d_conv, d_bias, d_scorer, d_norm_attn, d_norm_ffn = split_small(small_out.T, vocab, layers)
    return (encoded[None], d_embed, d_conv, d_bias, d_scorer, d_norm_attn, d_query, d_key, d_value, d_out, d_norm_ffn,
            d_gate, d_up, d_down)


def solution(mesh):
    placed = (
        P("dp", "ctx"),
        P("dp", None),
        P(None, ("dp", "ctx")),
        P(None, ("dp", "ctx")),
        P(("dp", "ctx")),
        P(("dp", "ctx")),
        P(None, ("dp", "ctx")),
        P(None, ("dp", "ctx"), None),
        P(None, ("dp", "ctx"), None),
        P(None, ("dp", "ctx"), None),
        P(None, ("dp", "ctx"), None),
        P(None, ("dp", "ctx")),
        P(None, ("dp", "ctx"), None),
        P(None, ("dp", "ctx"), None),
        P(None, ("dp", "ctx"), None),
        P("dp", "ctx", None),
    )
    return jax.shard_map(
        on_device,
        mesh=mesh,
        in_specs=placed,
        out_specs=(
            P("dp", "ctx", None),
            P(None, ("dp", "ctx")),
            P(None, ("dp", "ctx")),
            P(("dp", "ctx")),
            P(("dp", "ctx")),
            P(None, ("dp", "ctx")),
            P(None, ("dp", "ctx"), None),
            P(None, ("dp", "ctx"), None),
            P(None, ("dp", "ctx"), None),
            P(None, ("dp", "ctx"), None),
            P(None, ("dp", "ctx")),
            P(None, ("dp", "ctx"), None),
            P(None, ("dp", "ctx"), None),
            P(None, ("dp", "ctx"), None),
        ),
        check_vma=False,
    )
```

```python
import functools
import types
import jax
import jax.numpy as jnp
from jax import lax
from jax.experimental import pallas as pl
from jax.experimental.pallas import tpu as pltpu
from jax.sharding import PartitionSpec as P


MESH = pl.DeviceIdType.MESH
CORES = 2
LANES = 128
THIRD = 0.1
DEPTH = 2
SPLIT = 3
LAG = 1


def grid_of():
    dp, ctx = lax.axis_size("dp"), lax.axis_size("ctx")
    rows = 2 if ctx % 2 == 0 else 1
    return dp // CORES, rows, ctx // rows


def place_of():
    _, _, nx = grid_of()
    d, c = lax.axis_index("dp"), lax.axis_index("ctx")
    return d // CORES, d % CORES, c // nx, c % nx


def device(z, core, y, x):
    _, _, nx = grid_of()
    return (z * CORES + core, y * nx + x)


def along(axis):
    place = list(place_of())
    nz, ny, nx = grid_of()
    size = (nz, CORES, ny, nx)[axis]
    found = []
    for i in range(1, size):
        there = list(place)
        there[axis] = lax.rem(place[axis] + i, size)
        found.append((there[axis], device(*there)))
    return found


def sibling():
    z, core, y, x = place_of()
    return device(z, 1 - core, y, x)


def greet_all():
    barrier = pltpu.get_barrier_semaphore()
    targets = [target for axis in (0, 2, 3) for _, target in along(axis)] + [sibling()]
    _, ny, nx = grid_of()
    z, core, y, x = place_of()
    for i in range(1, ny):
        for j in range(1, nx):
            targets.append(device(z, core, lax.rem(y + i, ny), lax.rem(x + j, nx)))
    for target in targets:
        pl.semaphore_signal(barrier, inc=1, device_id=target, device_id_type=MESH)
    pl.semaphore_wait(barrier, len(targets))
    return targets


ORDERS = ((0, 3, 2), (0, 2, 3), (3, 2, 0))


def splits_of(width, count):
    units = width // LANES
    cuts = [units * i // count * LANES for i in range(count + 1)]
    return [(a, b - a) for a, b in zip(cuts, cuts[1:])]


def pieces_of(width, third, first=0):
    units = width // LANES
    last = int(units * third)
    left = (units - last + 1) // 2
    found, at = [], first // LANES
    for order, size in zip(ORDERS, (left, units - last - left, last)):
        if size:
            found.append((pl.ds(at * LANES, size * LANES), order))
        at += size
    return found


def hops(width, third):
    nz, ny, nx = grid_of()
    return len(pieces_of(width, third)) * (nz - 1 + ny - 1 + nx - 1) + 1


class Sender:
    def __init__(self, sems):
        self.sems, self.count, self.flying = sems, 0, []

    def send(self, src, dst, target):
        copy = pltpu.make_async_remote_copy(
            src_ref=src, dst_ref=dst, send_sem=self.sems.at[0, self.count], recv_sem=self.sems.at[1, self.count],
            device_id=target, device_id_type=MESH)
        copy.start()
        self.count += 1
        self.flying.append(copy)
        return copy

    def finish(self):
        for copy in self.flying:
            copy.wait_send()
        self.flying = []


class GatherChunk(Sender):
    phases = 4

    def __init__(self, shard, out, sems, local_sem, third):
        super().__init__(sems)
        self.shard, self.out, self.local_sem = shard, out, local_sem
        self.pieces = pieces_of(shard.shape[-1], third)
        self.waiting = []

    def stage(self, number):
        place = place_of()
        for copy in self.waiting:
            copy.wait_recv()
        self.waiting = []
        if number == 0:
            self.own = pltpu.make_async_copy(self.shard, self.out.at[place], self.local_sem)
            self.own.start()
        if number == 1:
            self.own.wait()
        if number < 3:
            for columns, order in self.pieces:
                have = order[:number]
                where = tuple(slice(None) if axis in have else place[axis] for axis in range(4)) + (slice(None), columns)
                src = self.out.at[where] if number else self.shard.at[:, columns]
                for _, target in along(order[number]):
                    self.waiting.append(self.send(src, self.out.at[where], target))
        else:
            where = (slice(None), place[1])
            self.waiting.append(self.send(self.out.at[where], self.out.at[where], sibling()))

    def arrive(self):
        for copy in self.waiting:
            copy.wait_recv()
        self.waiting = []


class Pipeline:
    def __init__(self, chunks):
        self.chunks, self.steps, self.done = chunks, [], [0] * len(chunks)
        phases = chunks[0].phases
        for t in range(len(chunks) + phases):
            for number in [0] + list(range(phases - 1, 0, -1)):
                if 0 <= t - number < len(chunks):
                    self.steps.append((t - number, number))

    def tick(self, count=1):
        for _ in range(count):
            if self.steps:
                i, number = self.steps.pop(0)
                self.chunks[i].stage(number)
                self.done[i] = number + 1

    def until(self, i):
        while self.done[i] < self.chunks[i].phases:
            self.tick()

    def need(self, i):
        self.until(i)
        self.chunks[i].arrive()


def gather_kernel(n, third, *refs):
    shards, outs, sems, local_sems = refs[:n], refs[n:2 * n], refs[2 * n:3 * n], refs[3 * n]
    greet_all()
    chunks = [GatherChunk(shards[i], outs[i], sems[i], local_sems.at[i], third) for i in range(n)]
    ticker = Pipeline(chunks)
    for i in range(n):
        ticker.need(i)
    for chunk in chunks:
        chunk.finish()


def gather_all(shards, collective_id, third=THIRD):
    nz, ny, nx = grid_of()
    n = len(shards)
    outs = pl.pallas_call(
        functools.partial(gather_kernel, n, third),
        out_shape=[jax.ShapeDtypeStruct((nz, CORES, ny, nx) + s.shape, s.dtype) for s in shards],
        in_specs=[pl.BlockSpec(memory_space=pl.ANY)] * n,
        out_specs=[pl.BlockSpec(memory_space=pl.ANY)] * n,
        scratch_shapes=[pltpu.SemaphoreType.DMA((2, hops(s.shape[-1], third))) for s in shards] + [pltpu.SemaphoreType.DMA((n,))],
        compiler_params=pltpu.CompilerParams(collective_id=collective_id, has_side_effects=True),
        name="gather_weights",
    )(*shards)
    return [o.reshape((-1,) + o.shape[5:]) for o in outs]


def add_into(dst, src, lead):
    if not lead:
        dst[...] = (dst[...].astype(jnp.float32) + src[...].astype(jnp.float32)).astype(dst.dtype)
        return

    def body(i, carry):
        add_into(dst.at[i], src.at[i], lead[1:])
        return carry
    lax.fori_loop(0, lead[0], body, 0)


class ScatterChunk(Sender):
    phases = 5

    def __init__(self, parts, out, scratch, sems, local_sem, third):
        super().__init__(sems)
        self.parts, self.out, self.local_sem = parts, out, local_sem
        self.held, self.across, *landing = scratch
        self.pieces = [(columns, order[::-1], landing[3 * i:3 * i + 3])
                       for i, (columns, order) in enumerate(pieces_of(parts.shape[-1], third))]
        self.waiting = []

    @staticmethod
    def scratch(shape, dtype, third):
        sizes = dict(zip((0, 2, 3), grid_of()))
        whole = (*sizes.values(), *shape)
        found = [whole, whole]
        for columns, order in pieces_of(shape[-1], third):
            order = order[::-1]
            for number in range(3):
                rest = [sizes[a] for a in sizes if a in order[number + 1:]]
                found.append((sizes[order[number]] - 1, *rest, shape[0], columns.size))
        return [pltpu.VMEM(s, dtype) for s in found]

    def stage(self, number):
        place = place_of()
        sizes = dict(zip((0, 2, 3), grid_of()))
        for copy in self.waiting:
            copy.wait_recv()
        self.waiting = []
        if number == 0:
            self.own = pltpu.make_async_copy(self.parts.at[:, place[1]], self.held, self.local_sem)
            self.own.start()
            self.waiting.append(self.send(self.parts.at[:, 1 - place[1]], self.across, sibling()))
            return
        if number == 1:
            self.own.wait()
            add_into(self.held, self.across, list(sizes.values()))
        for columns, order, landing in self.pieces:
            if number > 1:
                mine = order[:number - 1]
                where = tuple(place[a] if a in mine else slice(None) for a in sizes) + (slice(None), columns)
                lead = [sizes[a] for a in sizes if a not in mine]
                landed = landing[number - 2]
                if number < 4:
                    for i in range(landed.shape[0]):
                        add_into(self.held.at[where], landed.at[i], lead)
                else:
                    total = self.held[where].astype(jnp.float32)
                    for i in range(landed.shape[0]):
                        total = total + landed[i].astype(jnp.float32)
                    self.out[:, columns] = total
            if number < 4:
                axis, mine = order[number - 1], order[:number - 1]
                for i, (there, target) in enumerate(along(axis)):
                    where = tuple(there if a == axis else place[a] if a in mine else slice(None) for a in sizes)
                    src = self.held.at[where + (slice(None), columns)]
                    self.waiting.append(self.send(src, landing[number - 1].at[i], target))


def scatter_kernel(n, third, counts, *refs):
    parts, outs, rest = refs[:n], refs[n:2 * n], list(refs[2 * n:])
    greet_all()
    chunks = []
    for i in range(n):
        scratch = [rest.pop(0) for _ in range(counts[i])]
        chunks.append(ScatterChunk(parts[i], outs[i], scratch, rest.pop(0), rest.pop(0), third))
    ticker = Pipeline(chunks)
    for i in range(n):
        ticker.until(i)
    for chunk in chunks:
        chunk.finish()


def scatter_scratch(shape, dtype, third):
    scratch = ScatterChunk.scratch(shape, dtype, third)
    return scratch + [pltpu.SemaphoreType.DMA((2, hops(shape[-1], third))), pltpu.SemaphoreType.DMA]


def scatter_all(parts, collective_id, third=THIRD):
    nz, ny, nx = grid_of()
    n = len(parts)
    devices = nz * CORES * ny * nx
    parts = [p.reshape((nz, CORES, ny, nx, p.shape[0] // devices) + p.shape[1:]) for p in parts]
    scratch, counts = [], []
    for p in parts:
        made = scatter_scratch(p.shape[4:], p.dtype, third)
        counts.append(len(made) - 2)
        scratch += made
    return pl.pallas_call(
        functools.partial(scatter_kernel, n, third, counts),
        out_shape=[jax.ShapeDtypeStruct(p.shape[4:], jnp.float32) for p in parts],
        in_specs=[pl.BlockSpec(memory_space=pl.ANY)] * n,
        out_specs=[pl.BlockSpec(memory_space=pltpu.VMEM)] * n,
        scratch_shapes=scratch,
        compiler_params=pltpu.CompilerParams(collective_id=collective_id, has_side_effects=True, vmem_limit_bytes=60 << 20),
        name="scatter_grads",
    )(*parts)


HEADS = 12
HEAD_DIM = 64
CHUNK = 256
NORM_EPS = 1e-06
NEG_FILL = -1000000000.0
GELU_A = 0.7978845608028654
GELU_B = 0.044715


def dot(a, b):
    return jnp.dot(a, b, preferred_element_type=jnp.float32)


def dot_nt(a, b):
    return lax.dot_general(a, b, (((1,), (1,)), ((), ())), preferred_element_type=jnp.float32)


def low(v):
    return v.astype(jnp.bfloat16)


def flip(v):
    return low(v.astype(jnp.float32).T)


def inverse_rms(v):
    return lax.rsqrt(jnp.mean(v * v, -1, keepdims=True) + NORM_EPS)


def ends_of(lengths_ref):
    ends, total = [], 0
    for i in range(lengths_ref.shape[-1]):
        total = total + lengths_ref[0, i]
        ends.append(total)
    return ends


def segments(places, ends):
    seg = jnp.zeros(places.shape, jnp.int32)
    for end in ends:
        seg = seg + jnp.where(places >= end, 1, 0)
    return seg


def heads_each():
    return -(-HEADS // lax.axis_size("ctx"))


def others():
    size, me = lax.axis_size("ctx"), lax.axis_index("ctx")
    return [lax.rem(me + 1 + i, size) for i in range(size)]


def greet_group():
    barrier = pltpu.get_barrier_semaphore()
    peers_ = others()[:-1]
    for p in peers_:
        pl.semaphore_signal(barrier, inc=1, device_id=(lax.axis_index("dp"), p), device_id_type=MESH)
    pl.semaphore_wait(barrier, len(peers_))


def to_group(src, dst, sems, index, p):
    return pltpu.make_async_remote_copy(
        src_ref=src, dst_ref=dst, send_sem=sems.at[(0,) + index], recv_sem=sems.at[(1,) + index],
        device_id=(lax.axis_index("dp"), p), device_id_type=MESH)


def tokens_of(p, count):
    return pl.ds(pl.multiple_of(p * count, count), count)


def spread_heads(src, dst, sems, local_sem, each):
    me = lax.axis_index("ctx")
    count = src.shape[2]
    copies = []
    for h in range(each):
        rows = pl.ds(h * HEAD_DIM, HEAD_DIM)
        made = []
        for i, p in enumerate(others()):
            theirs = pl.ds(pl.multiple_of((p * each + h) * HEAD_DIM, HEAD_DIM), HEAD_DIM)
            a, b = src.at[:, theirs], dst.at[:, rows, tokens_of(me, count)]
            if i == lax.axis_size("ctx") - 1:
                copy = pltpu.make_async_copy(a, b, local_sem.at[h])
            else:
                copy = to_group(a, b, sems, (h, i), p)
            copy.start()
            made.append(copy)
        copies.append(made)
    return copies


def arrive(made):
    for copy in made[:-1]:
        copy.wait_recv()
    made[-1].wait()


def attention_forward(each, seg_all, ends, qkv, lse, out_send, att, qkv_copies, sems, tick=lambda: None):
    size, me = lax.axis_size("ctx"), lax.axis_index("ctx")
    count = att.shape[1]
    copies = []
    for h in range(each):
        arrive(qkv_copies[h])
        rows = pl.ds(h * HEAD_DIM, HEAD_DIM)
        key = flip(qkv[1, rows, :])
        value_t = qkv[2, rows, :]
        theirs = pl.ds(pl.multiple_of((me * each + h) * HEAD_DIM, HEAD_DIM), HEAD_DIM)
        for i, p in enumerate(others()):
            tokens = tokens_of(p, count)
            seg_q = segments(2 * (p * count + lax.broadcasted_iota(jnp.int32, (1, count), 1)), ends)
            scores = dot(key, qkv[0, rows, tokens])
            scores = jnp.where(seg_all[...] == seg_q, scores, NEG_FILL)
            top = jnp.max(scores, 0, keepdims=True)
            probs = jnp.exp(scores - top)
            total = jnp.sum(probs, 0, keepdims=True)
            lse[h, :, tokens] = top + jnp.log(total)
            result = low(dot(value_t, low(probs)) / total)
            if i == size - 1:
                att[theirs, :] = result
            else:
                out_send[h, i] = result
                copy = to_group(out_send.at[h, i], att.at[theirs], sems, (h, i), p)
                copy.start()
                copies.append(copy)
            tick()
    return copies


def gelu_parts(gate):
    inner = jnp.tanh(GELU_A * (gate + GELU_B * gate * gate * gate))
    half = 0.5 * (1.0 + inner)
    slope = half + 0.5 * gate * (1.0 - inner * inner) * GELU_A * (1.0 + 3.0 * GELU_B * gate * gate)
    return gate * half, slope


def layer_forward_kernel(lengths, x, gain_a, gain_f, w_attn_hbm, w_ffn_hbm, w_down_hbm,
                         out, middle, normed_t, qkv, lse, att, gate_out, up_out, nffn_t,
                         w_attn, w_ffn, w_down, qkv_all, out_send, seg_all, nffn,
                         sems_in, sems_out, local_sems, w_sems):
    each = heads_each()
    model = x.shape[1]
    loads = [pltpu.make_async_copy(a, b, w_sems.at[i]) for i, (a, b) in enumerate(
        ((w_attn_hbm, w_attn), (w_ffn_hbm, w_ffn), (w_down_hbm, w_down)))]
    for load in loads:
        load.start()
    greet_group()
    ends = ends_of(lengths)
    seg_all[...] = segments(2 * lax.broadcasted_iota(jnp.int32, seg_all.shape, 0), ends)
    stream = x[...]
    normed = low(stream * inverse_rms(stream) * gain_a[...])
    normed_t[...] = flip(normed)
    if qkv_all.shape[1] > model:
        qkv_all[:, model:, :] = jnp.zeros((3, qkv_all.shape[1] - model, qkv_all.shape[2]), jnp.bfloat16)
    loads[0].wait()
    for part in range(3):
        for c in range(model // CHUNK):
            columns = pl.ds(part * model + c * CHUNK, CHUNK)
            qkv_all[part, c * CHUNK:(c + 1) * CHUNK, :] = low(dot(normed, w_attn[:, columns]).T)
    qkv_copies = spread_heads(qkv_all, qkv, sems_in, local_sems, each)
    out_copies = attention_forward(each, seg_all, ends, qkv, lse, out_send, att, qkv_copies, sems_out)
    for copy in out_copies:
        copy.wait_recv()
    attended = flip(att[:model, :])
    mid = stream + dot(attended, w_attn[:, 3 * model:])
    middle[...] = mid
    after = low(mid * inverse_rms(mid) * gain_f[...])
    nffn[...] = after
    nffn_t[...] = flip(after)
    out[...] = mid
    loads[1].wait()
    loads[2].wait()
    hidden_count = w_down.shape[0]

    def step(c, carry):
        columns = pl.ds(pl.multiple_of(c * CHUNK, CHUNK), CHUNK)
        gate = dot(nffn[...], w_ffn[:, columns])
        up = dot(nffn[...], w_ffn[:, pl.ds(pl.multiple_of(hidden_count + c * CHUNK, CHUNK), CHUNK)])
        gate_out[:, columns] = gate
        up_out[:, columns] = up
        hidden = low(gelu_parts(gate)[0] * up)
        out[...] += dot(hidden, w_down[columns, :])
        return carry
    lax.fori_loop(0, hidden_count // CHUNK, step, 0)
    for made in qkv_copies:
        for copy in made[:-1]:
            copy.wait_send()
    for copy in out_copies:
        copy.wait_send()


VMEM = pl.BlockSpec(memory_space=pltpu.VMEM)
ANY = pl.BlockSpec(memory_space=pl.ANY)
SMEM = pl.BlockSpec(memory_space=pltpu.SMEM)


def layer_forward(lengths, x, gain_a, gain_f, w_attn, w_ffn, w_down, collective_id):
    size, each = lax.axis_size("ctx"), heads_each()
    count, model = x.shape
    wide = w_down.shape[0]
    group = count * size
    rows = each * size * HEAD_DIM
    f32, bf16 = jnp.float32, jnp.bfloat16
    made = lambda shape, dtype: jax.ShapeDtypeStruct(shape, dtype)
    return pl.pallas_call(
        layer_forward_kernel,
        out_shape=[made((count, model), f32), made((count, model), f32), made((model, count), bf16),
                   made((3, each * HEAD_DIM, group), bf16), made((each, 1, group), f32), made((rows, count), bf16),
                   made((count, wide), f32), made((count, wide), f32), made((model, count), bf16)],
        in_specs=[SMEM, VMEM, VMEM, VMEM, ANY, ANY, ANY],
        out_specs=[VMEM] * 9,
        scratch_shapes=[
            pltpu.VMEM(w_attn.shape, bf16), pltpu.VMEM(w_ffn.shape, bf16), pltpu.VMEM(w_down.shape, bf16),
            pltpu.VMEM((3, rows, count), bf16), pltpu.VMEM((each, size - 1, HEAD_DIM, count), bf16),
            pltpu.VMEM((group, count), jnp.int32), pltpu.VMEM((count, model), bf16),
            pltpu.SemaphoreType.DMA((2, each, size - 1)), pltpu.SemaphoreType.DMA((2, each, size - 1)),
            pltpu.SemaphoreType.DMA((each,)), pltpu.SemaphoreType.DMA((3,))],
        compiler_params=pltpu.CompilerParams(collective_id=collective_id, has_side_effects=True, vmem_limit_bytes=56 << 20),
        name="layer_forward",
    )(lengths, x, gain_a, gain_f, w_attn, w_ffn, w_down)


def layer_backward_kernel(lengths, grad, x, gain_a, gain_f, middle, normed_t, qkv, lse, att, gate_in, up_in, nffn_t,
                          w_attn_hbm, w_ffn_hbm, w_down_hbm,
                          grad_in, d_gain_a, d_gain_f, d_attn_hbm, d_ffn_hbm, d_down_hbm,
                          w_attn, w_ffn, w_down, d_attn, d_ffn, d_down, go_all, go, dqkv, q_send, kv_send, seg_all, total,
                          grad_low, mid_low, sems_in, sems_q, sems_kv, local_sems, w_sems, d_sems):
    each = heads_each()
    size, me = lax.axis_size("ctx"), lax.axis_index("ctx")
    count, model = x.shape
    wide = w_down.shape[0]
    loads = [pltpu.make_async_copy(a, b, w_sems.at[i]) for i, (a, b) in enumerate(
        ((w_down_hbm, w_down), (w_ffn_hbm, w_ffn), (w_attn_hbm, w_attn)))]
    for load in loads:
        load.start()
    greet_group()
    ends = ends_of(lengths)
    seg_all[...] = segments(2 * lax.broadcasted_iota(jnp.int32, seg_all.shape, 0), ends)
    grad_low[...] = low(grad[...])
    total[...] = jnp.zeros(total.shape, jnp.float32)
    loads[0].wait()
    loads[1].wait()

    def step(c, carry):
        columns = pl.ds(pl.multiple_of(c * CHUNK, CHUNK), CHUNK)
        later = pl.ds(pl.multiple_of(wide + c * CHUNK, CHUNK), CHUNK)
        g_hidden = dot_nt(grad_low[...], w_down[columns, :])
        up = up_in[:, columns]
        act, slope = gelu_parts(gate_in[:, columns])
        g_gate = low(g_hidden * up * slope)
        g_up = low(g_hidden * act)
        d_down[columns, :] = low(dot(low((act * up).T), grad_low[...]))
        d_ffn[:, columns] = low(dot(nffn_t[...], g_gate))
        d_ffn[:, later] = low(dot(nffn_t[...], g_up))
        total[...] += dot_nt(g_gate, w_ffn[:, columns]) + dot_nt(g_up, w_ffn[:, later])
        return carry
    lax.fori_loop(0, wide // CHUNK, step, 0)
    saves = [pltpu.make_async_copy(d_ffn, d_ffn_hbm, d_sems.at[0]), pltpu.make_async_copy(d_down, d_down_hbm, d_sems.at[1])]
    for save in saves:
        save.start()

    def norm_back(values, gain, upstream):
        scale = inverse_rms(values)
        scaled = upstream * gain
        along = jnp.mean(values * scaled, -1, keepdims=True)
        return scale * scaled - values * (scale * scale * scale * along), jnp.sum(upstream * values * scale, 0, keepdims=True)

    back, d_gain = norm_back(middle[...], gain_f[...], total[...])
    d_gain_f[...] = d_gain
    grad_in[...] = grad[...] + back
    mid_low[...] = low(grad_in[...])
    if go_all.shape[1] > model:
        go_all[:, model:, :] = jnp.zeros((1, go_all.shape[1] - model, count), jnp.bfloat16)
    loads[2].wait()
    for c in range(model // CHUNK):
        rows = slice(c * CHUNK, (c + 1) * CHUNK)
        go_all[0, rows, :] = low(dot_nt(mid_low[...], w_attn[rows, 3 * model:]).T)
    go_copies = spread_heads(go_all, go, sems_in, local_sems, each)
    for c in range(model // CHUNK):
        rows = slice(c * CHUNK, (c + 1) * CHUNK)
        d_attn[rows, 3 * model:] = low(dot(att[rows, :], mid_low[...]))
    sent = []
    for h in range(each):
        arrive(go_copies[h])
        rows = pl.ds(h * HEAD_DIM, HEAD_DIM)
        theirs = pl.ds(pl.multiple_of((me * each + h) * HEAD_DIM, HEAD_DIM), HEAD_DIM)
        key_t = qkv[1, rows, :]
        key, value = flip(key_t), flip(qkv[2, rows, :])
        g_key = jnp.zeros((HEAD_DIM, count * size), jnp.float32)
        g_value = jnp.zeros((HEAD_DIM, count * size), jnp.float32)
        for i, p in enumerate(others()):
            tokens = tokens_of(p, count)
            seg_q = segments(2 * (p * count + lax.broadcasted_iota(jnp.int32, (1, count), 1)), ends)
            query_t, go_t = qkv[0, rows, tokens], go[0, rows, tokens]
            scores = jnp.where(seg_all[...] == seg_q, dot(key, query_t), NEG_FILL)
            probs = jnp.exp(scores - lse[h, :, tokens])
            g_probs = dot(value, go_t)
            inner = jnp.sum(probs * g_probs, 0, keepdims=True)
            g_scores = low(probs * (g_probs - inner))
            g_query = low(dot(key_t, g_scores))
            g_key = g_key + dot_nt(query_t, g_scores)
            g_value = g_value + dot_nt(go_t, low(probs))
            if i == size - 1:
                dqkv[0, theirs, :] = g_query
            else:
                q_send[h, i] = g_query
                copy = to_group(q_send.at[h, i], dqkv.at[0, theirs], sems_q, (h, i), p)
                copy.start()
                sent.append(copy)
        kv_send[h, 0] = low(g_key)
        kv_send[h, 1] = low(g_value)
        for i, p in enumerate(others()):
            if i == size - 1:
                dqkv[1:, theirs, :] = kv_send[h, :, :, tokens_of(me, count)]
            else:
                copy = to_group(kv_send.at[h, :, :, tokens_of(p, count)], dqkv.at[pl.ds(1, 2), theirs], sems_kv, (h, i), p)
                copy.start()
                sent.append(copy)
    for copy in sent:
        copy.wait_recv()
    summed = jnp.zeros((model, count), jnp.float32)
    for part in range(3):
        for c in range(model // CHUNK):
            rows = slice(c * CHUNK, (c + 1) * CHUNK)
            columns = slice(part * model + c * CHUNK, part * model + (c + 1) * CHUNK)
            d_attn[:, columns] = low(dot_nt(normed_t[...], dqkv[part, rows, :]))
        summed = summed + dot(w_attn[:, part * model:(part + 1) * model], dqkv[part, :model, :])
    saves.append(pltpu.make_async_copy(d_attn, d_attn_hbm, d_sems.at[2]))
    saves[-1].start()
    back, d_gain = norm_back(x[...], gain_a[...], summed.T)
    d_gain_a[...] = d_gain
    grad_in[...] += back
    for made in go_copies:
        for copy in made[:-1]:
            copy.wait_send()
    for copy in sent:
        copy.wait_send()
    for save in saves:
        save.wait()


def layer_backward(lengths, grad, x, gain_a, gain_f, kept, w_attn, w_ffn, w_down, collective_id):
    size, each = lax.axis_size("ctx"), heads_each()
    count, model = x.shape
    wide = w_down.shape[0]
    group = count * size
    rows = each * size * HEAD_DIM
    f32, bf16 = jnp.float32, jnp.bfloat16
    made = lambda shape, dtype: jax.ShapeDtypeStruct(shape, dtype)
    return pl.pallas_call(
        layer_backward_kernel,
        out_shape=[made((count, model), f32), made((1, model), f32), made((1, model), f32),
                   made(w_attn.shape, bf16), made(w_ffn.shape, bf16), made(w_down.shape, bf16)],
        in_specs=[SMEM] + [VMEM] * 12 + [ANY] * 3,
        out_specs=[VMEM] * 3 + [ANY] * 3,
        scratch_shapes=[
            pltpu.VMEM(w_attn.shape, bf16), pltpu.VMEM(w_ffn.shape, bf16), pltpu.VMEM(w_down.shape, bf16),
            pltpu.VMEM(w_attn.shape, bf16), pltpu.VMEM(w_ffn.shape, bf16), pltpu.VMEM(w_down.shape, bf16),
            pltpu.VMEM((1, rows, count), bf16), pltpu.VMEM((1, each * HEAD_DIM, group), bf16),
            pltpu.VMEM((3, rows, count), bf16), pltpu.VMEM((each, size - 1, HEAD_DIM, count), bf16),
            pltpu.VMEM((each, 2, HEAD_DIM, group), bf16), pltpu.VMEM((group, count), jnp.int32),
            pltpu.VMEM((count, model), f32), pltpu.VMEM((count, model), bf16), pltpu.VMEM((count, model), bf16),
            pltpu.SemaphoreType.DMA((2, each, size - 1)), pltpu.SemaphoreType.DMA((2, each, size - 1)),
            pltpu.SemaphoreType.DMA((2, each, size - 1)), pltpu.SemaphoreType.DMA((each,)),
            pltpu.SemaphoreType.DMA((3,)), pltpu.SemaphoreType.DMA((3,))],
        compiler_params=pltpu.CompilerParams(collective_id=collective_id, has_side_effects=True, vmem_limit_bytes=60 << 20),
        name="layer_backward",
    )(lengths, grad, x, gain_a, gain_f, *kept, w_attn, w_ffn, w_down)


CONV = 4
BLOCKS = (1, 2, 3, 4)
HALO = 64


def halves_of(v):
    high = low(v)
    return high, low(v - high.astype(jnp.float32))


def dot_split(a, b):
    high, rest = halves_of(a)
    return dot(high, b) + dot(rest, b)


def dot_wide(a, b):
    (ah, al), (bh, bl) = halves_of(a), halves_of(b)
    return dot(ah, bh) + dot(ah, bl) + dot(al, bh)


def block_starts(places, ends):
    start = jnp.zeros(places.shape, jnp.int32)
    for end in ends:
        start = jnp.where(places >= end, end, start)
    rel = places - start
    found = []
    for size in BLOCKS:
        if size & (size - 1) == 0:
            found.append(places - (rel & (size - 1)))
        else:
            count = jnp.floor((rel.astype(jnp.float32) + 0.5) * (1.0 / size)).astype(jnp.int32)
            found.append(start + count * size)
    return found


def valid_of(places, ends):
    return (places >= 0) & (places < ends[-1])


def tap_ids(ids, first, span, ends):
    places = first - HALO + lax.broadcasted_iota(jnp.int32, (1, span), 1)
    own = segments(places, ends)
    count = ids.shape[1] // 3
    rows = []
    for tap in range(CONV):
        theirs = places + (tap - 1)
        at = count - HALO + tap - 1
        near = ids[:, at - at % 128:at - at % 128 + span + 128]
        near = lax.slice_in_dim(near, at % 128, at % 128 + span, axis=1)
        use = valid_of(places, ends) & valid_of(theirs, ends) & (segments(theirs, ends) == own)
        rows.append(jnp.where(use, near, -1))
    return rows, valid_of(places, ends)


def one_hot(row, vocab):
    return low(jnp.where(lax.broadcasted_iota(jnp.int32, (vocab, row.shape[1]), 0) == row, 1.0, 0.0))


def mix_blocks(first, span, tokens, ends):
    keys = block_starts(first - HALO + lax.broadcasted_iota(jnp.int32, (span, tokens), 0), ends)
    found = []
    for parity in range(2):
        own = block_starts(first + 2 * lax.broadcasted_iota(jnp.int32, (1, tokens), 1) + parity, ends)
        found.append([key == mine for key, mine in zip(keys, own)])
    return found


def gbst_forward(ends, ids, first, small, conv, choice, vocab, tokens, tick=lambda: None):
    span = conv.shape[1]
    taps, valid = tap_ids(ids, first, span, ends)
    table = small[:, :vocab]
    at = vocab + CONV
    total = small[:, at:at + 1] * jnp.where(valid, 1.0, 0.0)
    for tap in range(CONV):
        total = total + dot_split(table * small[:, vocab + tap:vocab + tap + 1], one_hot(taps[tap], vocab))
        tick()
    conv[...] = total
    scored = jnp.sum(total * small[:, at + 1:at + 2], 0, keepdims=True)
    scored = jnp.broadcast_to(scored, (8, span))
    parts = []
    for _ in range(3):
        parts.append(low(scored))
        scored = scored - parts[-1].astype(jnp.float32)
    mix = jnp.zeros((span, tokens), jnp.float32)
    for parity, blocks in enumerate(mix_blocks(first, span, tokens, ends)):
        logits = []
        for size, block in zip(BLOCKS, blocks):
            ones = low(jnp.where(block, 1.0, 0.0))
            logits.append((dot(parts[0], ones) + dot(parts[1], ones) + dot(parts[2], ones))[:1] * (1.0 / size))
        top = functools.reduce(jnp.maximum, logits)
        raised = [jnp.exp(v - top) for v in logits]
        whole = functools.reduce(jnp.add, raised)
        for i, (size, block) in enumerate(zip(BLOCKS, blocks)):
            chosen = raised[i] / whole
            choice[len(BLOCKS) * parity + i:len(BLOCKS) * parity + i + 1, :] = chosen
            mix = mix + jnp.where(block, chosen * (0.5 / size), 0.0)
        tick()
    return dot_wide(total, mix)


def gbst_backward(ends, ids, first, small, conv, choice, grad_t, vocab, out, tick=lambda: None):
    span, tokens = conv.shape[1], grad_t.shape[1]
    taps, valid = tap_ids(ids, first, span, ends)
    at = vocab + CONV
    total = conv[...]
    along = dot_wide(total.T, grad_t)
    mix = jnp.zeros((span, tokens), jnp.float32)
    scored = jnp.zeros((span, tokens), jnp.float32)
    for parity, blocks in enumerate(mix_blocks(first, span, tokens, ends)):
        chosen = [choice[len(BLOCKS) * parity + i:len(BLOCKS) * parity + i + 1, :] for i in range(len(BLOCKS))]
        grads = [jnp.sum(jnp.where(block, along, 0.0), 0, keepdims=True) * (0.5 / size) for size, block in zip(BLOCKS, blocks)]
        inner = functools.reduce(jnp.add, [c * g for c, g in zip(chosen, grads)])
        for i, (size, block) in enumerate(zip(BLOCKS, blocks)):
            mix = mix + jnp.where(block, chosen[i] * (0.5 / size), 0.0)
            scored = scored + jnp.where(block, chosen[i] * (grads[i] - inner) * (1.0 / size), 0.0)
    g_scored = jnp.sum(scored.T, 0, keepdims=True)
    g_conv = dot_wide(grad_t, mix.T) + small[:, at + 1:at + 2] * g_scored
    out[:, at + 1:at + 2] = jnp.sum(total * g_scored, 1, keepdims=True)
    g_conv = g_conv * jnp.where(valid, 1.0, 0.0)
    out[:, at:at + 1] = jnp.sum(g_conv, 1, keepdims=True)
    high, rest = halves_of(g_conv)
    table = small[:, :vocab]
    g_table = jnp.zeros(table.shape, jnp.float32)
    for tap in range(CONV):
        hot = one_hot(taps[tap], vocab)
        g_tap = dot_nt(high, hot) + dot_nt(rest, hot)
        g_table = g_table + g_tap * small[:, vocab + tap:vocab + tap + 1]
        out[:, vocab + tap:vocab + tap + 1] = jnp.sum(g_tap * table, 1, keepdims=True)
        tick()
    out[:, :vocab] = g_table


def gbst_forward_kernel(vocab, tokens, lengths, ids, small, out, conv, choice):
    ends = ends_of(lengths)
    first = lax.axis_index("ctx") * 2 * tokens
    out[...] = gbst_forward(ends, ids, first, small, conv, choice, vocab, tokens).T


def gbst_backward_kernel(vocab, lengths, ids, small, conv, choice, grad, out):
    ends = ends_of(lengths)
    first = lax.axis_index("ctx") * 2 * grad.shape[0]
    out[...] = jnp.zeros(out.shape, jnp.float32)
    gbst_backward(ends, ids, first, small, conv, choice, grad[...].T, vocab, out)


class Gather(Sender):
    phases = 4

    def __init__(self, sources, out, sems, local_sems, first=0, width=None):
        super().__init__(sems)
        self.out = out
        self.columns = pl.ds(first, width or out.shape[-1])
        self.pieces = pieces_of(self.columns.size, THIRD, first)
        self.waiting = []
        self.own = []
        for i, (source, at) in enumerate(sources):
            a, b = max(first, at), min(first + (width or out.shape[-1]), at + source.shape[-1])
            if a < b:
                there = out.at[place_of() + (slice(None), pl.ds(a, b - a))]
                copy = pltpu.make_async_copy(source.at[:, pl.ds(a - at, b - a)], there, local_sems.at[i])
                copy.start()
                self.own.append(copy)

    def stage(self, number):
        place = place_of()
        self.arrive()
        if number == 0:
            for copy in self.own:
                copy.wait()
        if number < 3:
            for columns, order in self.pieces:
                have = order[:number]
                where = tuple(slice(None) if axis in have else place[axis] for axis in range(4)) + (slice(None), columns)
                for _, target in along(order[number]):
                    self.waiting.append(self.send(self.out.at[where], self.out.at[where], target))
        else:
            where = (slice(None), place[1]) + (slice(None),) * 3 + (self.columns,)
            self.waiting.append(self.send(self.out.at[where], self.out.at[where], sibling()))

    def arrive(self):
        for copy in self.waiting:
            copy.wait_recv()
        self.waiting = []


class GatherHeads(Sender):
    phases = 3

    def __init__(self, shard, out, sems, local_sem):
        super().__init__(sems)
        self.shard, self.out = shard, out
        self.waiting = []
        self.own = pltpu.make_async_copy(shard.at[lax.axis_index("ctx")], out.at[place_of()], local_sem)
        self.own.start()

    def stage(self, number):
        z, core, y, x = place_of()
        self.arrive()
        if number == 0:
            for p in others()[:-1]:
                target = (lax.axis_index("dp"), p)
                self.waiting.append(self.send(self.shard.at[p], self.out.at[z, core, y, x], target))
        elif number == 1:
            self.own.wait()
            for _, target in along(0):
                self.waiting.append(self.send(self.out.at[z, core], self.out.at[z, core], target))
        else:
            where = (slice(None), core)
            self.waiting.append(self.send(self.out.at[where], self.out.at[where], sibling()))

    arrive = Gather.arrive


class Ticker:
    def __init__(self):
        self.chunks, self.steps = [], []

    def pipeline(self, chunks):
        self.chunks = chunks
        self.done = [0] * len(chunks)
        for t in range(len(chunks) + 4 * DEPTH):
            for number in (0, 3, 2, 1):
                i = t - DEPTH * number
                if 0 <= i < len(chunks) and number < chunks[i].phases:
                    self.steps.append((i, number))

    def tick(self, count=1):
        for _ in range(count):
            if self.steps:
                i, number = self.steps.pop(0)
                self.chunks[i].stage(number)
                self.done[i] = number + 1

    def need(self, i):
        while self.done[i] < self.chunks[i].phases:
            self.tick()
        self.chunks[i].arrive()


class Scatter(Sender):
    phases = 5

    def __init__(self, parts, emit, scratch, sems, local_sem, before=None, credit=None, final=True, first=0):
        super().__init__(sems)
        self.parts, self.emit, self.local_sem, self.first = parts, emit, local_sem, first
        self.held, self.across, *landing = scratch
        self.pieces = [(columns, order[::-1], landing[3 * i:3 * i + 3])
                       for i, (columns, order) in enumerate(pieces_of(self.held.shape[-1], THIRD))]
        self.waiting, self.before, self.credit, self.final = [], before, credit, final

    @staticmethod
    def scratch(shape, dtype):
        sizes = dict(zip((0, 2, 3), grid_of()))
        whole = (*sizes.values(), *shape)
        found = [whole, whole]
        for columns, order in pieces_of(shape[-1], THIRD):
            order = order[::-1]
            for number in range(3):
                rest = [sizes[a] for a in sizes if a in order[number + 1:]]
                found.append((sizes[order[number]] - 1, *rest, shape[0], columns.size))
        return [pltpu.VMEM(s, dtype) for s in found]

    def targets(self):
        return [target for axis in (0, 2, 3) for _, target in along(axis)] + [sibling()]

    def open(self):
        if self.before is not None:
            self.before.finish()
            pl.semaphore_wait(self.credit, len(self.targets()))

    def close(self):
        if not self.final:
            for target in self.targets():
                pl.semaphore_signal(self.credit, inc=1, device_id=target, device_id_type=MESH)

    arrive = Gather.arrive

    def stage(self, number):
        place = place_of()
        sizes = dict(zip((0, 2, 3), grid_of()))
        self.arrive()
        if number == 0:
            self.open()
            columns = (slice(None),) * 3 + (pl.ds(self.first, self.held.shape[-1]),)
            self.own = pltpu.make_async_copy(self.parts.at[(slice(None), place[1]) + columns], self.held, self.local_sem)
            self.own.start()
            self.waiting.append(self.send(self.parts.at[(slice(None), 1 - place[1]) + columns], self.across, sibling()))
            return
        if number == 1:
            self.own.wait()
            add_into(self.held, self.across, list(sizes.values()))
        for columns, order, landing in self.pieces:
            if number > 1:
                mine = order[:number - 1]
                where = tuple(place[a] if a in mine else slice(None) for a in sizes) + (slice(None), columns)
                lead = [sizes[a] for a in sizes if a not in mine]
                landed = landing[number - 2]
                if number < 4:
                    for i in range(landed.shape[0]):
                        add_into(self.held.at[where], landed.at[i], lead)
                else:
                    total = self.held[where].astype(jnp.float32)
                    for i in range(landed.shape[0]):
                        total = total + landed[i].astype(jnp.float32)
                    self.emit(pl.ds(self.first + columns.start, columns.size), total)
            if number < 4:
                axis, mine = order[number - 1], order[:number - 1]
                for i, (there, target) in enumerate(along(axis)):
                    where = tuple(there if a == axis else place[a] if a in mine else slice(None) for a in sizes)
                    src = self.held.at[where + (slice(None), columns)]
                    self.waiting.append(self.send(src, landing[number - 1].at[i], target))
        if number == 4:
            self.close()


class ScatterHeads(Scatter):
    phases = 4

    def __init__(self, parts, out, scratch, sems, local_sem, before=None, credit=None, final=True):
        Sender.__init__(self, sems)
        self.parts, self.out, self.local_sem = parts, out, local_sem
        self.across, self.landed, self.sums = scratch
        self.waiting, self.before, self.credit, self.final = [], before, credit, final

    def targets(self):
        return [target for _, target in along(0)] + [sibling()]

    def stage(self, number):
        nz, ny, nx = grid_of()
        z, core, y, x = place_of()
        me = lax.axis_index("ctx")
        self.arrive()
        if number == 0:
            if self.before is not None:
                pl.semaphore_wait(self.credit, len(self.targets()))
            self.waiting.append(self.send(self.parts.at[:, 1 - core], self.across, sibling()))
        elif number == 1:
            add_into(self.parts.at[:, core], self.across, [nz, ny, nx])
            for i, (there, target) in enumerate(along(0)):
                self.waiting.append(self.send(self.parts.at[there, core], self.landed.at[i], target))
        elif number == 2:
            for j in range(ny):
                for k in range(nx):
                    total = self.parts[z, core, j, k].astype(jnp.float32)
                    for i in range(nz - 1):
                        total = total + self.landed[i, j, k].astype(jnp.float32)
                    self.sums[j * nx + k] = total
            self.close()
            for p in others()[:-1]:
                self.waiting.append(self.send(self.sums.at[p], self.out.at[me], (lax.axis_index("dp"), p)))
            self.own = pltpu.make_async_copy(self.sums.at[me], self.out.at[me], self.local_sem)
            self.own.start()

    def finish(self):
        self.arrive()
        for copy in self.flying:
            copy.wait_send()
        self.flying = []
        if self.own is not None:
            self.own.wait()
        self.own = None


class Rota:
    def __init__(self):
        self.queue, self.count = [], 0

    def add(self, chunk):
        chunk.stage(0)
        self.queue.append([LAG + self.count, chunk, 1])
        self.count += 1

    def tick(self, count=1):
        for _ in range(count):
            if not self.queue:
                return
            item = min(self.queue, key=lambda found: found[0])
            item[1].stage(item[2])
            item[0] += LAG
            item[2] += 1
            if item[2] == item[1].phases:
                self.queue.remove(item)

    def close(self, chunk):
        while any(item[1] is chunk for item in self.queue):
            self.tick()


def run_kernel(body, inputs, outputs, scratch, collective_id, name):
    def leaves(value):
        return [v for part in value for v in leaves(part)] if isinstance(value, list) else [value]

    def again(value, refs):
        return [again(v, refs) for v in value] if isinstance(value, list) else next(refs)

    def flat(group):
        return leaves(list(group.values()))

    def rebuilt(group, refs):
        return {k: again(value, refs) for k, value in group.items()}

    def kernel(*refs):
        refs = iter(refs)
        body(types.SimpleNamespace(**rebuilt(inputs, refs), **rebuilt(outputs, refs), **rebuilt(scratch, refs)))
    found = pl.pallas_call(
        kernel,
        out_shape=[s for s, _ in flat(outputs)],
        in_specs=[s for _, s in flat(inputs)],
        out_specs=[s for _, s in flat(outputs)],
        scratch_shapes=flat(scratch),
        compiler_params=pltpu.CompilerParams(collective_id=collective_id, has_side_effects=True, vmem_limit_bytes=60 << 20),
        name=name,
    )(*[a for a, _ in flat(inputs)])
    return types.SimpleNamespace(**rebuilt(outputs, iter(found)))


class Keep:
    def __init__(self, sems):
        self.sems, self.count, self.flying = sems, 0, []

    def __call__(self, src, dst):
        copy = pltpu.make_async_copy(src, dst, self.sems.at[self.count])
        copy.start()
        self.count += 1
        self.flying.append(copy)
        return copy

    def finish(self):
        for copy in self.flying:
            copy.wait()


def unpack(blocks, dst):
    nz, cores, ny, nx, rows, width = blocks.shape
    each = ny * nx * rows
    part = next(p for p in (512, 256, 128) if width % p == 0)

    def body(i, carry):
        for c in range(width // part):
            columns = slice(c * part, (c + 1) * part)
            found = [blocks[i // cores, i % cores, y, x, :, columns].astype(jnp.float32) for y in range(ny) for x in range(nx)]
            dst[pl.ds(pl.multiple_of(i * each, each), each), columns] = low(jnp.concatenate(found, 0))
        return carry
    lax.fori_loop(0, nz * cores, body, 0)


def to_blocks(dst, columns, values):
    nz, cores, ny, nx, rows, _ = dst.shape
    for b in range(nz * cores * ny * nx):
        g, k = divmod(b, ny * nx)
        dst[g // cores, g % cores, k // nx, k % nx, :, columns] = low(values[b * rows:(b + 1) * rows])


def norm_back(values, gain, upstream):
    scale = inverse_rms(values)
    scaled = upstream * gain
    mean = jnp.mean(values * scaled, -1, keepdims=True)
    return scale * scaled - values * (scale * scale * scale * mean), jnp.sum(upstream * values * scale, 0, keepdims=True)


def from_slot(i):
    size, me = lax.axis_size("ctx"), lax.axis_index("ctx")
    return lax.rem(me + size - 1 - i, size)


def gain_rows(small, vocab, layers):
    at = vocab + CONV + 2
    rows = small[:, at // LANES * LANES:].T
    at = at % LANES
    return [rows[at + l:at + l + 1, :] for l in range(2 * layers)]


def head_columns(query_w, key_w, value_w, dst):
    layers, size, rows, width = dst.shape
    each = query_w.shape[2] // size
    rest = [jnp.zeros((rows, width - 3 * each), jnp.float32)] if width > 3 * each else []
    for l in range(layers):
        whole = [w[l].astype(jnp.float32) for w in (query_w, key_w, value_w)]
        for p in range(size):
            dst[l, p] = low(jnp.concatenate([w[:, p * each:(p + 1) * each] for w in whole] + rest, 1))


def forward_body(vocab, layers, r):
    ends = ends_of(r.lengths)
    size, me = lax.axis_size("ctx"), lax.axis_index("ctx")
    each = heads_each()
    base = each * HEAD_DIM
    keep = Keep(r.keep_sems)
    greet_all()
    ids, count = r.ids, r.byte_ids.shape[1]
    near = []
    for i, (there, at) in enumerate(((lax.rem(me + 1, size), 0), (lax.rem(me + size - 1, size), 2))):
        copy = to_group(r.byte_ids, ids.at[:, pl.ds(at * count, count)], r.ids_sems, (i,), there)
        copy.start()
        near.append(copy)
    ids[:, count:2 * count] = r.byte_ids[...]
    head_columns(r.query_w, r.key_w, r.value_w, r.heads_w)
    chunks = [Gather([(r.small, 0)], r.full_small, r.small_sems, r.local_sems.at[0])]
    model = r.encoded.shape[1]
    wide = r.gate_w.shape[2]
    for l in range(layers):
        chunks.append(GatherHeads(r.heads_w.at[l], r.full_heads[l], r.heads_sems.at[l], r.more_sems.at[l, 1]))
        sources = [(r.gate_w.at[l], 0), (r.up_w.at[l], wide), (r.out_w.at[l], 2 * wide)]
        for k, (at, part) in enumerate(splits_of(r.full_ffn[l].shape[-1], SPLIT)):
            chunks.append(Gather(sources, r.full_ffn[l], r.ffn_sems.at[l, k], r.local_sems.at[1 + l * SPLIT + k], at, part))
        chunks.append(Gather([(r.down_w.at[l], 0)], r.full_down[l], r.down_sems.at[l], r.more_sems.at[l]))
    ticker = Ticker()
    ticker.pipeline(chunks)
    tick = ticker.tick
    tick(2)
    tokens = count // 2
    seg_all = r.seg_all
    seg_all[...] = segments(2 * lax.broadcasted_iota(jnp.int32, seg_all.shape, 0), ends)
    for copy in near:
        copy.wait_recv()
    ticker.need(0)
    small = r.small_wide
    nz, cores, ny, nx, rows, _ = r.full_small.shape
    for b in range(nz * cores * ny * nx):
        place = (b // (cores * ny * nx), b // (ny * nx) % cores, b // nx % ny, b % nx)
        small[b * rows:(b + 1) * rows, :] = r.full_small[place].astype(jnp.float32)
    tick()
    stream = gbst_forward(ends, ids[...], me * count, small[...], r.conv, r.choice, vocab, tokens, tick).T
    gains = gain_rows(small, vocab, layers)
    keep(r.conv, r.out_conv)
    for l in range(layers):
        base_chunk = 1 + (2 + SPLIT) * l
        nrm, qkv, att = r.nrm[l], r.qkv[l], r.att[l]
        r.x[l][...] = stream
        r.mine[...] = flip(low(stream * inverse_rms(stream) * gains[l]))
        spread = []
        for i, p in enumerate(others()[:-1]):
            copy = to_group(r.mine, nrm.at[:, tokens_of(me, tokens)], r.nrm_sems.at[l], (i,), p)
            copy.start()
            spread.append(copy)
        nrm[:, tokens_of(me, tokens)] = r.mine[...]
        keep(r.x[l], r.out_x[l])
        ticker.need(base_chunk)
        unpack(r.full_heads[l], r.w_heads[l])
        keep(r.w_heads[l], r.out_w_heads[l])
        r.w_turned[...] = flip(r.w_heads[l][...])
        for i in range(-1, size - 1):
            if i >= 0:
                spread[i].wait_recv()
            theirs = tokens_of(me if i < 0 else from_slot(i), tokens)
            qkv[:, theirs] = low(dot(r.w_turned[...], nrm[:, theirs]))
            tick()
        keep(nrm, r.out_nrm[l])
        keep(qkv, r.out_qkv[l])
        copies = []
        for h in range(each):
            query = pl.ds(h * HEAD_DIM, HEAD_DIM)
            key = flip(qkv[base + h * HEAD_DIM:base + (h + 1) * HEAD_DIM, :])
            value_t = qkv[2 * base + h * HEAD_DIM:2 * base + (h + 1) * HEAD_DIM, :]
            rows = pl.ds(pl.multiple_of((me * each + h) * HEAD_DIM, HEAD_DIM), HEAD_DIM)
            for i, p in enumerate(others()):
                theirs = tokens_of(p, tokens)
                seg_q = segments(2 * (p * tokens + lax.broadcasted_iota(jnp.int32, (1, tokens), 1)), ends)
                scores = jnp.where(seg_all[...] == seg_q, dot(key, qkv[query, theirs]), NEG_FILL)
                top = jnp.max(scores, 0, keepdims=True)
                probs = jnp.exp(scores - top)
                total = jnp.sum(probs, 0, keepdims=True)
                r.lse[l][h, :, theirs] = top + jnp.log(total)
                result = low(dot(value_t, low(probs)) / total)
                if i == size - 1:
                    att[rows, :] = result
                else:
                    r.att_send[h, i] = result
                    copy = to_group(r.att_send.at[h, i], att.at[rows], r.att_sems.at[l], (h, i), p)
                    copy.start()
                    copies.append(copy)
                tick(i != 3)
        keep(r.lse[l], r.out_lse[l])
        held = None
        for k, (at, width) in enumerate(splits_of(r.w_ffn.shape[1], SPLIT)):
            ticker.need(base_chunk + 1 + k)
            columns = pl.ds(at, width)
            part_of = (slice(None),) * 5 + (columns,)
            load = pltpu.make_async_copy(r.full_ffn[l].at[part_of], r.blocks.at[part_of], r.load_sems.at[l, 1 + k])
            load.start()
            if held is not None:
                held[0].wait()
                unpack(r.blocks.at[held[1]], r.w_ffn.at[:, held[2]])
            held = (load, part_of, columns)
        tick()
        held[0].wait()
        unpack(r.blocks.at[held[1]], r.w_ffn.at[:, held[2]])
        for copy in copies:
            copy.wait_recv()
        keep(att, r.out_att[l])
        mid = stream + dot(flip(att[...]), r.w_ffn[:, 2 * wide:])
        r.middle[l][...] = mid
        after = low(mid * inverse_rms(mid) * gains[layers + l])
        r.nffn[...] = after
        r.nffn_t[l][...] = flip(after)
        r.total[...] = mid
        keep(r.middle[l], r.out_middle[l])
        keep(r.nffn_t[l], r.out_nffn_t[l])
        ticker.need(base_chunk + 1 + SPLIT)
        load = pltpu.make_async_copy(r.full_down[l], r.w_down, r.load_sems.at[l, 0])
        load.start()
        load.wait()
        part = wide // (nz * cores)

        def step(c, carry):
            columns = pl.ds(pl.multiple_of(c * part, part), part)
            gate = dot(r.nffn[...], r.w_ffn[:, columns])
            up = dot(r.nffn[...], r.w_ffn[:, pl.ds(pl.multiple_of(wide + c * part, part), part)])
            hidden = low(gelu_parts(gate)[0] * up)
            r.total[...] += dot(hidden, r.w_down[c // cores, c % cores].reshape(part, model))
            return carry
        half = nz * cores // 2
        lax.fori_loop(0, half, step, 0)
        tick(2)
        lax.fori_loop(half, nz * cores, step, 0)
        stream = r.total[...]
        for copy in spread + copies:
            copy.wait_send()
    r.encoded[...] = low(stream)
    for copy in near:
        copy.wait_send()
    for i, chunk in enumerate(chunks):
        ticker.need(i)
        chunk.finish()
    keep.finish()


def like(shape, dtype):
    return jax.ShapeDtypeStruct(shape, dtype)


def kept_shapes(tokens, model):
    size, each = lax.axis_size("ctx"), heads_each()
    f32, bf16 = jnp.float32, jnp.bfloat16
    turned = -(-3 * each * HEAD_DIM // LANES) * LANES
    return dict(x=((tokens, model), f32), middle=((tokens, model), f32), nrm=((model, tokens * size), bf16),
                qkv=((turned, tokens * size), bf16), lse=((each, 1, tokens * size), f32),
                att=((each * size * HEAD_DIM, tokens), bf16), nffn_t=((model, tokens), bf16))


def forward_pass(lengths, byte_ids, small, query_w, key_w, value_w, out_w, gate_w, up_w, down_w, vocab):
    nz, ny, nx = grid_of()
    size, each = lax.axis_size("ctx"), heads_each()
    layers, _, model = out_w.shape
    wide = gate_w.shape[2]
    tokens = byte_ids.shape[1] // 2
    span = byte_ids.shape[1] + 2 * HALO
    f32, bf16 = jnp.float32, jnp.bfloat16
    dma, vmem = pltpu.SemaphoreType.DMA, pltpu.VMEM
    blocks = lambda rows, width: (nz, CORES, ny, nx, rows, width)
    shapes = kept_shapes(tokens, model)
    per_layer = lambda made: [made] * layers
    ffn = blocks(gate_w.shape[1], 2 * wide + model)
    down = blocks(*down_w.shape[1:])
    heads = blocks(query_w.shape[1], shapes["qkv"][0][0])
    inputs = dict(lengths=(lengths, SMEM), byte_ids=(byte_ids, VMEM), small=(small, ANY), query_w=(query_w, VMEM), key_w=(key_w, VMEM),
                  value_w=(value_w, VMEM), out_w=(out_w, ANY), gate_w=(gate_w, ANY), up_w=(up_w, ANY), down_w=(down_w, ANY))
    outputs = dict(
        encoded=(like((tokens, model), bf16), VMEM), small_wide=(like((model, small.shape[1]), f32), VMEM),
        ids=(like((1, 3 * byte_ids.shape[1]), jnp.int32), VMEM), choice=(like((2 * len(BLOCKS), tokens), f32), VMEM),
        out_conv=(like((model, span), f32), ANY), full_ffn=per_layer((like(ffn, bf16), ANY)),
        full_down=per_layer((like(down, bf16), ANY)), out_w_heads=per_layer((like((model, heads[-1]), bf16), ANY)),
        out_x=per_layer((like(*shapes["x"]), ANY)), out_middle=per_layer((like(*shapes["middle"]), ANY)),
        out_nrm=per_layer((like(*shapes["nrm"]), ANY)), out_qkv=per_layer((like(*shapes["qkv"]), ANY)),
        out_lse=per_layer((like(*shapes["lse"]), ANY)), out_att=per_layer((like(*shapes["att"]), ANY)),
        out_nffn_t=per_layer((like(*shapes["nffn_t"]), ANY)))
    scratch = {k: per_layer(vmem(*v)) for k, v in shapes.items()}
    scratch.update(
        heads_w=vmem((layers, size) + heads[4:], bf16), full_small=vmem(blocks(*small.shape), bf16), conv=vmem((model, span), f32), full_heads=per_layer(vmem(heads, bf16)),
        w_heads=per_layer(vmem((model, heads[-1]), bf16)), w_turned=vmem((heads[-1], model), bf16), w_ffn=vmem((model, ffn[-1]), bf16),
        w_down=vmem(down, bf16), blocks=vmem(ffn, bf16), mine=vmem((model, tokens), bf16),
        att_send=vmem((each, size - 1, HEAD_DIM, tokens), bf16), seg_all=vmem((tokens * size, tokens), jnp.int32),
        nffn=vmem((tokens, model), bf16), total=vmem((tokens, model), f32),
        keep_sems=dma((1 + 8 * layers,)), ids_sems=dma((2, 2)), local_sems=dma((1 + layers * SPLIT, 3)), more_sems=dma((layers, 2)),
        load_sems=dma((layers, 1 + SPLIT)), nrm_sems=dma((layers, 2, size - 1)), att_sems=dma((layers, 2, each, size - 1)),
        small_sems=dma((2, hops(small.shape[1], THIRD))), heads_sems=dma((layers, 2, size + nz - 1)),
        ffn_sems=dma((layers, SPLIT, 2, hops(ffn[-1], THIRD))), down_sems=dma((layers, 2, hops(model, THIRD))))
    return run_kernel(functools.partial(forward_body, vocab, layers), inputs, outputs, scratch, 4, "forward_pass")


def backward_body(vocab, layers, r):
    ends = ends_of(r.lengths)
    size, me = lax.axis_size("ctx"), lax.axis_index("ctx")
    each = heads_each()
    base = each * HEAD_DIM
    tokens, model = r.out_grad.shape
    wide = r.w_down.shape[0]
    nz, cores, ny, nx, rows, _ = r.block_ffn.shape[1:]
    part = wide // (nz * cores)
    loads = {}

    def load(key, src, dst, sem):
        loads[key] = pltpu.make_async_copy(src, dst, sem)
        loads[key].start()

    def load_ffn(l):
        sems = r.load_sems.at[l]
        load(0, r.in_nffn_t[l], r.nffn_t, sems.at[0])
        load(1, r.in_w_down[l], r.w_down, sems.at[1])
        load(2, r.in_w_ffn[l], r.w_ffn, sems.at[2])
        load(3, r.in_middle[l], r.middle, sems.at[3])
        load(4, r.in_att[l], r.att, sems.at[4])

    def load_attention(l):
        sems = r.load_sems.at[l]
        load(5, r.in_qkv[l], r.qkv, sems.at[5])
        load(6, r.in_lse[l], r.lse, sems.at[6])
        load(7, r.in_w_heads[l], r.w_heads, sems.at[7])
        load(8, r.in_nrm[l], r.nrm, sems.at[8])
        load(9, r.in_x[l], r.x, sems.at[9])
    load_ffn(layers - 1)
    load_attention(layers - 1)
    greet_all()
    gains = gain_rows(r.small_wide, vocab, layers)
    d_gains = [None] * (2 * layers)
    seg_all = r.seg_all
    seg_all[...] = segments(2 * lax.broadcasted_iota(jnp.int32, seg_all.shape, 0), ends)
    r.dqkv[...] = jnp.zeros(r.dqkv.shape, jnp.bfloat16)
    r.grad[...] = r.out_grad[...].astype(jnp.float32)
    rota = Rota()
    tick = rota.tick
    before = [None] * (2 + SPLIT)
    made = []

    def begin(kind, chunk):
        made.append(chunk)
        before[kind] = chunk
        rota.add(chunk)
    for l in reversed(range(layers)):
        r.grad_low[...] = low(r.grad[...])
        r.total[...] = jnp.zeros(r.total.shape, jnp.float32)
        for key in range(3):
            loads[key].wait()
        r.nffn[...] = flip(r.nffn_t[...])

        def saves(c, slot):
            sems = r.save_sems.at[slot]
            columns = pl.ds(pl.multiple_of(c * part, part), part)
            later = pl.ds(pl.multiple_of(wide + c * part, part), part)
            where = (slice(None),) * 5
            return [pltpu.make_async_copy(r.block_down.at[slot], r.parts_down[l].at[c // cores, c % cores], sems.at[0]),
                    pltpu.make_async_copy(r.block_ffn.at[slot, :, :, :, :, :, pl.ds(0, part)], r.parts_ffn[l].at[where + (columns,)], sems.at[1]),
                    pltpu.make_async_copy(r.block_ffn.at[slot, :, :, :, :, :, pl.ds(part, part)], r.parts_ffn[l].at[where + (later,)], sems.at[2])]

        def step(c, carry):
            columns = pl.ds(pl.multiple_of(c * part, part), part)
            later = pl.ds(pl.multiple_of(wide + c * part, part), part)
            slot = lax.rem(c, 2)

            @pl.when(c >= 2)
            def _():
                for copy in saves(c - 2, slot):
                    copy.wait()
            gate = dot(r.nffn[...], r.w_ffn[:, columns])
            up = dot(r.nffn[...], r.w_ffn[:, later])
            g_hidden = dot_nt(r.grad_low[...], r.w_down[columns, :])
            act, slope = gelu_parts(gate)
            g_gate = low(g_hidden * up * slope)
            g_up = low(g_hidden * act)
            d_down = low(dot(low((act * up).T), r.grad_low[...]))
            r.block_down[slot] = d_down.reshape(r.block_down.shape[1:])
            to_blocks(r.block_ffn.at[slot], slice(0, part), dot(r.nffn_t[...], g_gate))
            to_blocks(r.block_ffn.at[slot], slice(part, 2 * part), dot(r.nffn_t[...], g_up))
            for copy in saves(c, slot):
                copy.start()
            r.total[...] += dot_nt(g_gate, r.w_ffn[:, columns]) + dot_nt(g_up, r.w_ffn[:, later])
            return carry
        for c in range(0, nz * cores, 2):
            lax.fori_loop(c, c + 2, step, 0)
            tick()
        for c in (nz * cores - 2, nz * cores - 1):
            for copy in saves(c, c % 2):
                copy.wait()

        def emit_down(columns, total, l=l):
            r.d_down[l, :, columns] = total

        def emit_ffn(columns, total, l=l):
            first, last = columns.start, columns.start + columns.size
            for out, start in ((r.d_gate, 0), (r.d_up, wide), (r.d_out, 2 * wide)):
                a, b = max(first, start), min(last, start + out.shape[2])
                if a < b:
                    out[l, :, a - start:b - start] = total[:, a - first:b - first]
        if before[0] is not None:
            rota.close(before[0])
        begin(0, Scatter(r.parts_down[l], emit_down, r.down_scratch, r.down_sems.at[l], r.own_sems.at[l, 0], before[0], r.credits.at[0], l == 0))
        loads[3].wait()
        loads[4].wait()
        back, d_gains[layers + l] = norm_back(r.middle[...], gains[layers + l], r.total[...])
        r.grad[...] += back
        r.grad_low[...] = low(r.grad[...])
        r.go_all[0] = flip(dot_nt(r.grad_low[...], r.w_ffn[:, 2 * wide:]))
        go_copies = spread_heads(r.go_all, r.go, r.go_sems.at[l], r.go_own.at[l], each)
        to_blocks(r.block_out, slice(0, model), dot(r.att[...], r.grad_low[...]))
        save = pltpu.make_async_copy(r.block_out, r.parts_ffn[l].at[(slice(None),) * 5 + (pl.ds(2 * wide, model),)], r.own_sems.at[l, 3])
        save.start()
        save.wait()
        for k, (at, _) in enumerate(splits_of(r.parts_ffn[l].shape[-1], SPLIT)):
            if before[2 + k] is not None:
                rota.close(before[2 + k])
            begin(2 + k, Scatter(r.parts_ffn[l], emit_ffn, r.ffn_scratch[k], r.ffn_sems.at[l, k], r.ffn_own.at[l, k],
                                 before[2 + k], r.credits.at[2 + k], l == 0, at))
        if l:
            load_ffn(l - 1)
        for key in range(5, 8):
            loads[key].wait()
        for h in range(each):
            arrive(go_copies[h])
            rows_h = [slice(k * base + h * HEAD_DIM, k * base + (h + 1) * HEAD_DIM) for k in range(3)]
            key_t = r.qkv[rows_h[1], :]
            key, value = flip(key_t), flip(r.qkv[rows_h[2], :])
            g_key = jnp.zeros((HEAD_DIM, tokens * size), jnp.float32)
            g_value = jnp.zeros((HEAD_DIM, tokens * size), jnp.float32)
            for p in range(size):
                theirs = slice(p * tokens, (p + 1) * tokens)
                seg_q = segments(2 * (p * tokens + lax.broadcasted_iota(jnp.int32, (1, tokens), 1)), ends)
                query_t, go_t = r.qkv[rows_h[0], theirs], r.go[0, h * HEAD_DIM:(h + 1) * HEAD_DIM, theirs]
                scores = jnp.where(seg_all[...] == seg_q, dot(key, query_t), NEG_FILL)
                probs = jnp.exp(scores - r.lse[h, :, theirs])
                g_probs = dot(value, go_t)
                inner = jnp.sum(probs * g_probs, 0, keepdims=True)
                g_scores = low(probs * (g_probs - inner))
                r.dqkv[rows_h[0], theirs] = low(dot(key_t, g_scores))
                g_key = g_key + dot_nt(query_t, g_scores)
                g_value = g_value + dot_nt(go_t, low(probs))
                tick(p != 3)
            r.dqkv[rows_h[1], :] = low(g_key)
            r.dqkv[rows_h[2], :] = low(g_value)
        spread = []
        for i, p in enumerate(others()):
            mine = dot(r.w_heads[...], r.dqkv[:, tokens_of(p, tokens)])
            if i == size - 1:
                r.small_grad[:, :tokens] = mine
            else:
                r.sum_send[i] = low(mine)
                copy = to_group(r.sum_send.at[i], r.sum_land.at[i], r.sum_sems.at[l], (i,), p)
                copy.start()
                spread.append(copy)
        for key in (8, 9):
            loads[key].wait()
        if before[1] is not None:
            rota.close(before[1])
            before[1].finish()

        def heads_step(i, carry):
            each_rows = ny * nx * rows
            found = dot_nt(r.nrm[pl.ds(pl.multiple_of(i * each_rows, each_rows), each_rows), :], r.dqkv[...])
            for k in range(ny * nx):
                r.block_heads[i // cores, i % cores, k // nx, k % nx] = low(found[k * rows:(k + 1) * rows])
            return carry
        lax.fori_loop(0, nz * cores, heads_step, 0)
        begin(1, ScatterHeads(r.block_heads, r.d_heads[l], r.heads_scratch, r.heads_sems.at[l], r.own_sems.at[l, 2], before[1], r.credits.at[1], l == 0))
        tick()
        for i, copy in enumerate(spread):
            copy.wait_recv()
            r.small_grad[:, :tokens] += r.sum_land[i].astype(jnp.float32)
        back, d_gains[l] = norm_back(r.x[...], gains[l], r.small_grad[:, :tokens].T)
        r.grad[...] += back
        if l:
            load_attention(l - 1)
        for copies in go_copies:
            for copy in copies[:-1]:
                copy.wait_send()
        for copy in spread:
            copy.wait_send()
    out = r.small_grad
    out[...] = jnp.zeros(out.shape, jnp.float32)
    gbst_backward(ends, r.ids[...], me * 2 * tokens, r.small_wide[...], r.conv, r.choice, r.grad[...].T, vocab, out, tick)
    at = vocab + CONV + 2
    turned = jnp.concatenate(d_gains + [jnp.zeros((-2 * layers % 8, model), jnp.float32)], 0).T
    for i in range(2 * layers):
        out[:, at + i:at + i + 1] = turned[:, i:i + 1]
    to_blocks(r.block_small, slice(None), out[...])

    def emit_small(columns, total):
        r.d_small[:, columns] = total
    begin(0, Scatter(r.block_small, emit_small, r.small_scratch, r.small_sems, r.own_sems.at[layers, 0]))
    while rota.queue:
        tick()
    for chunk in made:
        chunk.finish()
    for l in range(layers):
        for k, found in enumerate((r.d_query, r.d_key, r.d_value)):
            found[l] = jnp.concatenate([r.d_heads[l][p, :, k * base:(k + 1) * base] for p in range(size)], 1)


def backward_pass(lengths, out_grad, fwd, vocab):
    nz, ny, nx = grid_of()
    size, each = lax.axis_size("ctx"), heads_each()
    tokens, model = out_grad.shape
    layers = len(fwd.full_ffn)
    w_ffn = [w.reshape(-1, w.shape[-1]) for w in fwd.full_ffn]
    w_down = [w.reshape(-1, w.shape[-1]) for w in fwd.full_down]
    wide = w_down[0].shape[0]
    part = wide // (nz * CORES)
    f32, bf16 = jnp.float32, jnp.bfloat16
    dma, vmem = pltpu.SemaphoreType.DMA, pltpu.VMEM
    shapes = kept_shapes(tokens, model)
    per_layer = lambda found: [found] * layers
    heads_width = fwd.out_w_heads[0].shape[1]
    ffn, down = fwd.full_ffn[0].shape, fwd.full_down[0].shape
    heads = ffn[:5] + (heads_width,)
    small = ffn[:5] + (fwd.small_wide.shape[1],)
    anywhere = lambda arrays: [(a, ANY) for a in arrays]
    inputs = dict(
        lengths=(lengths, SMEM), out_grad=(out_grad, VMEM), small_wide=(fwd.small_wide, VMEM), ids=(fwd.ids, VMEM),
        choice=(fwd.choice, VMEM), conv=(fwd.out_conv, VMEM), in_w_heads=anywhere(fwd.out_w_heads), in_w_ffn=anywhere(w_ffn),
        in_w_down=anywhere(w_down), in_x=anywhere(fwd.out_x), in_middle=anywhere(fwd.out_middle), in_nrm=anywhere(fwd.out_nrm),
        in_qkv=anywhere(fwd.out_qkv), in_lse=anywhere(fwd.out_lse), in_att=anywhere(fwd.out_att), in_nffn_t=anywhere(fwd.out_nffn_t))
    outputs = dict(
        d_small=(like(small[4:], f32), VMEM), d_query=(like((layers, ffn[4], model), f32), VMEM),
        d_key=(like((layers, ffn[4], model), f32), VMEM), d_value=(like((layers, ffn[4], model), f32), VMEM),
        d_gate=(like((layers, ffn[4], wide), f32), VMEM), d_up=(like((layers, ffn[4], wide), f32), VMEM),
        d_out=(like((layers, ffn[4], model), f32), VMEM), d_down=(like((layers,) + down[4:], f32), VMEM),
        parts_ffn=per_layer((like(ffn, bf16), ANY)), parts_down=per_layer((like(down, bf16), ANY)))
    scratch = {k: vmem(*v) for k, v in shapes.items()}
    scratch.update(
        grad=vmem((tokens, model), f32), total=vmem((tokens, model), f32), grad_low=vmem((tokens, model), bf16),
        nffn=vmem((tokens, model), bf16), w_heads=vmem((model, heads_width), bf16), w_ffn=vmem(w_ffn[0].shape, bf16),
        w_down=vmem(w_down[0].shape, bf16), block_ffn=vmem((2,) + ffn[:5] + (2 * part,), bf16), block_down=vmem((2,) + down[2:], bf16),
        block_out=vmem(ffn[:5] + (model,), bf16), block_heads=vmem(heads, bf16), block_small=vmem(small, bf16),
        go_all=vmem((1,) + shapes["att"][0], bf16), go=vmem((1, each * HEAD_DIM, tokens * size), bf16), dqkv=vmem(*shapes["qkv"]),
        sum_send=vmem((size - 1, model, tokens), bf16),
        sum_land=vmem((size - 1, model, tokens), bf16),
        seg_all=vmem((tokens * size, tokens), jnp.int32), small_grad=vmem(fwd.small_wide.shape, f32),
        down_scratch=Scatter.scratch(down[4:], bf16), ffn_scratch=[Scatter.scratch((ffn[4], w), bf16) for _, w in splits_of(ffn[-1], SPLIT)], ffn_own=dma((layers, SPLIT)),
        small_scratch=Scatter.scratch(small[4:], bf16),
        d_heads=per_layer(vmem((size,) + heads[4:], f32)), heads_scratch=[vmem((nz, ny, nx) + heads[4:], bf16), vmem((nz - 1, ny, nx) + heads[4:], bf16), vmem((size,) + heads[4:], f32)],
        load_sems=dma((layers, 10)), save_sems=dma((2, 3)), own_sems=dma((layers + 1, 4)), go_own=dma((layers, each)),
        go_sems=dma((layers, 2, each, size - 1)), sum_sems=dma((layers, 2, size - 1)), heads_sems=dma((layers, 2, size + nz - 1)),
        ffn_sems=dma((layers, SPLIT, 2, hops(ffn[-1], THIRD))), down_sems=dma((layers, 2, hops(model, THIRD))),
        small_sems=dma((2, hops(small[-1], THIRD))), credits=pltpu.SemaphoreType.REGULAR((2 + SPLIT,)))
    return run_kernel(functools.partial(backward_body, vocab, layers), inputs, outputs, scratch, 5, "backward_pass")


def packed_small(embed, conv_weight, conv_bias, scorer, norm_attn, norm_ffn):
    rows = jnp.concatenate([embed, conv_weight, conv_bias[None], scorer[None], norm_attn, norm_ffn], 0).T
    return jnp.pad(rows, ((0, 0), (0, -rows.shape[1] % 128)))


def split_small(rows, vocab, layers):
    at = vocab + CONV
    return (rows[:vocab], rows[vocab:at], rows[at], rows[at + 1], rows[at + 2 : at + 2 + layers],
            rows[at + 2 + layers : at + 2 + 2 * layers])


def separate_forward(lengths, byte_ids, shards, layer_count, vocab, model):
    ring, tokens = lax.axis_size("ctx"), byte_ids.shape[1] // 2
    up = [(i, (i + 1) % ring) for i in range(ring)]
    down = [(j, i) for i, j in up]
    ids = jnp.concatenate([lax.ppermute(byte_ids, "ctx", up), byte_ids, lax.ppermute(byte_ids, "ctx", down)], 1)
    small_full, *full = [a.reshape(-1, a.shape[-1]) for a in gather_all(shards, 0)]
    small_wide = small_full.astype(jnp.float32)
    gains = small_wide.T[vocab + CONV + 2 :]
    stream, conv, choice = pl.pallas_call(
        functools.partial(gbst_forward_kernel, vocab, tokens),
        out_shape=[
            jax.ShapeDtypeStruct((tokens, model), jnp.float32),
            jax.ShapeDtypeStruct((model, byte_ids.shape[1] + 2 * HALO), jnp.float32),
            jax.ShapeDtypeStruct((2 * len(BLOCKS), tokens), jnp.float32),
        ],
        in_specs=[SMEM, VMEM, VMEM],
        out_specs=[VMEM] * 3,
        compiler_params=pltpu.CompilerParams(vmem_limit_bytes=56 << 20),
        name="mix_bytes",
    )(lengths, ids, small_wide)
    kept = []
    for layer in range(layer_count):
        before = stream
        stream, *saved = layer_forward(
            lengths, stream, gains[layer][None], gains[layer_count + layer][None], *full[3 * layer : 3 * layer + 3], 2
        )
        kept.append((before, saved))
    return stream.astype(jnp.bfloat16), full, small_wide, ids, conv, choice, kept


def fused_step(lengths, byte_ids, small, query_w, key_w, value_w, out_w, gate_w, up_w, down_w, out_grad, vocab):
    fwd = forward_pass(lengths, byte_ids, small, query_w, key_w, value_w, out_w, gate_w, up_w, down_w, vocab)
    back = backward_pass(lengths, out_grad, fwd, vocab)
    grads = (back.d_query, back.d_key, back.d_value, back.d_out, back.d_gate, back.d_up, back.d_down)
    return fwd.encoded, back.d_small, grads


def separate_step(lengths, byte_ids, small, query_w, key_w, value_w, out_w, gate_w, up_w, down_w, out_grad, vocab):
    layer_count, _, model = query_w.shape
    shards = [small]
    for layer in range(layer_count):
        shards.append(jnp.concatenate([w[layer] for w in (query_w, key_w, value_w, out_w)], 1))
        shards.append(jnp.concatenate([gate_w[layer], up_w[layer]], 1))
        shards.append(down_w[layer])
    encoded, full, small_wide, ids, conv, choice, kept = separate_forward(lengths, byte_ids, shards, layer_count, vocab, model)
    gains = small_wide.T[vocab + CONV + 2 :]
    gains_a, gains_f = gains[:layer_count], gains[layer_count : 2 * layer_count]
    grad_stream = out_grad.astype(jnp.float32)
    partial = []
    gains = []
    for layer in reversed(range(layer_count)):
        before, saved = kept[layer]
        weights = full[3 * layer : 3 * layer + 3]
        grad_stream, d_gain_attn, d_gain_ffn, *grads = layer_backward(
            lengths, grad_stream, before, gains_a[layer][None], gains_f[layer][None], saved, *weights, 3
        )
        partial = list(grads) + partial
        gains = [(d_gain_attn[0], d_gain_ffn[0])] + gains
    small_grad = pl.pallas_call(
        functools.partial(gbst_backward_kernel, vocab),
        out_shape=jax.ShapeDtypeStruct(small_wide.shape, jnp.float32),
        in_specs=[SMEM] + [VMEM] * 5,
        out_specs=VMEM,
        compiler_params=pltpu.CompilerParams(vmem_limit_bytes=56 << 20),
        name="mix_bytes_backward",
    )(lengths, ids, small_wide, conv, choice, grad_stream)
    columns = jnp.stack([a for a, _ in gains] + [f for _, f in gains]).T
    small_grad = lax.dynamic_update_slice(small_grad, columns, (0, vocab + CONV + 2))
    outs = scatter_all([p.astype(jnp.bfloat16) for p in [small_grad] + partial], 1)
    small_out, *rest = outs
    attn_out, ffn_out, down_out = rest[0::3], rest[1::3], rest[2::3]
    columns = [jnp.stack([a[:, i * model : (i + 1) * model] for a in attn_out]) for i in range(4)]
    wide = ffn_out[0].shape[1] // 2
    halves_out = [jnp.stack([a[:, :wide] for a in ffn_out]), jnp.stack([a[:, wide:] for a in ffn_out])]
    return encoded, small_out, (*columns, *halves_out, jnp.stack(down_out))


def on_device(
    byte_ids,
    lengths,
    embed,
    conv_weight,
    conv_bias,
    scorer,
    norm_attn,
    query_w,
    key_w,
    value_w,
    attn_out_w,
    norm_ffn,
    gate_w,
    up_w,
    down_w,
    out_grad,
):
    layers, vocab = query_w.shape[0], embed.shape[0]
    small = packed_small(embed, conv_weight, conv_bias, scorer, norm_attn, norm_ffn)
    if query_w.shape[1] % 8 == 0 and HEADS % lax.axis_size("ctx") == 0:
        step = fused_step
    else:
        step = separate_step
    encoded, small_out, wide_grads = step(
        lengths, byte_ids, small, query_w, key_w, value_w, attn_out_w, gate_w, up_w, down_w, out_grad[0], vocab
    )
    d_query, d_key, d_value, d_out, d_gate, d_up, d_down = wide_grads
    d_embed, d_conv, d_bias, d_scorer, d_norm_attn, d_norm_ffn = split_small(small_out.T, vocab, layers)
    return (encoded[None], d_embed, d_conv, d_bias, d_scorer, d_norm_attn, d_query, d_key, d_value, d_out, d_norm_ffn,
            d_gate, d_up, d_down)


def solution(mesh):
    placed = (
        P("dp", "ctx"),
        P("dp", None),
        P(None, ("dp", "ctx")),
        P(None, ("dp", "ctx")),
        P(("dp", "ctx")),
        P(("dp", "ctx")),
        P(None, ("dp", "ctx")),
        P(None, ("dp", "ctx"), None),
        P(None, ("dp", "ctx"), None),
        P(None, ("dp", "ctx"), None),
        P(None, ("dp", "ctx"), None),
        P(None, ("dp", "ctx")),
        P(None, ("dp", "ctx"), None),
        P(None, ("dp", "ctx"), None),
        P(None, ("dp", "ctx"), None),
        P("dp", "ctx", None),
    )
    return jax.shard_map(
        on_device,
        mesh=mesh,
        in_specs=placed,
        out_specs=(
            P("dp", "ctx", None),
            P(None, ("dp", "ctx")),
            P(None, ("dp", "ctx")),
            P(("dp", "ctx")),
            P(("dp", "ctx")),
            P(None, ("dp", "ctx")),
            P(None, ("dp", "ctx"), None),
            P(None, ("dp", "ctx"), None),
            P(None, ("dp", "ctx"), None),
            P(None, ("dp", "ctx"), None),
            P(None, ("dp", "ctx")),
            P(None, ("dp", "ctx"), None),
            P(None, ("dp", "ctx"), None),
            P(None, ("dp", "ctx"), None),
        ),
        check_vma=False,
    )
```
